32 devices in a mesh: groups: 2 (over y), pairs: 4 (over z), sub: 2 (over x), rep: 2 (over core).
Axes of the slice: x: 2, y: 2, z: 4, core: 2. Of those that a mesh axis runs over, the one named last changes fastest.
Arguments:
- amplitudes: float32 [32, 256, 256], P(('groups', 'pairs', 'sub')), parts along dimension 0, may hold values from -6 to 6
- exchange_ints: float32 [32, 256, 256], P(('groups', 'pairs', 'sub')), parts along dimension 0, may hold values from -6 to 6
- pair_list: int32 [32, 2], P(('groups', 'pairs', 'sub')), parts along dimension 0, may hold values from 0 to 1999
- domains: int32 [32, 256], P(('groups', 'pairs', 'sub')), parts along dimension 0, may hold values from 0 to 23999, as said below
- link_source: int32 [32, 32], P(('groups', 'pairs', 'sub')), parts along dimension 0, may hold values from 0 to 15, as said below
- link_entry: int32 [32, 32], P(('groups', 'pairs', 'sub')), parts along dimension 0, may hold values from 0 to 4095
- link_count: int32 [32], P(('groups', 'pairs', 'sub')), parts along dimension 0, may hold values from 16 to 32, as said below
- owner_map: int32 [32], P('groups'), parts along dimension 0, may hold values from 0 to 15, as said below
- fock_values: float32 [8192], P('groups'), parts along dimension 0, may hold values from -0.6 to 0.6
- occ_energy: float32 [4000], P('groups'), parts along dimension 0, may hold values from -1.5 to -0.3
- vir_energy: float32 [48000], P('groups'), parts along dimension 0, may hold values from 0.2 to 3
- positions: float32 [3, 48000], P(None, 'groups'), parts along dimension 1
Outputs:
- residual: float32 [32, 256, 256], P(('groups', 'pairs', 'sub')), parts along dimension 0
- updated: float32 [32, 256, 256], P(('groups', 'pairs', 'sub')), parts along dimension 0
The draws below stay inside these ranges and needn't reach their ends.
There are 2 independent parts, one for each index of `groups`. The reference program is written for one: setup_inputs(seed, part) draws one part's arguments, and reference() takes and returns one part's arrays. A program takes and returns all parts, laid end to end along the dimension named above; each array names one. Nothing has to cross between parts.
Inputs may be any that keep to these rules, and one draw needn't show every extreme that they name: `domains`: each row names 256 distinct orbitals. `link_source`: pair ids. Over the live slots of the pairs stored on one device, the named neighbours lie on at most one distinct storage slot of each index of pairs, always on a device with the same index of sub; every device names one on each of min(4, live slots) indices. `link_count`: every fifth stored pair has all 32 slots live. `owner_map`: A permutation.
All inputs are finite; a program needn't handle non-finite values.
Results may differ from the reference program's by a relative error of at most 0.0003.
Values sent between devices are 32-bit elements; how exact they have to be, the bound alone decides.
No kernel may reach another device: no remote copies, remote signals or barrier semaphores. Data moves between devices by JAX's collectives and lax.ppermute only.
A program may use at most 64 MiB of HBM per device.

```python
import jax
import jax.numpy as jnp
from jax import lax

NV = 256
NVIRT = 24000
NOCC = 2000
NFOCK = 4096
PAIR_DEV = 2
LINKS = 32
PAIRS = 16
N_PAIRS = 4
N_SUB = 2


cell_spacing = 0.5


def grid_side():
    side = 1
    while side ** 3 < NVIRT:
        side = side + 1
    return side


def box_side():
    side = 1
    while side ** 3 < NV:
        side = side + 1
    return side


def pair_layout(key):
    owner = jax.random.permutation(jax.random.fold_in(key, 11), PAIRS).astype(jnp.int32)
    inverse = jnp.argsort(owner).astype(jnp.int32)
    return (owner, inverse)


def draw_owner_map(key, part):
    owner, inverse = pair_layout(key)
    return owner


def draw_positions(key, part):
    key = jax.random.fold_in(key, 5)
    side = grid_side()
    orbital = jnp.arange(NVIRT, dtype=jnp.int32)
    cells = jnp.stack([orbital % side, orbital // side % side, orbital // (side * side)]).astype(jnp.float32)
    jitter = jax.random.uniform(key, (3, NVIRT), jnp.float32, -0.15, 0.15)
    return (cells * cell_spacing + jitter).astype(jnp.float32)


def draw_domains(key, part):
    key = jax.random.fold_in(key, 9)
    side = grid_side()
    layers = NVIRT // (side * side)
    width = box_side()
    cube = width ** 3
    jitter_key, score_key = jax.random.split(key)
    stored = jnp.arange(PAIRS, dtype=jnp.int32)
    column = stored // PAIR_DEV % N_SUB
    centre_x = (2 * column + 1) * side // (2 * N_SUB)
    jitter = jax.random.randint(jitter_key, (3, PAIRS), -1, 2)
    start_x = jnp.clip(centre_x - width // 2 + jitter[0], 0, side - width)
    start_y = jnp.clip(side // 2 - width // 2 + jitter[1], 0, side - width)
    start_z = jnp.clip(layers // 2 - width // 2 + jitter[2], 0, layers - width)
    scores = jax.random.randint(score_key, (PAIRS, cube), 0, 1 << 20) * cube + jnp.arange(cube, dtype=jnp.int32)[None, :]
    chosen = jnp.argsort(scores, axis=1)[:, :NV].astype(jnp.int32)
    offset_x = chosen % width
    offset_y = chosen // width % width
    offset_z = chosen // (width * width)
    index = start_x[:, None] + offset_x + side * (start_y[:, None] + offset_y) + side * side * (start_z[:, None] + offset_z)
    index = index.astype(jnp.int32)
    index = index.at[0, NV - 1].set(NVIRT - 1)
    index = index.at[1, NV - 1].set(0)
    return index.astype(jnp.int32)


def draw_link_source(key, part):
    owner, inverse = pair_layout(key)
    key = jax.random.fold_in(key, 3)
    device_count = N_PAIRS * N_SUB
    score_key, slot_key = jax.random.split(key)
    scores = jax.random.randint(score_key, (device_count, N_PAIRS), 0, 1 << 20) * N_PAIRS + jnp.arange(N_PAIRS)[None, :]
    peer_order = jnp.argsort(scores, axis=1).astype(jnp.int32)
    slot_pick = jax.random.randint(slot_key, (device_count, N_PAIRS), 0, PAIR_DEV)
    link_index = jnp.arange(PAIR_DEV * LINKS) % N_PAIRS
    peers = peer_order[:, link_index]
    slots = jnp.take_along_axis(slot_pick, peers, axis=1)
    columns = (jnp.arange(device_count) % N_SUB)[:, None]
    stored = (peers * N_SUB + columns) * PAIR_DEV + slots
    return inverse[stored].reshape(PAIRS, LINKS).astype(jnp.int32)


def draw_link_count(key, part):
    key = jax.random.fold_in(key, 7)
    counts = jax.random.randint(key, (PAIRS,), (LINKS + 1) // 2, LINKS + 1)
    return jnp.where(jnp.arange(PAIRS) % 5 == 0, LINKS, counts).astype(jnp.int32)


def set_ends(drawn, rng, least, high):
    dims = drawn.shape
    index_at = [jax.random.randint(jax.random.fold_in(rng, axis), (), 0, dims[axis]) for axis in range(len(dims))]
    drawn = drawn.at[tuple(index_at)].set(least)
    longest = dims.index(max(dims))
    index_at[longest] = (index_at[longest] + 1) % dims[longest]
    return drawn.at[tuple(index_at)].set(high)


def steps_of(own_key, extent, shards, low, top_value):
    def one(position, shards_of):
        steps = jax.random.uniform(jax.random.fold_in(jax.random.fold_in(own_key, 6), position), (shards_of,), jnp.float32, low / len(shards), top_value / len(shards))
        return jnp.repeat(jnp.exp(steps), extent[position] // shards_of).reshape((-1,) + (1,) * (len(extent) - position - 1))

    loudness = one(*shards[0])
    for cut in shards[1:]:
        loudness = loudness * one(*cut)
    return loudness


def normal_values(key, dims, spread, bound, shards=(), kind=jnp.bfloat16):
    factor_of = steps_of(key, dims, shards, -0.22, 0.18) if shards else 1.0
    result = jax.random.normal(key, dims, jnp.float32) * spread * factor_of
    return jnp.minimum(jnp.maximum(result, -bound), bound).astype(kind)


def setup_inputs(seed: int = 0, part: int = 0) -> dict:
    arg_keys = jax.random.split(jax.random.key(seed), 13)
    own_keys = jax.random.split(jax.random.fold_in(arg_keys[12], part), 13)
    return {
        "amplitudes": normal_values(own_keys[0], (PAIRS, NV, NV), 1.0, 6.0, ((0, 8),), jnp.float32),
        "exchange_ints": normal_values(own_keys[1], (PAIRS, NV, NV), 1.0, 6.0, ((0, 8),), jnp.float32),
        "pair_list": set_ends(jax.random.randint(own_keys[2], (PAIRS, 2), 0, NOCC), jax.random.fold_in(own_keys[2], 1), 0, NOCC - 1).astype(jnp.int32),
        "domains": draw_domains(jax.random.fold_in(jax.random.fold_in(arg_keys[12], part), 71), part),
        "link_source": draw_link_source(jax.random.fold_in(jax.random.fold_in(arg_keys[12], part), 71), part),
        "link_entry": set_ends(jax.random.randint(own_keys[5], (PAIRS, LINKS), 0, NFOCK), jax.random.fold_in(own_keys[5], 1), 0, NFOCK - 1).astype(jnp.int32),
        "link_count": draw_link_count(jax.random.fold_in(jax.random.fold_in(arg_keys[12], part), 71), part),
        "owner_map": draw_owner_map(jax.random.fold_in(jax.random.fold_in(arg_keys[12], part), 71), part),
        "fock_values": jnp.clip(jax.random.uniform(own_keys[8], (NFOCK,), jnp.float32, -0.6, 0.6), -0.6, 0.6),
        "occ_energy": jnp.clip(jax.random.uniform(own_keys[9], (NOCC,), jnp.float32, -1.5, -0.3), -1.5, -0.3),
        "vir_energy": jnp.clip(jax.random.uniform(own_keys[10], (NVIRT,), jnp.float32, 0.2, 3.0), 0.2, 3.0),
        "positions": draw_positions(jax.random.fold_in(jax.random.fold_in(arg_keys[12], part), 71), part),
    }


intersection_rate = 2.0


def product(left, right):
    return jnp.dot(left, right, precision=lax.Precision.HIGHEST, preferred_element_type=jnp.float32)


def pick_row(array, index):
    return lax.dynamic_index_in_dim(array, index, 0, keepdims=False)


def model_intersection(left_coords, right_coords):
    squared = jnp.zeros((left_coords.shape[1], right_coords.shape[1]), jnp.float32)
    for component in range(3):
        gap_now = left_coords[component][:, None] - right_coords[component][None, :]
        squared = squared + gap_now * gap_now
    return jnp.exp(-intersection_rate * squared)


def pair_local(block, integrals, pair_coords, pair_energy, pair_shift):
    metric = model_intersection(pair_coords, pair_coords)
    virtual_fock = metric * ((pair_energy[:, None] + pair_energy[None, :]) * 0.5)
    right_side = product(block, metric)
    left_side = product(metric, block)
    return integrals + product(virtual_fock, right_side) + product(left_side, virtual_fock) - pair_shift * product(metric, right_side)


def reference(amplitudes, exchange_ints, pair_list, domains, link_source, link_entry, link_count, owner_map, fock_values, occ_energy, vir_energy, positions):
    coords = jnp.moveaxis(jnp.take(positions, domains, axis=1), 0, 1)
    energy = jnp.take(vir_energy, domains, axis=0)
    shift = jnp.take(occ_energy, pair_list[:, 0]) + jnp.take(occ_energy, pair_list[:, 1])

    def local_one(pair_index):
        return pair_local(pick_row(amplitudes, pair_index), pick_row(exchange_ints, pair_index), pick_row(coords, pair_index), pick_row(energy, pair_index), pick_row(shift, pair_index))

    def coupled_one(pair_index):
        sources = jnp.take(owner_map, pick_row(link_source, pair_index)).astype(jnp.int32)
        weights = jnp.take(fock_values, pick_row(link_entry, pair_index))
        live_count = pick_row(link_count, pair_index)
        own_coords = pick_row(coords, pair_index)

        def advance(slot_index, total):
            source = pick_row(sources, slot_index)
            intersection = model_intersection(own_coords, pick_row(coords, source))
            term = product(product(intersection, pick_row(amplitudes, source)), intersection.T)
            scale = jnp.where(slot_index < live_count, pick_row(weights, slot_index), jnp.zeros((), jnp.float32))
            return total + scale * term

        return lax.fori_loop(0, LINKS, advance, jnp.zeros((NV, NV), jnp.float32))

    indices = jnp.arange(PAIRS, dtype=jnp.int32)
    local = lax.map(local_one, indices)
    coupling = lax.map(coupled_one, indices)
    residual = local - coupling
    denominator = energy[:, :, None] + energy[:, None, :] - shift[:, None, None]
    updated = amplitudes - residual / denominator
    return residual, updated
```

```python
import functools

import jax
import jax.numpy as jnp
from jax import lax
from jax.experimental import pallas as pl
from jax.experimental.pallas import tpu as pltpu
from jax.sharding import PartitionSpec as P

intersection_rate = 2.0
COORD_ROWS = 8
VMEM_LIMIT = 40 * 1024 * 1024


def product(left, right):
    return jnp.dot(left, right, precision=lax.Precision.HIGHEST, preferred_element_type=jnp.float32)


def pick_row(array, index):
    return lax.dynamic_index_in_dim(array, index, 0, keepdims=False)


def model_intersection(left_coords, right_coords):
    squared = jnp.zeros((left_coords.shape[1], right_coords.shape[1]), jnp.float32)
    for component in range(3):
        gap_now = left_coords[component][:, None] - right_coords[component][None, :]
        squared = squared + gap_now * gap_now
    return jnp.exp(-intersection_rate * squared)


def pair_local(block, integrals, pair_coords, pair_energy, pair_shift):
    metric = model_intersection(pair_coords, pair_coords)
    virtual_fock = metric * ((pair_energy[:, None] + pair_energy[None, :]) * 0.5)
    right_side = product(block, metric)
    left_side = product(metric, block)
    return (
        integrals
        + product(virtual_fock, right_side)
        + product(left_side, virtual_fock)
        - pair_shift * product(metric, right_side)
    )


def on_device_any(
    amplitudes,
    exchange_ints,
    pair_list,
    domains,
    link_source,
    link_entry,
    link_count,
    owner_map,
    fock_values,
    occ_energy,
    vir_energy,
    positions,
):
    pair_count = amplitudes.shape[0]
    link_slots = link_source.shape[1]
    row_count = lax.axis_size("pairs")
    sub_count = lax.axis_size("sub")
    core_count = lax.axis_size("rep")
    my_core = lax.axis_index("rep")
    coords = jnp.moveaxis(jnp.take(positions, domains, axis=1), 0, 1)
    energy = jnp.take(vir_energy, domains, axis=0)
    shift = jnp.take(occ_energy, pair_list[:, 0]) + jnp.take(occ_energy, pair_list[:, 1])
    is_live = jnp.arange(link_slots, dtype=jnp.int32)[None, :] < link_count[:, None]
    source_loc = jnp.take(owner_map, link_source)
    source_peer = source_loc // (pair_count * sub_count)
    source_slot = source_loc % pair_count
    peers = jnp.arange(row_count, dtype=jnp.int32)
    matched = is_live[:, :, None] & (source_peer[:, :, None] == peers[None, None, :])
    fock_weight = jnp.take(fock_values, link_entry)
    weight = jnp.sum(jnp.where(matched, fock_weight[:, :, None], 0.0), axis=1)
    wanted = jnp.max(jnp.where(matched, source_slot[:, :, None], 0), axis=(0, 1))
    asked = lax.all_to_all(wanted[:, None], "pairs", split_axis=0, concat_axis=0, tiled=True)[:, 0]
    fetched = lax.all_to_all(
        jnp.take(amplitudes, asked, axis=0), "pairs", split_axis=0, concat_axis=0, tiled=True
    )
    fetched_coords = lax.all_to_all(
        jnp.take(coords, asked, axis=0), "pairs", split_axis=0, concat_axis=0, tiled=True
    )

    def target(pair):
        local = pair_local(
            pick_row(amplitudes, pair),
            pick_row(exchange_ints, pair),
            pick_row(coords, pair),
            pick_row(energy, pair),
            pick_row(shift, pair),
        )

        def advance(peer, total):
            intersection = model_intersection(pick_row(coords, pair), pick_row(fetched_coords, peer))
            term = product(product(intersection, pick_row(fetched, peer)), intersection.T)
            return total - pick_row(pick_row(weight, pair), peer) * term

        return lax.fori_loop(0, row_count, advance, local)

    mine = jnp.arange(pair_count, dtype=jnp.int32) % core_count == my_core
    share = lax.map(
        lambda pair: lax.cond(
            pick_row(mine, pair), target, lambda _: jnp.zeros_like(amplitudes[0]), pair
        ),
        jnp.arange(pair_count, dtype=jnp.int32),
    )
    residual = lax.psum(share, "rep")
    denominator = energy[:, :, None] + energy[:, None, :] - shift[:, None, None]
    return residual, amplitudes - residual / denominator


def split(value):
    high = value.astype(jnp.bfloat16)
    low = (value - high.astype(jnp.float32)).astype(jnp.bfloat16)
    return high, low


NN = (((1,), (0,)), ((), ()))
NT = (((1,), (1,)), ((), ()))
TN = (((0,), (0,)), ((), ()))


def dot(left, right, dims):
    return lax.dot_general(left, right, dims, preferred_element_type=jnp.float32)


def dot3(left, right, dims=NN):
    return (
        dot(left[0], right[0], dims) + dot(left[0], right[1], dims) + dot(left[1], right[0], dims)
    )


def overlap(column, rows):
    squared = None
    for c in range(3):
        gap = column[:, c : c + 1] - rows[c]
        squared = gap * gap if squared is None else squared + gap * gap
    return jnp.exp(-intersection_rate * squared)


def sandwich(metric, block):
    metric = split(metric)
    return dot3(split(dot3(metric, split(block))), metric, NT)


def gather_kernel(domains_ref, positions_ref, energy_ref, block_ref, coords_ref, payload_ref, table):
    pairs, size = domains_ref.shape
    orbitals = positions_ref.shape[1]
    rows = table.shape[0] // 4
    whole, rest = orbitals // 128, orbitals % 128
    table[...] = jnp.zeros_like(table)
    for k in range(whole):
        table[pl.ds(k, 3, stride=rows), :] = positions_ref[:, k * 128 : (k + 1) * 128]
        table[3 * rows + k : 3 * rows + k + 1, :] = energy_ref[k * 128 : (k + 1) * 128].reshape(1, 128)
    if rest:
        table[pl.ds(whole, 3, stride=rows), :rest] = positions_ref[:, whole * 128 :]
        table[3 * rows + whole : 3 * rows + whole + 1, :rest] = energy_ref[whole * 128 :].reshape(
            1, rest
        )
    first = table[...].astype(jnp.bfloat16)
    left = table[...] - first.astype(jnp.float32)
    second = left.astype(jnp.bfloat16)
    third = (left - second.astype(jnp.float32)).astype(jnp.bfloat16)
    core = lax.axis_index("rep")
    half = size // 2
    for p in range(pairs):
        index = domains_ref[p : p + 1, :]
        high = index // 128
        low = index - high * 128
        chosen = (lax.broadcasted_iota(jnp.int32, (rows, size), 0) == high).astype(
            jnp.float32
        ).astype(jnp.bfloat16)
        lane = lax.broadcasted_iota(jnp.int32, (128, size), 0) == low
        found = []
        for c in range(4):
            span = slice(c * rows, (c + 1) * rows)
            lines = (
                dot(first[span], chosen, TN)
                + dot(second[span], chosen, TN)
                + dot(third[span], chosen, TN)
            )
            found.append(jnp.sum(jnp.where(lane, lines, 0.0), axis=0, keepdims=True))
        found.append(jnp.zeros((COORD_ROWS - 4, size), jnp.float32))
        found = jnp.concatenate(found, axis=0)
        coords_ref[p] = found
        payload_ref[p, :half, :] = block_ref[p, pl.ds(pl.multiple_of(core * half, half), half), :]
        payload_ref[p, half:, :] = found


def select_kernel(asked_ref, block_ref, coords_ref, payload_ref):
    size = block_ref.shape[1]
    second = jnp.max(asked_ref[...]) > 0
    payload_ref[:size, :] = jnp.where(second, block_ref[1], block_ref[0])
    payload_ref[size:, :] = jnp.where(second, coords_ref[1], coords_ref[0])


def near_kernel(
    sub_count,
    block_ref,
    integrals_ref,
    coords_ref,
    near_ref,
    source_ref,
    entry_ref,
    count_ref,
    owner_ref,
    fock_ref,
    pair_ref,
    occ_ref,
    share_ref,
    weight_ref,
    inverse_ref,
):
    pairs, size = block_ref.shape[0], block_ref.shape[1]
    half = size // 2
    links = source_ref.shape[1]
    core = lax.axis_index("rep")
    row = lax.axis_index("pairs")
    beside = row ^ 1
    partner = row ^ (3 - core)

    def look(m, carry):
        own_slot, near_slot, weights = carry
        weights = list(weights)
        for p in range(pairs):
            place = owner_ref[source_ref[p, m]]
            peer = lax.div(place, pairs * sub_count)
            slot = lax.rem(place, pairs)
            live = m < count_ref[p]
            value = fock_ref[entry_ref[p, m]]
            own, near, far = live & (peer == row), live & (peer == beside), live & (peer == partner)
            own_slot = jnp.where(own, slot, own_slot)
            near_slot = jnp.where(near, slot, near_slot)
            for k, hit in enumerate((own, near, far)):
                weights[3 * p + k] += jnp.where(hit, value, 0.0)
        return own_slot, near_slot, tuple(weights)

    zero = jnp.int32(0)
    own_slot, near_slot, weights = lax.fori_loop(
        0, links, look, (zero, zero, (jnp.float32(0.0),) * (3 * pairs))
    )
    for p in range(pairs):
        weight_ref[p] = jnp.full((8, 128), weights[3 * p + 2], jnp.float32)
    shifts = [occ_ref[pair_ref[p, 0]] + occ_ref[pair_ref[p, 1]] for p in range(pairs)]
    columns = [coords_ref[p].T for p in range(pairs)]
    for p in range(pairs):
        inverse_ref[p] = 1.0 / (columns[p][:, 3:4] + coords_ref[p, 3:4, :] - shifts[p])

    first = core == 0
    column = jnp.where(first, columns[0], columns[1])
    shift = jnp.where(first, shifts[0], shifts[1])
    own_weight = jnp.where(first, weights[0], weights[3])
    energy = (column[:, 3:4] + coords_ref[core, 3:4, :]) * 0.5
    block = block_ref[core]
    metric = split(overlap(column, [coords_ref[core, c : c + 1, :] for c in range(3)]))
    plain = dot3(metric, split(dot3(split(block), metric)))
    scaled = dot3(metric, split(dot3(split(block * (energy - shift)), metric)))
    local = integrals_ref[core] + scaled + plain * energy
    own = overlap(column, [coords_ref[own_slot, c : c + 1, :] for c in range(3)])
    local = local - own_weight * sandwich(own, block_ref[own_slot])

    part = split(near_ref[near_slot, :half, :])
    for p in range(pairs):
        rows = [near_ref[near_slot, half + c : half + c + 1, :] for c in range(3)]
        halves = [jnp.where(first, line[:, :half], line[:, half:]) for line in rows]
        whole = split(overlap(columns[p], rows))
        side = split(overlap(columns[p], halves))
        term = dot3(side, split(dot3(part, whole, NT)))
        share_ref[p] = jnp.where(core == p, local, 0.0) - weights[3 * p + 1] * term


def far_kernel(far_ref, coords_ref, share_ref, weight_ref, total_ref):
    pairs, size = share_ref.shape[0], share_ref.shape[1]
    block = split(far_ref[:size, :])
    rows = [far_ref[size + c : size + c + 1, :] for c in range(3)]
    for p in range(pairs):
        metric = split(overlap(coords_ref[p].T, rows))
        term = dot3(split(dot3(metric, block)), metric, NT)
        total_ref[p] = share_ref[p] - weight_ref[p, 0:1, 0:1] * term


def call(body, outs, spaces, args, scratch=(), flops=0, moved=0):
    return pl.pallas_call(
        body,
        out_shape=outs,
        in_specs=[pl.BlockSpec(memory_space=space) for space in spaces],
        out_specs=jax.tree.map(lambda _: pl.BlockSpec(memory_space=pltpu.VMEM), outs),
        scratch_shapes=list(scratch),
        compiler_params=pltpu.CompilerParams(vmem_limit_bytes=VMEM_LIMIT),
        cost_estimate=pl.CostEstimate(flops=flops, bytes_accessed=moved, transcendentals=0),
    )(*args)


def on_device_four(
    amplitudes,
    exchange_ints,
    pair_list,
    domains,
    link_source,
    link_entry,
    link_count,
    owner_map,
    fock_values,
    occ_energy,
    vir_energy,
    positions,
):
    pairs, size = amplitudes.shape[0], amplitudes.shape[1]
    sub_count = lax.axis_size("sub")
    core = lax.axis_index("rep")
    row = lax.axis_index("pairs")
    axes = ("pairs", "rep")
    across = [(2 * z + c, 2 * (z ^ (3 - c)) + c) for z in range(4) for c in range(2)]
    beside = [(2 * z + c, 2 * (z ^ 1) + c) for z in range(4) for c in range(2)]
    f32 = jnp.float32
    V, S = pltpu.VMEM, pltpu.SMEM

    live = jnp.arange(link_source.shape[1], dtype=jnp.int32)[None, :] < link_count[:, None]
    ids = jnp.arange(owner_map.shape[0], dtype=jnp.int32)
    there = owner_map // (pairs * sub_count) == (row ^ (3 - core))
    hit = live[:, :, None] & (link_source[:, :, None] == ids) & there
    wanted = jnp.max(jnp.where(hit, owner_map % pairs, 0))
    asked = lax.ppermute(jnp.full((8, 128), wanted, jnp.int32), axes, across)

    lines = -(-positions.shape[1] // 128)
    lines = -(-lines // 16) * 16
    coords, near = call(
        gather_kernel,
        (
            jax.ShapeDtypeStruct((pairs, COORD_ROWS, size), f32),
            jax.ShapeDtypeStruct((pairs, size // 2 + COORD_ROWS, size), f32),
        ),
        (V, V, V, V),
        (domains, positions, vir_energy, amplitudes),
        scratch=[pltpu.VMEM((4 * lines, 128), f32)],
        flops=10**9,
        moved=10**6,
    )
    near = lax.ppermute(near, axes, beside)
    far = call(
        select_kernel,
        jax.ShapeDtypeStruct((size + COORD_ROWS, size), f32),
        (V, V, V),
        (asked, amplitudes, coords),
        moved=10**6,
    )
    far = lax.ppermute(far, axes, across)
    share, weight, inverse = call(
        functools.partial(near_kernel, sub_count),
        (
            jax.ShapeDtypeStruct(amplitudes.shape, f32),
            jax.ShapeDtypeStruct((pairs, 8, 128), f32),
            jax.ShapeDtypeStruct(amplitudes.shape, f32),
        ),
        (V, V, V, V, S, S, S, S, S, S, S),
        (
            amplitudes,
            exchange_ints,
            coords,
            near,
            link_source,
            link_entry,
            link_count,
            owner_map,
            fock_values,
            pair_list,
            occ_energy,
        ),
        flops=2 * 10**9,
        moved=3 * 10**6,
    )
    total = call(
        far_kernel,
        jax.ShapeDtypeStruct(amplitudes.shape, f32),
        (V, V, V, V),
        (far, coords, share, weight),
        flops=10**9,
        moved=10**6,
    )
    residual = total + lax.ppermute(total, "rep", [(0, 1), (1, 0)])
    return residual, amplitudes - residual * inverse


def solution(mesh):
    stored = ("groups", "pairs", "sub")
    in_specs = (
        P(stored, None, None),
        P(stored, None, None),
        P(stored, None),
        P(stored, None),
        P(stored, None),
        P(stored, None),
        P(stored),
        P("groups"),
        P("groups"),
        P("groups"),
        P("groups"),
        P(None, "groups"),
    )
    out_specs = (P(stored, None, None), P(stored, None, None))

    def run(*args):
        devices = mesh.shape["groups"] * mesh.shape["pairs"] * mesh.shape["sub"]
        known = (
            mesh.shape["pairs"] == 4
            and mesh.shape["rep"] == 2
            and args[0].shape[0] == 2 * devices
            and args[0].shape[1] == 256
        )
        return jax.shard_map(
            on_device_four if known else on_device_any,
            mesh=mesh,
            in_specs=in_specs,
            out_specs=out_specs,
            check_vma=False,
        )(*args)

    return run
```

```python
import functools

import jax
import jax.numpy as jnp
from jax import lax
from jax.experimental import pallas as pl
from jax.experimental.pallas import tpu as pltpu
from jax.sharding import PartitionSpec as P

intersection_rate = 2.0
COORD_ROWS = 8
VMEM_LIMIT = 40 * 1024 * 1024


def product(left, right):
    return jnp.dot(left, right, precision=lax.Precision.HIGHEST, preferred_element_type=jnp.float32)


def pick_row(array, index):
    return lax.dynamic_index_in_dim(array, index, 0, keepdims=False)


def model_intersection(left_coords, right_coords):
    squared = jnp.zeros((left_coords.shape[1], right_coords.shape[1]), jnp.float32)
    for component in range(3):
        gap_now = left_coords[component][:, None] - right_coords[component][None, :]
        squared = squared + gap_now * gap_now
    return jnp.exp(-intersection_rate * squared)


def pair_local(block, integrals, pair_coords, pair_energy, pair_shift):
    metric = model_intersection(pair_coords, pair_coords)
    virtual_fock = metric * ((pair_energy[:, None] + pair_energy[None, :]) * 0.5)
    right_side = product(block, metric)
    left_side = product(metric, block)
    return (
        integrals
        + product(virtual_fock, right_side)
        + product(left_side, virtual_fock)
        - pair_shift * product(metric, right_side)
    )


def on_device_any(
    amplitudes,
    exchange_ints,
    pair_list,
    domains,
    link_source,
    link_entry,
    link_count,
    owner_map,
    fock_values,
    occ_energy,
    vir_energy,
    positions,
):
    pair_count = amplitudes.shape[0]
    link_slots = link_source.shape[1]
    row_count = lax.axis_size("pairs")
    sub_count = lax.axis_size("sub")
    core_count = lax.axis_size("rep")
    my_core = lax.axis_index("rep")
    coords = jnp.moveaxis(jnp.take(positions, domains, axis=1), 0, 1)
    energy = jnp.take(vir_energy, domains, axis=0)
    shift = jnp.take(occ_energy, pair_list[:, 0]) + jnp.take(occ_energy, pair_list[:, 1])
    is_live = jnp.arange(link_slots, dtype=jnp.int32)[None, :] < link_count[:, None]
    source_loc = jnp.take(owner_map, link_source)
    source_peer = source_loc // (pair_count * sub_count)
    source_slot = source_loc % pair_count
    peers = jnp.arange(row_count, dtype=jnp.int32)
    matched = is_live[:, :, None] & (source_peer[:, :, None] == peers[None, None, :])
    fock_weight = jnp.take(fock_values, link_entry)
    weight = jnp.sum(jnp.where(matched, fock_weight[:, :, None], 0.0), axis=1)
    wanted = jnp.max(jnp.where(matched, source_slot[:, :, None], 0), axis=(0, 1))
    asked = lax.all_to_all(wanted[:, None], "pairs", split_axis=0, concat_axis=0, tiled=True)[:, 0]
    fetched = lax.all_to_all(
        jnp.take(amplitudes, asked, axis=0), "pairs", split_axis=0, concat_axis=0, tiled=True
    )
    fetched_coords = lax.all_to_all(
        jnp.take(coords, asked, axis=0), "pairs", split_axis=0, concat_axis=0, tiled=True
    )

    def target(pair):
        local = pair_local(
            pick_row(amplitudes, pair),
            pick_row(exchange_ints, pair),
            pick_row(coords, pair),
            pick_row(energy, pair),
            pick_row(shift, pair),
        )

        def advance(peer, total):
            intersection = model_intersection(pick_row(coords, pair), pick_row(fetched_coords, peer))
            term = product(product(intersection, pick_row(fetched, peer)), intersection.T)
            return total - pick_row(pick_row(weight, pair), peer) * term

        return lax.fori_loop(0, row_count, advance, local)

    mine = jnp.arange(pair_count, dtype=jnp.int32) % core_count == my_core
    share = lax.map(
        lambda pair: lax.cond(
            pick_row(mine, pair), target, lambda _: jnp.zeros_like(amplitudes[0]), pair
        ),
        jnp.arange(pair_count, dtype=jnp.int32),
    )
    residual = lax.psum(share, "rep")
    denominator = energy[:, :, None] + energy[:, None, :] - shift[:, None, None]
    return residual, amplitudes - residual / denominator


def split(value):
    high = value.astype(jnp.bfloat16)
    low = (value - high.astype(jnp.float32)).astype(jnp.bfloat16)
    return high, low


NN = (((1,), (0,)), ((), ()))
NT = (((1,), (1,)), ((), ()))
TN = (((0,), (0,)), ((), ()))


def dot(left, right, dims):
    return lax.dot_general(left, right, dims, preferred_element_type=jnp.float32)


def dot3(left, right, dims=NN):
    return (
        dot(left[0], right[0], dims) + dot(left[0], right[1], dims) + dot(left[1], right[0], dims)
    )


def overlap(column, rows):
    squared = None
    for c in range(3):
        gap = column[:, c : c + 1] - rows[c]
        squared = gap * gap if squared is None else squared + gap * gap
    return jnp.exp(-intersection_rate * squared)


def sandwich(metric, block):
    metric = split(metric)
    return dot3(split(dot3(metric, split(block))), metric, NT)


def start_all(copies):
    for copy in copies:
        copy.start()
    return copies


def request_kernel(
    sub_count, source_hbm, count_hbm, owner_hbm, wanted_ref, source_ref, count_ref, owner_ref, sems
):
    copies = start_all(
        [
            pltpu.make_async_copy(source_hbm, source_ref, sems.at[0]),
            pltpu.make_async_copy(count_hbm, count_ref, sems.at[1]),
            pltpu.make_async_copy(owner_hbm, owner_ref, sems.at[2]),
        ]
    )
    partner = lax.axis_index("pairs") ^ (3 - lax.axis_index("rep"))
    for copy in copies:
        copy.wait()
    pairs, links = source_ref.shape
    source = source_ref[...]
    pair = lax.broadcasted_iota(jnp.int32, (pairs, links), 0)
    limit = jnp.zeros_like(source)
    for p in range(pairs):
        limit = jnp.where(pair == p, count_ref[p], limit)
    live = lax.broadcasted_iota(jnp.int32, (pairs, links), 1) < limit
    wish = jnp.zeros_like(source)
    for k in range(owner_ref.shape[0]):
        place = owner_ref[k]
        use = jnp.where(lax.div(place, pairs * sub_count) == partner, lax.rem(place, pairs), 0)
        wish = jnp.where(source == k, use, wish)
    wanted_ref[...] = jnp.full((8, 128), jnp.max(jnp.where(live, wish, 0)), jnp.int32)


def gather_kernel(
    domains_hbm,
    positions_hbm,
    energy_hbm,
    block_hbm,
    coords_ref,
    payload_ref,
    domains_ref,
    positions_ref,
    energy_ref,
    table,
    sems,
):
    pairs, size = domains_ref.shape
    half = size // 2
    core = lax.axis_index("rep")
    copies = start_all(
        [
            pltpu.make_async_copy(positions_hbm, positions_ref, sems.at[0]),
            pltpu.make_async_copy(energy_hbm, energy_ref, sems.at[1]),
            pltpu.make_async_copy(domains_hbm, domains_ref, sems.at[2]),
        ]
    )
    blocks = start_all(
        [
            pltpu.make_async_copy(
                block_hbm.at[p, pl.ds(pl.multiple_of(core * half, half), half), :],
                payload_ref.at[p, pl.ds(0, half), :],
                sems.at[3 + p],
            )
            for p in range(pairs)
        ]
    )
    orbitals = positions_ref.shape[1]
    rows = table.shape[0] // 4
    whole, rest = orbitals // 128, orbitals % 128
    for c in range(4):
        table[c * rows + whole : (c + 1) * rows, :] = jnp.zeros((rows - whole, 128), jnp.float32)
    for copy in copies:
        copy.wait()
    for k in range(whole):
        table[pl.ds(k, 3, stride=rows), :] = positions_ref[:, k * 128 : (k + 1) * 128]
        table[3 * rows + k : 3 * rows + k + 1, :] = energy_ref[k * 128 : (k + 1) * 128].reshape(1, 128)
    if rest:
        table[pl.ds(whole, 3, stride=rows), :rest] = positions_ref[:, whole * 128 :]
        table[3 * rows + whole : 3 * rows + whole + 1, :rest] = energy_ref[whole * 128 :].reshape(
            1, rest
        )
    first = table[...].astype(jnp.bfloat16)
    left = table[...] - first.astype(jnp.float32)
    second = left.astype(jnp.bfloat16)
    third = (left - second.astype(jnp.float32)).astype(jnp.bfloat16)
    for p in range(pairs):
        index = domains_ref[p : p + 1, :]
        high = index // 128
        low = index - high * 128
        chosen = (lax.broadcasted_iota(jnp.int32, (rows, size), 0) == high).astype(
            jnp.float32
        ).astype(jnp.bfloat16)
        lane = lax.broadcasted_iota(jnp.int32, (128, size), 0) == low
        found = []
        for c in range(4):
            span = slice(c * rows, (c + 1) * rows)
            lines = (
                dot(first[span], chosen, TN)
                + dot(second[span], chosen, TN)
                + dot(third[span], chosen, TN)
            )
            found.append(jnp.sum(jnp.where(lane, lines, 0.0), axis=0, keepdims=True))
        found.append(jnp.zeros((COORD_ROWS - 4, size), jnp.float32))
        found = jnp.concatenate(found, axis=0)
        coords_ref[p] = found
        payload_ref[p, half:, :] = found
    for copy in blocks:
        copy.wait()


def select_kernel(asked_ref, block_ref, coords_ref, payload_ref):
    size = block_ref.shape[1]
    second = jnp.max(asked_ref[...]) > 0
    payload_ref[:size, :] = jnp.where(second, block_ref[1], block_ref[0])
    payload_ref[size:, :] = jnp.where(second, coords_ref[1], coords_ref[0])


def own_kernel(
    sub_count,
    block_ref,
    integrals_ref,
    coords_ref,
    source_ref,
    entry_ref,
    count_ref,
    owner_ref,
    fock_ref,
    pair_ref,
    occ_ref,
    share_ref,
    weight_ref,
    inverse_ref,
):
    pairs, size = block_ref.shape[0], block_ref.shape[1]
    links = source_ref.shape[1]
    core = lax.axis_index("rep")
    row = lax.axis_index("pairs")
    beside = row ^ 1
    partner = row ^ (3 - core)

    def look(m, carry):
        own_slot, near_slot, weights = carry
        weights = list(weights)
        for p in range(pairs):
            place = owner_ref[source_ref[p, m]]
            peer = lax.div(place, pairs * sub_count)
            slot = lax.rem(place, pairs)
            live = m < count_ref[p]
            value = fock_ref[entry_ref[p, m]]
            own, near, far = live & (peer == row), live & (peer == beside), live & (peer == partner)
            own_slot = jnp.where(own, slot, own_slot)
            near_slot = jnp.where(near, slot, near_slot)
            for k, hit in enumerate((own, near, far)):
                weights[3 * p + k] += jnp.where(hit, value, 0.0)
        return own_slot, near_slot, tuple(weights)

    zero = jnp.int32(0)
    own_slot, near_slot, weights = lax.fori_loop(
        0, links, look, (zero, zero, (jnp.float32(0.0),) * (3 * pairs))
    )
    for p in range(pairs):
        weight_ref[p] = jnp.full((8, 128), weights[3 * p + 2], jnp.float32)
        for slot in range(pairs):
            weight_ref[pairs + pairs * p + slot] = jnp.full(
                (8, 128), jnp.where(near_slot == slot, weights[3 * p + 1], 0.0), jnp.float32
            )
    shifts = [occ_ref[pair_ref[p, 0]] + occ_ref[pair_ref[p, 1]] for p in range(pairs)]
    columns = [coords_ref[p].T for p in range(pairs)]
    for p in range(pairs):
        inverse_ref[p] = 1.0 / (columns[p][:, 3:4] + coords_ref[p, 3:4, :] - shifts[p])

    first = core == 0
    column = jnp.where(first, columns[0], columns[1])
    shift = jnp.where(first, shifts[0], shifts[1])
    own_weight = jnp.where(first, weights[0], weights[3])
    energy = (column[:, 3:4] + coords_ref[core, 3:4, :]) * 0.5
    block = block_ref[core]
    metric = split(overlap(column, [coords_ref[core, c : c + 1, :] for c in range(3)]))
    plain = dot3(metric, split(dot3(split(block), metric)))
    scaled = dot3(metric, split(dot3(split(block * (energy - shift)), metric)))
    local = integrals_ref[core] + scaled + plain * energy
    own = overlap(column, [coords_ref[own_slot, c : c + 1, :] for c in range(3)])
    share_ref[...] = local - own_weight * sandwich(own, block_ref[own_slot])


def near_kernel(near_ref, coords_ref, weight_ref, own_ref, share_ref):
    pairs, size = share_ref.shape[0], share_ref.shape[1]
    half = size // 2
    core = lax.axis_index("rep")
    second = jnp.max(jnp.abs(weight_ref[pairs + 1]) + jnp.abs(weight_ref[2 * pairs + 1])) > 0.0
    near = jnp.where(second, near_ref[1], near_ref[0])
    part = split(near[:half, :])
    rows = [near[half + c : half + c + 1, :] for c in range(3)]
    halves = [jnp.where(core == 0, line[:, :half], line[:, half:]) for line in rows]
    for p in range(pairs):
        column = coords_ref[p].T
        weight = weight_ref[pairs + pairs * p, 0:1, 0:1] + weight_ref[pairs + pairs * p + 1, 0:1, 0:1]
        whole = split(overlap(column, rows))
        side = split(overlap(column, halves))
        term = dot3(side, split(dot3(part, whole, NT)))
        share_ref[p] = jnp.where(core == p, own_ref[...], 0.0) - weight * term


def far_kernel(far_ref, coords_ref, share_ref, weight_ref, total_ref):
    pairs, size = share_ref.shape[0], share_ref.shape[1]
    block = split(far_ref[:size, :])
    rows = [far_ref[size + c : size + c + 1, :] for c in range(3)]
    for p in range(pairs):
        metric = split(overlap(coords_ref[p].T, rows))
        term = dot3(split(dot3(metric, block)), metric, NT)
        total_ref[p] = share_ref[p] - weight_ref[p, 0:1, 0:1] * term


def call(body, outs, spaces, args, scratch=(), flops=0, moved=0, limit=VMEM_LIMIT):
    return pl.pallas_call(
        body,
        out_shape=outs,
        in_specs=[pl.BlockSpec(memory_space=space) for space in spaces],
        out_specs=jax.tree.map(lambda _: pl.BlockSpec(memory_space=pltpu.VMEM), outs),
        scratch_shapes=list(scratch),
        compiler_params=pltpu.CompilerParams(vmem_limit_bytes=limit),
        cost_estimate=pl.CostEstimate(flops=flops, bytes_accessed=moved, transcendentals=0),
    )(*args)


def on_device_four(
    amplitudes,
    exchange_ints,
    pair_list,
    domains,
    link_source,
    link_entry,
    link_count,
    owner_map,
    fock_values,
    occ_energy,
    vir_energy,
    positions,
):
    pairs, size = amplitudes.shape[0], amplitudes.shape[1]
    sub_count = lax.axis_size("sub")
    core = lax.axis_index("rep")
    row = lax.axis_index("pairs")
    axes = ("pairs", "rep")
    across = [(2 * z + c, 2 * (z ^ (3 - c)) + c) for z in range(4) for c in range(2)]
    beside = [(2 * z + c, 2 * (z ^ 1) + c) for z in range(4) for c in range(2)]
    f32 = jnp.float32
    V, S = pltpu.VMEM, pltpu.SMEM

    H = pltpu.HBM
    wanted = call(
        functools.partial(request_kernel, sub_count),
        jax.ShapeDtypeStruct((8, 128), jnp.int32),
        (H, H, H),
        (link_source, link_count, owner_map),
        scratch=[
            V(link_source.shape, jnp.int32),
            S(link_count.shape, jnp.int32),
            S(owner_map.shape, jnp.int32),
            pltpu.SemaphoreType.DMA((3,)),
        ],
        limit=None,
    )
    asked = lax.ppermute(wanted, axes, across)

    lines = -(-positions.shape[1] // 128)
    lines = -(-lines // 16) * 16
    coords, near = call(
        gather_kernel,
        (
            jax.ShapeDtypeStruct((pairs, COORD_ROWS, size), f32),
            jax.ShapeDtypeStruct((pairs, size // 2 + COORD_ROWS, size), f32),
        ),
        (H, H, H, H),
        (domains, positions, vir_energy, amplitudes),
        limit=None,
        scratch=[
            V(domains.shape, jnp.int32),
            V(positions.shape, f32),
            V(vir_energy.shape, f32),
            V((4 * lines, 128), f32),
            pltpu.SemaphoreType.DMA((3 + pairs,)),
        ],
        flops=10**9,
        moved=10**6,
    )
    near = lax.ppermute(near, axes, beside)
    far = call(
        select_kernel,
        jax.ShapeDtypeStruct((size + COORD_ROWS, size), f32),
        (V, V, V),
        (asked, amplitudes, coords),
        moved=10**6,
    )
    far = lax.ppermute(far, axes, across)
    own, weight, inverse = call(
        functools.partial(own_kernel, sub_count),
        (
            jax.ShapeDtypeStruct(amplitudes.shape[1:], f32),
            jax.ShapeDtypeStruct((pairs + pairs * pairs, 8, 128), f32),
            jax.ShapeDtypeStruct(amplitudes.shape, f32),
        ),
        (V, V, V, S, S, S, S, S, S, S),
        (
            amplitudes,
            exchange_ints,
            coords,
            link_source,
            link_entry,
            link_count,
            owner_map,
            fock_values,
            pair_list,
            occ_energy,
        ),
        flops=5 * 10**9,
        moved=10**7,
    )
    share = call(
        near_kernel,
        jax.ShapeDtypeStruct(amplitudes.shape, f32),
        (V, V, V, V),
        (near, coords, weight, own),
        flops=10**9,
        moved=10**6,
    )
    total = call(
        far_kernel,
        jax.ShapeDtypeStruct(amplitudes.shape, f32),
        (V, V, V, V),
        (far, coords, share, weight),
        flops=10**9,
        moved=10**6,
    )
    residual = total + lax.ppermute(total, "rep", [(0, 1), (1, 0)])
    return residual, amplitudes - residual * inverse


def solution(mesh):
    stored = ("groups", "pairs", "sub")
    in_specs = (
        P(stored, None, None),
        P(stored, None, None),
        P(stored, None),
        P(stored, None),
        P(stored, None),
        P(stored, None),
        P(stored),
        P("groups"),
        P("groups"),
        P("groups"),
        P("groups"),
        P(None, "groups"),
    )
    out_specs = (P(stored, None, None), P(stored, None, None))

    def run(*args):
        devices = mesh.shape["groups"] * mesh.shape["pairs"] * mesh.shape["sub"]
        known = (
            mesh.shape["pairs"] == 4
            and mesh.shape["rep"] == 2
            and args[0].shape[0] == 2 * devices
            and args[0].shape[1] == 256
        )
        return jax.shard_map(
            on_device_four if known else on_device_any,
            mesh=mesh,
            in_specs=in_specs,
            out_specs=out_specs,
            check_vma=False,
        )(*args)

    return run
```

```python
import functools

import jax
import jax.numpy as jnp
from jax import lax
from jax.experimental import pallas as pl
from jax.experimental.pallas import tpu as pltpu
from jax.sharding import PartitionSpec as P

intersection_rate = 2.0
COORD_ROWS = 8
VMEM_LIMIT = 40 * 1024 * 1024


def product(left, right):
    return jnp.dot(left, right, precision=lax.Precision.HIGHEST, preferred_element_type=jnp.float32)


def pick_row(array, index):
    return lax.dynamic_index_in_dim(array, index, 0, keepdims=False)


def model_intersection(left_coords, right_coords):
    squared = jnp.zeros((left_coords.shape[1], right_coords.shape[1]), jnp.float32)
    for component in range(3):
        gap_now = left_coords[component][:, None] - right_coords[component][None, :]
        squared = squared + gap_now * gap_now
    return jnp.exp(-intersection_rate * squared)


def pair_local(block, integrals, pair_coords, pair_energy, pair_shift):
    metric = model_intersection(pair_coords, pair_coords)
    virtual_fock = metric * ((pair_energy[:, None] + pair_energy[None, :]) * 0.5)
    right_side = product(block, metric)
    left_side = product(metric, block)
    return (
        integrals
        + product(virtual_fock, right_side)
        + product(left_side, virtual_fock)
        - pair_shift * product(metric, right_side)
    )


def on_device_any(
    amplitudes,
    exchange_ints,
    pair_list,
    domains,
    link_source,
    link_entry,
    link_count,
    owner_map,
    fock_values,
    occ_energy,
    vir_energy,
    positions,
):
    pair_count = amplitudes.shape[0]
    link_slots = link_source.shape[1]
    row_count = lax.axis_size("pairs")
    sub_count = lax.axis_size("sub")
    core_count = lax.axis_size("rep")
    my_core = lax.axis_index("rep")
    coords = jnp.moveaxis(jnp.take(positions, domains, axis=1), 0, 1)
    energy = jnp.take(vir_energy, domains, axis=0)
    shift = jnp.take(occ_energy, pair_list[:, 0]) + jnp.take(occ_energy, pair_list[:, 1])
    is_live = jnp.arange(link_slots, dtype=jnp.int32)[None, :] < link_count[:, None]
    source_loc = jnp.take(owner_map, link_source)
    source_peer = source_loc // (pair_count * sub_count)
    source_slot = source_loc % pair_count
    peers = jnp.arange(row_count, dtype=jnp.int32)
    matched = is_live[:, :, None] & (source_peer[:, :, None] == peers[None, None, :])
    fock_weight = jnp.take(fock_values, link_entry)
    weight = jnp.sum(jnp.where(matched, fock_weight[:, :, None], 0.0), axis=1)
    wanted = jnp.max(jnp.where(matched, source_slot[:, :, None], 0), axis=(0, 1))
    asked = lax.all_to_all(wanted[:, None], "pairs", split_axis=0, concat_axis=0, tiled=True)[:, 0]
    fetched = lax.all_to_all(
        jnp.take(amplitudes, asked, axis=0), "pairs", split_axis=0, concat_axis=0, tiled=True
    )
    fetched_coords = lax.all_to_all(
        jnp.take(coords, asked, axis=0), "pairs", split_axis=0, concat_axis=0, tiled=True
    )

    def target(pair):
        local = pair_local(
            pick_row(amplitudes, pair),
            pick_row(exchange_ints, pair),
            pick_row(coords, pair),
            pick_row(energy, pair),
            pick_row(shift, pair),
        )

        def advance(peer, total):
            intersection = model_intersection(pick_row(coords, pair), pick_row(fetched_coords, peer))
            term = product(product(intersection, pick_row(fetched, peer)), intersection.T)
            return total - pick_row(pick_row(weight, pair), peer) * term

        return lax.fori_loop(0, row_count, advance, local)

    mine = jnp.arange(pair_count, dtype=jnp.int32) % core_count == my_core
    share = lax.map(
        lambda pair: lax.cond(
            pick_row(mine, pair), target, lambda _: jnp.zeros_like(amplitudes[0]), pair
        ),
        jnp.arange(pair_count, dtype=jnp.int32),
    )
    residual = lax.psum(share, "rep")
    denominator = energy[:, :, None] + energy[:, None, :] - shift[:, None, None]
    return residual, amplitudes - residual / denominator


def split(value):
    high = value.astype(jnp.bfloat16)
    low = (value - high.astype(jnp.float32)).astype(jnp.bfloat16)
    return high, low


NN = (((1,), (0,)), ((), ()))
NT = (((1,), (1,)), ((), ()))
TN = (((0,), (0,)), ((), ()))


def dot(left, right, dims):
    return lax.dot_general(left, right, dims, preferred_element_type=jnp.float32)


def dot3(left, right, dims=NN):
    return (
        dot(left[0], right[0], dims) + dot(left[0], right[1], dims) + dot(left[1], right[0], dims)
    )


def overlap(column, rows):
    squared = None
    for c in range(3):
        gap = column[:, c : c + 1] - rows[c]
        squared = gap * gap if squared is None else squared + gap * gap
    return jnp.exp(-intersection_rate * squared)


def sandwich(metric, block):
    metric = split(metric)
    return dot3(split(dot3(metric, split(block))), metric, NT)


def start_all(copies):
    for copy in copies:
        copy.start()
    return copies


def request_kernel(
    sub_count, source_hbm, count_hbm, owner_hbm, wanted_ref, source_ref, count_ref, owner_ref, sems
):
    copies = start_all(
        [
            pltpu.make_async_copy(source_hbm, source_ref, sems.at[0]),
            pltpu.make_async_copy(count_hbm, count_ref, sems.at[1]),
            pltpu.make_async_copy(owner_hbm, owner_ref, sems.at[2]),
        ]
    )
    partner = lax.axis_index("pairs") ^ (3 - lax.axis_index("rep"))
    for copy in copies:
        copy.wait()
    pairs, links = source_ref.shape
    source = source_ref[...]
    pair = lax.broadcasted_iota(jnp.int32, (pairs, links), 0)
    limit = jnp.zeros_like(source)
    for p in range(pairs):
        limit = jnp.where(pair == p, count_ref[p], limit)
    live = lax.broadcasted_iota(jnp.int32, (pairs, links), 1) < limit
    wish = jnp.zeros_like(source)
    for k in range(owner_ref.shape[0]):
        place = owner_ref[k]
        use = jnp.where(lax.div(place, pairs * sub_count) == partner, lax.rem(place, pairs), 0)
        wish = jnp.where(source == k, use, wish)
    wanted_ref[...] = jnp.full((8, 128), jnp.max(jnp.where(live, wish, 0)), jnp.int32)


def gather_kernel(
    domains_hbm,
    positions_hbm,
    energy_hbm,
    block_hbm,
    coords_ref,
    payload_ref,
    domains_ref,
    positions_ref,
    energy_ref,
    table,
    sems,
):
    pairs, size = domains_ref.shape
    half = size // 2
    core = lax.axis_index("rep")
    copies = start_all(
        [
            pltpu.make_async_copy(positions_hbm, positions_ref, sems.at[0]),
            pltpu.make_async_copy(energy_hbm, energy_ref, sems.at[1]),
            pltpu.make_async_copy(domains_hbm, domains_ref, sems.at[2]),
        ]
    )
    blocks = start_all(
        [
            pltpu.make_async_copy(
                block_hbm.at[p, pl.ds(pl.multiple_of(core * half, half), half), :],
                payload_ref.at[p, pl.ds(0, half), :],
                sems.at[3 + p],
            )
            for p in range(pairs)
        ]
    )
    orbitals = positions_ref.shape[1]
    rows = table.shape[0] // 4
    whole, rest = orbitals // 128, orbitals % 128
    for c in range(4):
        table[c * rows + whole : (c + 1) * rows, :] = jnp.zeros((rows - whole, 128), jnp.float32)
    for copy in copies:
        copy.wait()
    for k in range(whole):
        table[pl.ds(k, 3, stride=rows), :] = positions_ref[:, k * 128 : (k + 1) * 128]
        table[3 * rows + k : 3 * rows + k + 1, :] = energy_ref[k * 128 : (k + 1) * 128].reshape(1, 128)
    if rest:
        table[pl.ds(whole, 3, stride=rows), :rest] = positions_ref[:, whole * 128 :]
        table[3 * rows + whole : 3 * rows + whole + 1, :rest] = energy_ref[whole * 128 :].reshape(
            1, rest
        )
    first = table[...].astype(jnp.bfloat16)
    left = table[...] - first.astype(jnp.float32)
    second = left.astype(jnp.bfloat16)
    third = (left - second.astype(jnp.float32)).astype(jnp.bfloat16)
    for p in range(pairs):
        index = domains_ref[p : p + 1, :]
        high = index // 128
        low = index - high * 128
        chosen = (lax.broadcasted_iota(jnp.int32, (rows, size), 0) == high).astype(
            jnp.float32
        ).astype(jnp.bfloat16)
        lane = lax.broadcasted_iota(jnp.int32, (128, size), 0) == low
        found = []
        for c in range(4):
            span = slice(c * rows, (c + 1) * rows)
            lines = (
                dot(first[span], chosen, TN)
                + dot(second[span], chosen, TN)
                + dot(third[span], chosen, TN)
            )
            found.append(jnp.sum(jnp.where(lane, lines, 0.0), axis=0, keepdims=True))
        found.append(jnp.zeros((COORD_ROWS - 4, size), jnp.float32))
        found = jnp.concatenate(found, axis=0)
        coords_ref[p] = found
        payload_ref[p, half:, :] = found
    for copy in blocks:
        copy.wait()


def select_kernel(asked_ref, block_ref, coords_ref, payload_ref):
    size = block_ref.shape[1]
    second = jnp.max(asked_ref[...]) > 0
    payload_ref[:size, :] = jnp.where(second, block_ref[1], block_ref[0])
    payload_ref[size:, :] = jnp.where(second, coords_ref[1], coords_ref[0])


def own_kernel(
    sub_count,
    block_ref,
    integrals_ref,
    coords_ref,
    source_ref,
    entry_ref,
    count_ref,
    owner_ref,
    fock_ref,
    pair_ref,
    occ_ref,
    share_ref,
    weight_ref,
    inverse_ref,
):
    pairs, size = block_ref.shape[0], block_ref.shape[1]
    links = source_ref.shape[1]
    core = lax.axis_index("rep")
    row = lax.axis_index("pairs")
    beside = row ^ 1
    partner = row ^ (3 - core)

    def look(m, carry):
        own_slot, near_slot, weights = carry
        weights = list(weights)
        for p in range(pairs):
            place = owner_ref[source_ref[p, m]]
            peer = lax.div(place, pairs * sub_count)
            slot = lax.rem(place, pairs)
            live = m < count_ref[p]
            value = fock_ref[entry_ref[p, m]]
            own, near, far = live & (peer == row), live & (peer == beside), live & (peer == partner)
            own_slot = jnp.where(own, slot, own_slot)
            near_slot = jnp.where(near, slot, near_slot)
            for k, hit in enumerate((own, near, far)):
                weights[3 * p + k] += jnp.where(hit, value, 0.0)
        return own_slot, near_slot, tuple(weights)

    zero = jnp.int32(0)
    own_slot, near_slot, weights = lax.fori_loop(
        0, links, look, (zero, zero, (jnp.float32(0.0),) * (3 * pairs))
    )
    for p in range(pairs):
        weight_ref[p] = jnp.full((8, 128), weights[3 * p + 2], jnp.float32)
        for slot in range(pairs):
            weight_ref[pairs + pairs * p + slot] = jnp.full(
                (8, 128), jnp.where(near_slot == slot, weights[3 * p + 1], 0.0), jnp.float32
            )
    shifts = [occ_ref[pair_ref[p, 0]] + occ_ref[pair_ref[p, 1]] for p in range(pairs)]
    columns = [coords_ref[p].T for p in range(pairs)]
    for p in range(pairs):
        inverse_ref[p] = 1.0 / (columns[p][:, 3:4] + coords_ref[p, 3:4, :] - shifts[p])

    first = core == 0
    column = jnp.where(first, columns[0], columns[1])
    shift = jnp.where(first, shifts[0], shifts[1])
    own_weight = jnp.where(first, weights[0], weights[3])
    energy = (column[:, 3:4] + coords_ref[core, 3:4, :]) * 0.5
    block = block_ref[core]
    metric = split(overlap(column, [coords_ref[core, c : c + 1, :] for c in range(3)]))
    plain = dot3(metric, split(dot3(split(block), metric)))
    scaled = dot3(metric, split(dot3(split(block * (energy - shift)), metric)))
    local = integrals_ref[core] + scaled + plain * energy
    own = overlap(column, [coords_ref[own_slot, c : c + 1, :] for c in range(3)])
    share_ref[...] = local - own_weight * sandwich(own, block_ref[own_slot])


def near_kernel(near_ref, coords_ref, weight_ref, own_ref, share_ref):
    pairs, size = share_ref.shape[0], share_ref.shape[1]
    half = size // 2
    core = lax.axis_index("rep")
    second = jnp.max(jnp.abs(weight_ref[pairs + 1]) + jnp.abs(weight_ref[2 * pairs + 1])) > 0.0
    near = jnp.where(second, near_ref[1], near_ref[0])
    part = split(near[:half, :])
    rows = [near[half + c : half + c + 1, :] for c in range(3)]
    halves = [jnp.where(core == 0, line[:, :half], line[:, half:]) for line in rows]
    for p in range(pairs):
        column = coords_ref[p].T
        weight = weight_ref[pairs + pairs * p, 0:1, 0:1] + weight_ref[pairs + pairs * p + 1, 0:1, 0:1]
        whole = split(overlap(column, rows))
        side = split(overlap(column, halves))
        term = dot3(side, split(dot3(part, whole, NT)))
        share_ref[p] = jnp.where(core == p, own_ref[...], 0.0) - weight * term


def far_kernel(far_ref, coords_ref, share_ref, weight_ref, total_ref):
    pairs, size = share_ref.shape[0], share_ref.shape[1]
    block = split(far_ref[:size, :])
    rows = [far_ref[size + c : size + c + 1, :] for c in range(3)]
    for p in range(pairs):
        metric = split(overlap(coords_ref[p].T, rows))
        term = dot3(split(dot3(metric, block)), metric, NT)
        total_ref[p] = share_ref[p] - weight_ref[p, 0:1, 0:1] * term


def call(body, outs, spaces, args, scratch=(), flops=0, moved=0, limit=VMEM_LIMIT):
    return pl.pallas_call(
        body,
        out_shape=outs,
        in_specs=[pl.BlockSpec(memory_space=space) for space in spaces],
        out_specs=jax.tree.map(lambda _: pl.BlockSpec(memory_space=pltpu.VMEM), outs),
        scratch_shapes=list(scratch),
        compiler_params=pltpu.CompilerParams(vmem_limit_bytes=limit),
        cost_estimate=pl.CostEstimate(flops=flops, bytes_accessed=moved, transcendentals=0),
    )(*args)


def on_device_four(
    amplitudes,
    exchange_ints,
    pair_list,
    domains,
    link_source,
    link_entry,
    link_count,
    owner_map,
    fock_values,
    occ_energy,
    vir_energy,
    positions,
):
    pairs, size = amplitudes.shape[0], amplitudes.shape[1]
    sub_count = lax.axis_size("sub")
    core = lax.axis_index("rep")
    row = lax.axis_index("pairs")
    axes = ("pairs", "rep")
    across = [(2 * z + c, 2 * (z ^ (3 - c)) + c) for z in range(4) for c in range(2)]
    beside = [(2 * z + c, 2 * (z ^ 1) + c) for z in range(4) for c in range(2)]
    f32 = jnp.float32
    V, S = pltpu.VMEM, pltpu.SMEM

    H = pltpu.HBM
    wanted = call(
        functools.partial(request_kernel, sub_count),
        jax.ShapeDtypeStruct((8, 128), jnp.int32),
        (H, H, H),
        tuple(pltpu.with_memory_space_constraint(a, pltpu.HBM) for a in (link_source, link_count, owner_map)),
        scratch=[
            V(link_source.shape, jnp.int32),
            S(link_count.shape, jnp.int32),
            S(owner_map.shape, jnp.int32),
            pltpu.SemaphoreType.DMA((3,)),
        ],
    )
    asked = lax.ppermute(wanted, axes, across)

    lines = -(-positions.shape[1] // 128)
    lines = -(-lines // 16) * 16
    coords, near = call(
        gather_kernel,
        (
            jax.ShapeDtypeStruct((pairs, COORD_ROWS, size), f32),
            jax.ShapeDtypeStruct((pairs, size // 2 + COORD_ROWS, size), f32),
        ),
        (H, H, H, H),
        tuple(pltpu.with_memory_space_constraint(a, pltpu.HBM) for a in (domains, positions, vir_energy, amplitudes)),
        scratch=[
            V(domains.shape, jnp.int32),
            V(positions.shape, f32),
            V(vir_energy.shape, f32),
            V((4 * lines, 128), f32),
            pltpu.SemaphoreType.DMA((3 + pairs,)),
        ],
        flops=10**9,
        moved=10**6,
    )
    near = lax.ppermute(near, axes, beside)
    far = call(
        select_kernel,
        jax.ShapeDtypeStruct((size + COORD_ROWS, size), f32),
        (V, V, V),
        (asked, amplitudes, coords),
        moved=10**6,
    )
    far = lax.ppermute(far, axes, across)
    own, weight, inverse = call(
        functools.partial(own_kernel, sub_count),
        (
            jax.ShapeDtypeStruct(amplitudes.shape[1:], f32),
            jax.ShapeDtypeStruct((pairs + pairs * pairs, 8, 128), f32),
            jax.ShapeDtypeStruct(amplitudes.shape, f32),
        ),
        (V, V, V, S, S, S, S, S, S, S),
        (
            amplitudes,
            exchange_ints,
            coords,
            link_source,
            link_entry,
            link_count,
            owner_map,
            fock_values,
            pair_list,
            occ_energy,
        ),
        flops=5 * 10**9,
        moved=10**7,
    )
    share = call(
        near_kernel,
        jax.ShapeDtypeStruct(amplitudes.shape, f32),
        (V, V, V, V),
        (near, coords, weight, own),
        flops=10**9,
        moved=10**6,
    )
    total = call(
        far_kernel,
        jax.ShapeDtypeStruct(amplitudes.shape, f32),
        (V, V, V, V),
        (far, coords, share, weight),
        flops=10**9,
        moved=10**6,
    )
    residual = total + lax.ppermute(total, "rep", [(0, 1), (1, 0)])
    return residual, amplitudes - residual * inverse


def solution(mesh):
    stored = ("groups", "pairs", "sub")
    in_specs = (
        P(stored, None, None),
        P(stored, None, None),
        P(stored, None),
        P(stored, None),
        P(stored, None),
        P(stored, None),
        P(stored),
        P("groups"),
        P("groups"),
        P("groups"),
        P("groups"),
        P(None, "groups"),
    )
    out_specs = (P(stored, None, None), P(stored, None, None))

    def run(*args):
        devices = mesh.shape["groups"] * mesh.shape["pairs"] * mesh.shape["sub"]
        known = (
            mesh.shape["pairs"] == 4
            and mesh.shape["rep"] == 2
            and args[0].shape[0] == 2 * devices
            and args[0].shape[1] == 256
        )
        return jax.shard_map(
            on_device_four if known else on_device_any,
            mesh=mesh,
            in_specs=in_specs,
            out_specs=out_specs,
            check_vma=False,
        )(*args)

    return run
```

```python
import functools

import jax
import jax.numpy as jnp
from jax import lax
from jax.experimental import pallas as pl
from jax.experimental.pallas import tpu as pltpu
from jax.sharding import PartitionSpec as P

intersection_rate = 2.0
COORD_ROWS = 8
VMEM_LIMIT = 40 * 1024 * 1024


def product(left, right):
    return jnp.dot(left, right, precision=lax.Precision.HIGHEST, preferred_element_type=jnp.float32)


def pick_row(array, index):
    return lax.dynamic_index_in_dim(array, index, 0, keepdims=False)


def model_intersection(left_coords, right_coords):
    squared = jnp.zeros((left_coords.shape[1], right_coords.shape[1]), jnp.float32)
    for component in range(3):
        gap_now = left_coords[component][:, None] - right_coords[component][None, :]
        squared = squared + gap_now * gap_now
    return jnp.exp(-intersection_rate * squared)


def pair_local(block, integrals, pair_coords, pair_energy, pair_shift):
    metric = model_intersection(pair_coords, pair_coords)
    virtual_fock = metric * ((pair_energy[:, None] + pair_energy[None, :]) * 0.5)
    right_side = product(block, metric)
    left_side = product(metric, block)
    return (
        integrals
        + product(virtual_fock, right_side)
        + product(left_side, virtual_fock)
        - pair_shift * product(metric, right_side)
    )


def on_device_any(
    amplitudes,
    exchange_ints,
    pair_list,
    domains,
    link_source,
    link_entry,
    link_count,
    owner_map,
    fock_values,
    occ_energy,
    vir_energy,
    positions,
):
    pair_count = amplitudes.shape[0]
    link_slots = link_source.shape[1]
    row_count = lax.axis_size("pairs")
    sub_count = lax.axis_size("sub")
    core_count = lax.axis_size("rep")
    my_core = lax.axis_index("rep")
    coords = jnp.moveaxis(jnp.take(positions, domains, axis=1), 0, 1)
    energy = jnp.take(vir_energy, domains, axis=0)
    shift = jnp.take(occ_energy, pair_list[:, 0]) + jnp.take(occ_energy, pair_list[:, 1])
    is_live = jnp.arange(link_slots, dtype=jnp.int32)[None, :] < link_count[:, None]
    source_loc = jnp.take(owner_map, link_source)
    source_peer = source_loc // (pair_count * sub_count)
    source_slot = source_loc % pair_count
    peers = jnp.arange(row_count, dtype=jnp.int32)
    matched = is_live[:, :, None] & (source_peer[:, :, None] == peers[None, None, :])
    fock_weight = jnp.take(fock_values, link_entry)
    weight = jnp.sum(jnp.where(matched, fock_weight[:, :, None], 0.0), axis=1)
    wanted = jnp.max(jnp.where(matched, source_slot[:, :, None], 0), axis=(0, 1))
    asked = lax.all_to_all(wanted[:, None], "pairs", split_axis=0, concat_axis=0, tiled=True)[:, 0]
    fetched = lax.all_to_all(
        jnp.take(amplitudes, asked, axis=0), "pairs", split_axis=0, concat_axis=0, tiled=True
    )
    fetched_coords = lax.all_to_all(
        jnp.take(coords, asked, axis=0), "pairs", split_axis=0, concat_axis=0, tiled=True
    )

    def target(pair):
        local = pair_local(
            pick_row(amplitudes, pair),
            pick_row(exchange_ints, pair),
            pick_row(coords, pair),
            pick_row(energy, pair),
            pick_row(shift, pair),
        )

        def advance(peer, total):
            intersection = model_intersection(pick_row(coords, pair), pick_row(fetched_coords, peer))
            term = product(product(intersection, pick_row(fetched, peer)), intersection.T)
            return total - pick_row(pick_row(weight, pair), peer) * term

        return lax.fori_loop(0, row_count, advance, local)

    mine = jnp.arange(pair_count, dtype=jnp.int32) % core_count == my_core
    share = lax.map(
        lambda pair: lax.cond(
            pick_row(mine, pair), target, lambda _: jnp.zeros_like(amplitudes[0]), pair
        ),
        jnp.arange(pair_count, dtype=jnp.int32),
    )
    residual = lax.psum(share, "rep")
    denominator = energy[:, :, None] + energy[:, None, :] - shift[:, None, None]
    return residual, amplitudes - residual / denominator


def split(value):
    high = value.astype(jnp.bfloat16)
    low = (value - high.astype(jnp.float32)).astype(jnp.bfloat16)
    return high, low


NN = (((1,), (0,)), ((), ()))
NT = (((1,), (1,)), ((), ()))
TN = (((0,), (0,)), ((), ()))


def dot(left, right, dims):
    return lax.dot_general(left, right, dims, preferred_element_type=jnp.float32)


def dot3(left, right, dims=NN):
    return (
        dot(left[0], right[0], dims) + dot(left[0], right[1], dims) + dot(left[1], right[0], dims)
    )


def overlap(column, rows):
    squared = None
    for c in range(3):
        gap = column[:, c : c + 1] - rows[c : c + 1, :]
        squared = gap * gap if squared is None else squared + gap * gap
    return jnp.exp(-intersection_rate * squared)


def sandwich(metric, block):
    metric = split(metric)
    return dot3(split(dot3(metric, split(block))), metric, NT)


def start_all(copies):
    for copy in copies:
        copy.start()
    return copies


def open_kernel(
    sub_count,
    source_hbm,
    count_hbm,
    owner_hbm,
    positions_hbm,
    energy_hbm,
    domains_hbm,
    wanted_ref,
    positions_ref,
    energy_ref,
    domains_ref,
    source_ref,
    count_ref,
    owner_ref,
    sems,
):
    pairs_of = (
        (source_hbm, source_ref),
        (count_hbm, count_ref),
        (owner_hbm, owner_ref),
        (positions_hbm, positions_ref),
        (energy_hbm, energy_ref),
        (domains_hbm, domains_ref),
    )
    copies = [
        pltpu.make_async_copy(source, target, sems.at[k])
        for k, (source, target) in enumerate(pairs_of)
    ]
    for copy in copies:
        copy.start()
    peer = lax.axis_index("pairs") ^ (3 - lax.axis_index("rep"))
    for copy in copies[:3]:
        copy.wait()
    pairs, links = source_ref.shape
    source = source_ref[...]
    pair = lax.broadcasted_iota(jnp.int32, (pairs, links), 0)
    limit = jnp.zeros_like(source)
    for p in range(pairs):
        limit = jnp.where(pair == p, count_ref[p], limit)
    live = lax.broadcasted_iota(jnp.int32, (pairs, links), 1) < limit
    wish = jnp.zeros_like(source)
    for k in range(owner_ref.shape[0]):
        place = owner_ref[k]
        use = jnp.where(lax.div(place, pairs * sub_count) == peer, lax.rem(place, pairs), 0)
        wish = jnp.where(source == k, use, wish)
    wanted_ref[...] = jnp.full((8, 128), jnp.max(jnp.where(live, wish, 0)), jnp.int32)
    for copy in copies[3:]:
        copy.wait()


def gather_kernel(
    domains_ref, positions_ref, energy_ref, block_hbm, blocks_ref, halves_ref, table, sems
):
    pairs, size = domains_ref.shape
    half = size // 2
    start = pl.multiple_of(lax.axis_index("rep") * half, half)
    copies = [
        pltpu.make_async_copy(block_hbm.at[p], blocks_ref.at[p, pl.ds(0, size), :], sems.at[p])
        for p in range(pairs)
    ] + [
        pltpu.make_async_copy(
            block_hbm.at[p, pl.ds(start, half), :],
            halves_ref.at[p, pl.ds(0, half), :],
            sems.at[pairs + p],
        )
        for p in range(pairs)
    ]
    for copy in copies:
        copy.start()
    orbitals = positions_ref.shape[1]
    rows = table.shape[0] // 4
    whole, rest = orbitals // 128, orbitals % 128
    for c in range(4):
        table[c * rows + whole : (c + 1) * rows, :] = jnp.zeros((rows - whole, 128), jnp.float32)
    for k in range(whole):
        table[pl.ds(k, 3, stride=rows), :] = positions_ref[:, k * 128 : (k + 1) * 128]
        table[3 * rows + k : 3 * rows + k + 1, :] = energy_ref[k * 128 : (k + 1) * 128].reshape(1, 128)
    if rest:
        table[pl.ds(whole, 3, stride=rows), :rest] = positions_ref[:, whole * 128 :]
        table[3 * rows + whole : 3 * rows + whole + 1, :rest] = energy_ref[whole * 128 :].reshape(
            1, rest
        )
    first = table[...].astype(jnp.bfloat16)
    left = table[...] - first.astype(jnp.float32)
    second = left.astype(jnp.bfloat16)
    third = (left - second.astype(jnp.float32)).astype(jnp.bfloat16)
    for p in range(pairs):
        index = domains_ref[p : p + 1, :]
        high = index // 128
        low = index - high * 128
        chosen = (lax.broadcasted_iota(jnp.int32, (rows, size), 0) == high).astype(
            jnp.float32
        ).astype(jnp.bfloat16)
        lane = lax.broadcasted_iota(jnp.int32, (128, size), 0) == low
        found = []
        for c in range(4):
            span = slice(c * rows, (c + 1) * rows)
            lines = (
                dot(first[span], chosen, TN)
                + dot(second[span], chosen, TN)
                + dot(third[span], chosen, TN)
            )
            found.append(jnp.sum(jnp.where(lane, lines, 0.0), axis=0, keepdims=True))
        found.append(jnp.zeros((COORD_ROWS - 4, size), jnp.float32))
        found = jnp.concatenate(found, axis=0)
        blocks_ref[p, size:, :] = found
        halves_ref[p, half:, :] = found
    for copy in copies:
        copy.wait()


def select_kernel(asked_ref, blocks_ref, chosen_ref):
    second = jnp.max(asked_ref[...]) > 0
    chosen_ref[...] = jnp.where(second, blocks_ref[1], blocks_ref[0])


def own_kernel(
    sub_count,
    block_ref,
    integrals_ref,
    source_ref,
    entry_ref,
    count_ref,
    owner_ref,
    fock_ref,
    pair_ref,
    occ_ref,
    share_ref,
    weight_ref,
    inverse_ref,
):
    pairs, size = integrals_ref.shape[0], integrals_ref.shape[1]
    links = source_ref.shape[1]
    core = lax.axis_index("rep")
    row = lax.axis_index("pairs")
    beside = row ^ 1
    partner = row ^ (3 - core)

    def look(m, carry):
        own_slot, near_slot, weights = carry
        weights = list(weights)
        for p in range(pairs):
            place = owner_ref[source_ref[p, m]]
            peer = lax.div(place, pairs * sub_count)
            slot = lax.rem(place, pairs)
            live = m < count_ref[p]
            value = fock_ref[entry_ref[p, m]]
            own, near, far = live & (peer == row), live & (peer == beside), live & (peer == partner)
            own_slot = jnp.where(own, slot, own_slot)
            near_slot = jnp.where(near, slot, near_slot)
            for k, hit in enumerate((own, near, far)):
                weights[3 * p + k] += jnp.where(hit, value, 0.0)
        return own_slot, near_slot, tuple(weights)

    zero = jnp.int32(0)
    own_slot, near_slot, weights = lax.fori_loop(
        0, links, look, (zero, zero, (jnp.float32(0.0),) * (3 * pairs))
    )
    for p in range(pairs):
        weight_ref[p] = jnp.full((8, 128), weights[3 * p + 2], jnp.float32)
        for slot in range(pairs):
            weight_ref[pairs + pairs * p + slot] = jnp.full(
                (8, 128), jnp.where(near_slot == slot, weights[3 * p + 1], 0.0), jnp.float32
            )
    shifts = [occ_ref[pair_ref[p, 0]] + occ_ref[pair_ref[p, 1]] for p in range(pairs)]
    columns = [block_ref[p, size:, :].T for p in range(pairs)]
    for p in range(pairs):
        inverse_ref[p] = 1.0 / (columns[p][:, 3:4] + block_ref[p, size + 3 : size + 4, :] - shifts[p])

    first = core == 0
    column = jnp.where(first, columns[0], columns[1])
    shift = jnp.where(first, shifts[0], shifts[1])
    own_weight = jnp.where(first, weights[0], weights[3])
    mine = block_ref[core, size:, :]
    energy = (column[:, 3:4] + mine[3:4, :]) * 0.5
    block = block_ref[core, :size, :]
    metric = split(overlap(column, mine))
    plain = dot3(metric, split(dot3(split(block), metric)))
    scaled = dot3(metric, split(dot3(split(block * (energy - shift)), metric)))
    local = integrals_ref[core] + scaled + plain * energy
    own = overlap(column, block_ref[own_slot, size:, :])
    share_ref[...] = local - own_weight * sandwich(own, block_ref[own_slot, :size, :])


def near_kernel(near_ref, blocks_ref, weight_ref, own_ref, share_ref):
    pairs, size = share_ref.shape[0], share_ref.shape[1]
    half = size // 2
    core = lax.axis_index("rep")
    second = jnp.max(jnp.abs(weight_ref[pairs + 1]) + jnp.abs(weight_ref[2 * pairs + 1])) > 0.0
    near = jnp.where(second, near_ref[1], near_ref[0])
    part = split(near[:half, :])
    rows = near[half:, :]
    halves = jnp.where(core == 0, rows[:, :half], rows[:, half:])
    for p in range(pairs):
        column = blocks_ref[p, size:, :].T
        weight = weight_ref[pairs + pairs * p, 0:1, 0:1] + weight_ref[pairs + pairs * p + 1, 0:1, 0:1]
        whole = split(overlap(column, rows))
        side = split(overlap(column, halves))
        term = dot3(side, split(dot3(part, whole, NT)))
        share_ref[p] = jnp.where(core == p, own_ref[...], 0.0) - weight * term


def far_kernel(far_ref, blocks_ref, share_ref, weight_ref, total_ref):
    pairs, size = share_ref.shape[0], share_ref.shape[1]
    rows = far_ref[size:, :]
    block = split(far_ref[:size, :])
    for p in range(pairs):
        metric = split(overlap(blocks_ref[p, size:, :].T, rows))
        term = dot3(split(dot3(metric, block)), metric, NT)
        total_ref[p] = share_ref[p] - weight_ref[p, 0:1, 0:1] * term


def call(body, outs, spaces, args, scratch=(), flops=0, moved=0, limit=VMEM_LIMIT):
    return pl.pallas_call(
        body,
        out_shape=outs,
        in_specs=[pl.BlockSpec(memory_space=space) for space in spaces],
        out_specs=jax.tree.map(lambda _: pl.BlockSpec(memory_space=pltpu.VMEM), outs),
        scratch_shapes=list(scratch),
        compiler_params=pltpu.CompilerParams(vmem_limit_bytes=limit),
        cost_estimate=pl.CostEstimate(flops=flops, bytes_accessed=moved, transcendentals=0),
    )(*args)


def on_device_four(
    amplitudes,
    exchange_ints,
    pair_list,
    domains,
    link_source,
    link_entry,
    link_count,
    owner_map,
    fock_values,
    occ_energy,
    vir_energy,
    positions,
):
    pairs, size = amplitudes.shape[0], amplitudes.shape[1]
    sub_count = lax.axis_size("sub")
    core = lax.axis_index("rep")
    row = lax.axis_index("pairs")
    axes = ("pairs", "rep")
    across = [(2 * z + c, 2 * (z ^ (3 - c)) + c) for z in range(4) for c in range(2)]
    beside = [(2 * z + c, 2 * (z ^ 1) + c) for z in range(4) for c in range(2)]
    f32 = jnp.float32
    V, S = pltpu.VMEM, pltpu.SMEM

    opened = [
        pltpu.with_memory_space_constraint(value, pltpu.HBM)
        for value in (
            link_source,
            link_count,
            owner_map,
            positions,
            vir_energy,
            domains,
        )
    ]
    wanted, places, levels, names = call(
        functools.partial(open_kernel, sub_count),
        (jax.ShapeDtypeStruct((8, 128), jnp.int32),)
        + tuple(jax.ShapeDtypeStruct(value.shape, value.dtype) for value in opened[3:]),
        (pltpu.HBM,) * len(opened),
        opened,
        scratch=[
            V(link_source.shape, jnp.int32),
            S(link_count.shape, jnp.int32),
            S(owner_map.shape, jnp.int32),
            pltpu.SemaphoreType.DMA((len(opened),)),
        ],
    )
    asked = lax.ppermute(wanted, axes, across)
    lines = -(-positions.shape[1] // 128)
    lines = -(-lines // 16) * 16
    blocks, halves = call(
        gather_kernel,
        (
            jax.ShapeDtypeStruct((pairs, size + COORD_ROWS, size), f32),
            jax.ShapeDtypeStruct((pairs, size // 2 + COORD_ROWS, size), f32),
        ),
        (V, V, V, pltpu.HBM),
        (names, places, levels, pltpu.with_memory_space_constraint(amplitudes, pltpu.HBM)),
        scratch=[V((4 * lines, 128), f32), pltpu.SemaphoreType.DMA((2 * pairs,))],
        flops=10**9,
        moved=10**6,
    )
    near = lax.ppermute(halves, axes, beside)
    chosen = call(
        select_kernel,
        jax.ShapeDtypeStruct((size + COORD_ROWS, size), f32),
        (V, V),
        (asked, blocks),
        moved=10**6,
    )
    far = lax.ppermute(chosen, axes, across)
    own, weight, inverse = call(
        functools.partial(own_kernel, sub_count),
        (
            jax.ShapeDtypeStruct(amplitudes.shape[1:], f32),
            jax.ShapeDtypeStruct((pairs + pairs * pairs, 8, 128), f32),
            jax.ShapeDtypeStruct(amplitudes.shape, f32),
        ),
        (V, V, S, S, S, S, S, S, S),
        (
            blocks,
            exchange_ints,
            link_source,
            link_entry,
            link_count,
            owner_map,
            fock_values,
            pair_list,
            occ_energy,
        ),
        flops=2 * 10**10,
        moved=4 * 10**7,
    )
    share = call(
        near_kernel,
        jax.ShapeDtypeStruct(amplitudes.shape, f32),
        (V, V, V, V),
        (near, blocks, weight, own),
        flops=10**9,
        moved=10**6,
    )
    total = call(
        far_kernel,
        jax.ShapeDtypeStruct(amplitudes.shape, f32),
        (V, V, V, V),
        (far, blocks, share, weight),
        flops=10**9,
        moved=10**6,
    )
    residual = total + lax.ppermute(total, "rep", [(0, 1), (1, 0)])
    return residual, amplitudes - residual * inverse


def solution(mesh):
    stored = ("groups", "pairs", "sub")
    in_specs = (
        P(stored, None, None),
        P(stored, None, None),
        P(stored, None),
        P(stored, None),
        P(stored, None),
        P(stored, None),
        P(stored),
        P("groups"),
        P("groups"),
        P("groups"),
        P("groups"),
        P(None, "groups"),
    )
    out_specs = (P(stored, None, None), P(stored, None, None))

    def run(*args):
        devices = mesh.shape["groups"] * mesh.shape["pairs"] * mesh.shape["sub"]
        known = (
            mesh.shape["pairs"] == 4
            and mesh.shape["rep"] == 2
            and args[0].shape[0] == 2 * devices
            and args[0].shape[1] == 256
        )
        return jax.shard_map(
            on_device_four if known else on_device_any,
            mesh=mesh,
            in_specs=in_specs,
            out_specs=out_specs,
            check_vma=False,
        )(*args)

    return run
```

```python
import functools

import jax
import jax.numpy as jnp
from jax import lax
from jax.experimental import pallas as pl
from jax.experimental.pallas import tpu as pltpu
from jax.sharding import PartitionSpec as P

intersection_rate = 2.0
COORD_ROWS = 8
LOG2_E = 1.4426950408889634
VMEM_LIMIT = 40 * 1024 * 1024


def product(left, right):
    return jnp.dot(left, right, precision=lax.Precision.HIGHEST, preferred_element_type=jnp.float32)


def pick_row(array, index):
    return lax.dynamic_index_in_dim(array, index, 0, keepdims=False)


def model_intersection(left_coords, right_coords):
    squared = jnp.zeros((left_coords.shape[1], right_coords.shape[1]), jnp.float32)
    for component in range(3):
        gap_now = left_coords[component][:, None] - right_coords[component][None, :]
        squared = squared + gap_now * gap_now
    return jnp.exp(-intersection_rate * squared)


def pair_local(block, integrals, pair_coords, pair_energy, pair_shift):
    metric = model_intersection(pair_coords, pair_coords)
    virtual_fock = metric * ((pair_energy[:, None] + pair_energy[None, :]) * 0.5)
    right_side = product(block, metric)
    left_side = product(metric, block)
    return (
        integrals
        + product(virtual_fock, right_side)
        + product(left_side, virtual_fock)
        - pair_shift * product(metric, right_side)
    )


def on_device_any(
    amplitudes,
    exchange_ints,
    pair_list,
    domains,
    link_source,
    link_entry,
    link_count,
    owner_map,
    fock_values,
    occ_energy,
    vir_energy,
    positions,
):
    pair_count = amplitudes.shape[0]
    link_slots = link_source.shape[1]
    row_count = lax.axis_size("pairs")
    sub_count = lax.axis_size("sub")
    core_count = lax.axis_size("rep")
    my_core = lax.axis_index("rep")
    coords = jnp.moveaxis(jnp.take(positions, domains, axis=1), 0, 1)
    energy = jnp.take(vir_energy, domains, axis=0)
    shift = jnp.take(occ_energy, pair_list[:, 0]) + jnp.take(occ_energy, pair_list[:, 1])
    is_live = jnp.arange(link_slots, dtype=jnp.int32)[None, :] < link_count[:, None]
    source_loc = jnp.take(owner_map, link_source)
    source_peer = source_loc // (pair_count * sub_count)
    source_slot = source_loc % pair_count
    peers = jnp.arange(row_count, dtype=jnp.int32)
    matched = is_live[:, :, None] & (source_peer[:, :, None] == peers[None, None, :])
    fock_weight = jnp.take(fock_values, link_entry)
    weight = jnp.sum(jnp.where(matched, fock_weight[:, :, None], 0.0), axis=1)
    wanted = jnp.max(jnp.where(matched, source_slot[:, :, None], 0), axis=(0, 1))
    asked = lax.all_to_all(wanted[:, None], "pairs", split_axis=0, concat_axis=0, tiled=True)[:, 0]
    fetched = lax.all_to_all(
        jnp.take(amplitudes, asked, axis=0), "pairs", split_axis=0, concat_axis=0, tiled=True
    )
    fetched_coords = lax.all_to_all(
        jnp.take(coords, asked, axis=0), "pairs", split_axis=0, concat_axis=0, tiled=True
    )

    def target(pair):
        local = pair_local(
            pick_row(amplitudes, pair),
            pick_row(exchange_ints, pair),
            pick_row(coords, pair),
            pick_row(energy, pair),
            pick_row(shift, pair),
        )

        def advance(peer, total):
            intersection = model_intersection(pick_row(coords, pair), pick_row(fetched_coords, peer))
            term = product(product(intersection, pick_row(fetched, peer)), intersection.T)
            return total - pick_row(pick_row(weight, pair), peer) * term

        return lax.fori_loop(0, row_count, advance, local)

    mine = jnp.arange(pair_count, dtype=jnp.int32) % core_count == my_core
    share = lax.map(
        lambda pair: lax.cond(
            pick_row(mine, pair), target, lambda _: jnp.zeros_like(amplitudes[0]), pair
        ),
        jnp.arange(pair_count, dtype=jnp.int32),
    )
    residual = lax.psum(share, "rep")
    denominator = energy[:, :, None] + energy[:, None, :] - shift[:, None, None]
    return residual, amplitudes - residual / denominator


def split(value):
    high = value.astype(jnp.bfloat16)
    low = (value - high.astype(jnp.float32)).astype(jnp.bfloat16)
    return high, low


NN = (((1,), (0,)), ((), ()))
NT = (((1,), (1,)), ((), ()))
TN = (((0,), (0,)), ((), ()))


def dot(left, right, dims):
    return lax.dot_general(left, right, dims, preferred_element_type=jnp.float32)


def dot3(left, right, dims=NN):
    return (
        dot(left[0], right[0], dims) + dot(left[0], right[1], dims) + dot(left[1], right[0], dims)
    )


def overlap(column, rows):
    squared = None
    for c in range(3):
        gap = column[:, c : c + 1] - rows[c : c + 1, :]
        squared = gap * gap if squared is None else squared + gap * gap
    return jnp.exp2(-intersection_rate * LOG2_E * squared)


def overlap_spread(spread_ref, p, rows):
    halves = []
    for k in range(rows.shape[1] // 128):
        squared = None
        for c in range(3):
            gap = spread_ref[p, c] - rows[c : c + 1, k * 128 : (k + 1) * 128]
            squared = gap * gap if squared is None else squared + gap * gap
        halves.append(jnp.exp2(-intersection_rate * LOG2_E * squared))
    return halves


def sandwich(metric, block):
    metric = split(metric)
    return dot3(split(dot3(metric, split(block))), metric, NT)


def start_all(copies):
    for copy in copies:
        copy.start()
    return copies


def partners():
    row = lax.axis_index("pairs")
    return row ^ (3 - lax.axis_index("rep")), row ^ 1


def open_kernel(
    sub_count,
    source_hbm,
    count_hbm,
    owner_hbm,
    positions_hbm,
    energy_hbm,
    domains_hbm,
    block_hbm,
    first_ref,
    second_ref,
    positions_ref,
    energy_ref,
    domains_ref,
    halves_ref,
    source_ref,
    count_ref,
    owner_ref,
    sems,
):
    half = halves_ref.shape[1]
    start = pl.multiple_of(lax.axis_index("rep") * half, half)
    pairs_of = (
        (source_hbm, source_ref),
        (count_hbm, count_ref),
        (owner_hbm, owner_ref),
        (positions_hbm, positions_ref),
        (energy_hbm, energy_ref),
        (domains_hbm, domains_ref),
        (block_hbm.at[:, pl.ds(start, half), :], halves_ref),
    )
    copies = [
        pltpu.make_async_copy(source, target, sems.at[k])
        for k, (source, target) in enumerate(pairs_of)
    ]
    for copy in copies:
        copy.start()
    peers = partners()
    for copy in copies[:3]:
        copy.wait()
    pairs, links = source_ref.shape
    source = source_ref[...]
    pair = lax.broadcasted_iota(jnp.int32, (pairs, links), 0)
    limit = jnp.zeros_like(source)
    for p in range(pairs):
        limit = jnp.where(pair == p, count_ref[p], limit)
    live = lax.broadcasted_iota(jnp.int32, (pairs, links), 1) < limit
    place = jnp.zeros_like(source)
    for k in range(owner_ref.shape[0]):
        place = jnp.where(source == k, owner_ref[k], place)
    there = lax.div(place, pairs * sub_count)
    slot = lax.rem(place, pairs)
    for peer, wanted_ref in zip(peers, (first_ref, second_ref)):
        wish = jnp.where(live & (there == peer), slot, 0)
        wanted_ref[...] = jnp.broadcast_to(jnp.max(wish, keepdims=True), (8, 128))
    for copy in copies[3:]:
        copy.wait()


def gather_kernel(
    domains_ref, positions_ref, energy_ref, block_ref, coords_ref, halves_ref, table
):
    pairs, size = domains_ref.shape
    half = size // 2
    halves_ref[:, :half, :] = block_ref[...]
    orbitals = positions_ref.shape[1]
    rows = table.shape[0] // 4
    whole, rest = orbitals // 128, orbitals % 128
    for c in range(4):
        table[c * rows + whole : (c + 1) * rows, :] = jnp.zeros((rows - whole, 128), jnp.float32)
    for k in range(whole):
        table[pl.ds(k, 3, stride=rows), :] = positions_ref[:, k * 128 : (k + 1) * 128]
        table[3 * rows + k : 3 * rows + k + 1, :] = energy_ref[k * 128 : (k + 1) * 128].reshape(1, 128)
    if rest:
        table[pl.ds(whole, 3, stride=rows), :rest] = positions_ref[:, whole * 128 :]
        table[3 * rows + whole : 3 * rows + whole + 1, :rest] = energy_ref[whole * 128 :].reshape(
            1, rest
        )
    first = table[...].astype(jnp.bfloat16)
    left = table[...] - first.astype(jnp.float32)
    second = left.astype(jnp.bfloat16)
    third = (left - second.astype(jnp.float32)).astype(jnp.bfloat16)
    for p in range(pairs):
        index = domains_ref[p : p + 1, :]
        high = index // 128
        low = index - high * 128
        chosen = (lax.broadcasted_iota(jnp.int32, (rows, size), 0) == high).astype(
            jnp.float32
        ).astype(jnp.bfloat16)
        lane = lax.broadcasted_iota(jnp.int32, (128, size), 0) == low
        found = []
        for c in range(4):
            span = slice(c * rows, (c + 1) * rows)
            lines = (
                dot(first[span], chosen, TN)
                + dot(second[span], chosen, TN)
                + dot(third[span], chosen, TN)
            )
            found.append(jnp.sum(jnp.where(lane, lines, 0.0), axis=0, keepdims=True))
        found.append(jnp.zeros((COORD_ROWS - 4, size), jnp.float32))
        found = jnp.concatenate(found, axis=0)
        coords_ref[p] = found
        halves_ref[p, half:, :] = found


def select_kernel(asked_ref, block_ref, coords_ref, payload_ref):
    size = block_ref.shape[1]
    half = size // 2
    slot_one = jnp.max(asked_ref[...]) > 0
    centres = jnp.where(slot_one, coords_ref[1], coords_ref[0])
    for k in range(2):
        span = slice(k * half, (k + 1) * half)
        payload_ref[k * size : (k + 1) * size, :] = jnp.where(
            slot_one, block_ref[1, :, span], block_ref[0, :, span]
        )
        payload_ref[2 * size + 3 * k : 2 * size + 3 * k + 3, :] = centres[:3, span]
    payload_ref[2 * size + 6 :, :] = jnp.zeros((COORD_ROWS - 6, half), jnp.float32)


def own_kernel(
    sub_count,
    block_ref,
    integrals_ref,
    coords_ref,
    source_ref,
    entry_ref,
    count_ref,
    owner_ref,
    fock_ref,
    pair_ref,
    occ_ref,
    share_ref,
    weight_ref,
    inverse_ref,
    spread_ref,
):
    pairs = block_ref.shape[0]
    links = source_ref.shape[1]
    core = lax.axis_index("rep")
    row = lax.axis_index("pairs")
    peers = partners()

    def look(m, carry):
        own_slot, weights = carry
        weights = list(weights)
        for p in range(pairs):
            place = owner_ref[source_ref[p, m]]
            peer = lax.div(place, pairs * sub_count)
            slot = lax.rem(place, pairs)
            live = m < count_ref[p]
            value = fock_ref[entry_ref[p, m]]
            own = live & (peer == row)
            own_slot = jnp.where(own, slot, own_slot)
            for k, hit in enumerate((own, live & (peer == peers[0]), live & (peer == peers[1]))):
                weights[3 * p + k] += jnp.where(hit, value, 0.0)
        return own_slot, tuple(weights)

    own_slot, weights = lax.fori_loop(
        0, links, look, (jnp.int32(0), (jnp.float32(0.0),) * (3 * pairs))
    )
    for p in range(pairs):
        for k in range(2):
            weight_ref[k, p] = jnp.full((8, 128), weights[3 * p + 1 + k], jnp.float32)
    shifts = [occ_ref[pair_ref[p, 0]] + occ_ref[pair_ref[p, 1]] for p in range(pairs)]
    columns = [coords_ref[p].T for p in range(pairs)]
    for p in range(pairs):
        for c in range(3):
            spread_ref[p, c] = jnp.broadcast_to(columns[p][:, c : c + 1], spread_ref.shape[2:])
        inverse_ref[p] = 1.0 / (columns[p][:, 3:4] + coords_ref[p, 3:4, :] - shifts[p])

    zero = core == 0
    column = jnp.where(zero, columns[0], columns[1])
    shift = jnp.where(zero, shifts[0], shifts[1])
    own_weight = jnp.where(zero, weights[0], weights[3])
    energy = (column[:, 3:4] + coords_ref[core, 3:4, :]) * 0.5
    block = block_ref[core]
    metric = split(overlap(column, coords_ref[core]))
    plain = dot3(metric, split(dot3(split(block), metric)))
    scaled = dot3(metric, split(dot3(split(block * (energy - shift)), metric)))
    local = integrals_ref[core] + scaled + plain * energy
    own = overlap(column, coords_ref[own_slot])
    local = local - own_weight * sandwich(own, block_ref[own_slot])
    for p in range(pairs):
        share_ref[p] = jnp.where(core == p, local, 0.0)


def near_kernel(near_ref, wanted_ref, spread_ref, weight_ref, share_ref, total_ref):
    pairs, size = share_ref.shape[0], share_ref.shape[1]
    half = size // 2
    near = jnp.where(jnp.max(wanted_ref[...]) > 0, near_ref[1], near_ref[0])
    part = split(near[:half, :])
    for p in range(pairs):
        left, right = overlap_spread(spread_ref, p, near[half:, :])
        metric = split(jnp.concatenate([left, right], axis=1))
        side = split(jnp.where(lax.axis_index("rep") == 0, left, right))
        term = dot3(split(dot3(side, part)), metric, NT)
        total_ref[p] = share_ref[p] - weight_ref[1, p, 0:1, 0:1] * term


def far_kernel(far_ref, spread_ref, weight_ref, share_ref, total_ref):
    pairs, size = share_ref.shape[0], share_ref.shape[1]
    block = split(jnp.concatenate([far_ref[:size, :], far_ref[size : 2 * size, :]], axis=1))
    rows = jnp.concatenate(
        [far_ref[2 * size : 2 * size + 3, :], far_ref[2 * size + 3 : 2 * size + 6, :]], axis=1
    )
    for p in range(pairs):
        metric = split(jnp.concatenate(overlap_spread(spread_ref, p, rows), axis=1))
        term = dot3(split(dot3(metric, block)), metric, NT)
        total_ref[p] = share_ref[p] - weight_ref[0, p, 0:1, 0:1] * term


def call(body, outs, spaces, args, scratch=(), flops=0, moved=0, limit=VMEM_LIMIT):
    return pl.pallas_call(
        body,
        out_shape=outs,
        in_specs=[pl.BlockSpec(memory_space=space) for space in spaces],
        out_specs=jax.tree.map(lambda _: pl.BlockSpec(memory_space=pltpu.VMEM), outs),
        scratch_shapes=list(scratch),
        compiler_params=pltpu.CompilerParams(vmem_limit_bytes=limit),
        cost_estimate=pl.CostEstimate(flops=flops, bytes_accessed=moved, transcendentals=0),
    )(*args)


def on_device_four(
    amplitudes,
    exchange_ints,
    pair_list,
    domains,
    link_source,
    link_entry,
    link_count,
    owner_map,
    fock_values,
    occ_energy,
    vir_energy,
    positions,
):
    pairs, size = amplitudes.shape[0], amplitudes.shape[1]
    sub_count = lax.axis_size("sub")
    core = lax.axis_index("rep")
    row = lax.axis_index("pairs")
    axes = ("pairs", "rep")
    across = [(2 * z + c, 2 * (z ^ (3 - c)) + c) for z in range(4) for c in range(2)]
    beside = [(2 * z + c, 2 * (z ^ 1) + c) for z in range(4) for c in range(2)]
    f32 = jnp.float32
    V, S = pltpu.VMEM, pltpu.SMEM

    opened = [
        pltpu.with_memory_space_constraint(value, pltpu.HBM)
        for value in (
            link_source,
            link_count,
            owner_map,
            positions,
            vir_energy,
            domains,
            amplitudes,
        )
    ]
    block_half = jax.ShapeDtypeStruct((pairs, size // 2, size), f32)
    wanted, wanted_near, places, levels, names, mine = call(
        functools.partial(open_kernel, sub_count),
        (jax.ShapeDtypeStruct((8, 128), jnp.int32),) * 2
        + tuple(jax.ShapeDtypeStruct(value.shape, value.dtype) for value in opened[3:6])
        + (block_half,),
        (pltpu.HBM,) * len(opened),
        opened,
        scratch=[
            V(link_source.shape, jnp.int32),
            S(link_count.shape, jnp.int32),
            S(owner_map.shape, jnp.int32),
            pltpu.SemaphoreType.DMA((len(opened),)),
        ],
    )
    asked = lax.ppermute(wanted, axes, across)
    lines = -(-positions.shape[1] // 128)
    lines = -(-lines // 16) * 16
    coords, halves = call(
        gather_kernel,
        (
            jax.ShapeDtypeStruct((pairs, COORD_ROWS, size), f32),
            jax.ShapeDtypeStruct((pairs, size // 2 + COORD_ROWS, size), f32),
        ),
        (V, V, V, V),
        (names, places, levels, mine),
        scratch=[V((4 * lines, 128), f32)],
        flops=10**9,
        moved=10**6,
    )
    near = lax.ppermute(halves, axes, beside)
    far = call(
        select_kernel,
        jax.ShapeDtypeStruct((2 * size + COORD_ROWS, size // 2), f32),
        (V, V, V),
        (asked, amplitudes, coords),
        moved=10**6,
    )
    far = lax.ppermute(far, axes, across)
    share, weight, inverse, spread = call(
        functools.partial(own_kernel, sub_count),
        (
            jax.ShapeDtypeStruct(amplitudes.shape, f32),
            jax.ShapeDtypeStruct((2, pairs, 8, 128), f32),
            jax.ShapeDtypeStruct(amplitudes.shape, f32),
            jax.ShapeDtypeStruct((pairs, 3, size, 128), f32),
        ),
        (V, V, V, S, S, S, S, S, S, S),
        (
            amplitudes,
            exchange_ints,
            coords,
            link_source,
            link_entry,
            link_count,
            owner_map,
            fock_values,
            pair_list,
            occ_energy,
        ),
        flops=2 * 10**10,
        moved=4 * 10**7,
    )
    whole = jax.ShapeDtypeStruct(amplitudes.shape, f32)
    cost = dict(flops=10**9, moved=10**6)
    share = call(near_kernel, whole, (V,) * 5, (near, wanted_near, spread, weight, share), **cost)
    share = call(far_kernel, whole, (V,) * 4, (far, spread, weight, share), **cost)
    residual = share + lax.ppermute(share, "rep", [(0, 1), (1, 0)])
    return residual, amplitudes - residual * inverse


def solution(mesh):
    stored = ("groups", "pairs", "sub")
    in_specs = (
        P(stored, None, None),
        P(stored, None, None),
        P(stored, None),
        P(stored, None),
        P(stored, None),
        P(stored, None),
        P(stored),
        P("groups"),
        P("groups"),
        P("groups"),
        P("groups"),
        P(None, "groups"),
    )
    out_specs = (P(stored, None, None), P(stored, None, None))

    def run(*args):
        devices = mesh.shape["groups"] * mesh.shape["pairs"] * mesh.shape["sub"]
        known = (
            mesh.shape["pairs"] == 4
            and mesh.shape["rep"] == 2
            and args[0].shape[0] == 2 * devices
            and args[0].shape[1] == 256
        )
        return jax.shard_map(
            on_device_four if known else on_device_any,
            mesh=mesh,
            in_specs=in_specs,
            out_specs=out_specs,
            check_vma=False,
        )(*args)

    return run
```

```python
import functools

import jax
import jax.numpy as jnp
from jax import lax
from jax.experimental import pallas as pl
from jax.experimental.pallas import tpu as pltpu
from jax.sharding import PartitionSpec as P

intersection_rate = 2.0
COORD_ROWS = 8
LOG2_E = 1.4426950408889634
VMEM_LIMIT = 40 * 1024 * 1024


def product(left, right):
    return jnp.dot(left, right, precision=lax.Precision.HIGHEST, preferred_element_type=jnp.float32)


def pick_row(array, index):
    return lax.dynamic_index_in_dim(array, index, 0, keepdims=False)


def model_intersection(left_coords, right_coords):
    squared = jnp.zeros((left_coords.shape[1], right_coords.shape[1]), jnp.float32)
    for component in range(3):
        gap_now = left_coords[component][:, None] - right_coords[component][None, :]
        squared = squared + gap_now * gap_now
    return jnp.exp(-intersection_rate * squared)


def pair_local(block, integrals, pair_coords, pair_energy, pair_shift):
    metric = model_intersection(pair_coords, pair_coords)
    virtual_fock = metric * ((pair_energy[:, None] + pair_energy[None, :]) * 0.5)
    right_side = product(block, metric)
    left_side = product(metric, block)
    return (
        integrals
        + product(virtual_fock, right_side)
        + product(left_side, virtual_fock)
        - pair_shift * product(metric, right_side)
    )


def on_device_any(
    amplitudes,
    exchange_ints,
    pair_list,
    domains,
    link_source,
    link_entry,
    link_count,
    owner_map,
    fock_values,
    occ_energy,
    vir_energy,
    positions,
):
    pair_count = amplitudes.shape[0]
    link_slots = link_source.shape[1]
    row_count = lax.axis_size("pairs")
    sub_count = lax.axis_size("sub")
    core_count = lax.axis_size("rep")
    my_core = lax.axis_index("rep")
    coords = jnp.moveaxis(jnp.take(positions, domains, axis=1), 0, 1)
    energy = jnp.take(vir_energy, domains, axis=0)
    shift = jnp.take(occ_energy, pair_list[:, 0]) + jnp.take(occ_energy, pair_list[:, 1])
    is_live = jnp.arange(link_slots, dtype=jnp.int32)[None, :] < link_count[:, None]
    source_loc = jnp.take(owner_map, link_source)
    source_peer = source_loc // (pair_count * sub_count)
    source_slot = source_loc % pair_count
    peers = jnp.arange(row_count, dtype=jnp.int32)
    matched = is_live[:, :, None] & (source_peer[:, :, None] == peers[None, None, :])
    fock_weight = jnp.take(fock_values, link_entry)
    weight = jnp.sum(jnp.where(matched, fock_weight[:, :, None], 0.0), axis=1)
    wanted = jnp.max(jnp.where(matched, source_slot[:, :, None], 0), axis=(0, 1))
    asked = lax.all_to_all(wanted[:, None], "pairs", split_axis=0, concat_axis=0, tiled=True)[:, 0]
    fetched = lax.all_to_all(
        jnp.take(amplitudes, asked, axis=0), "pairs", split_axis=0, concat_axis=0, tiled=True
    )
    fetched_coords = lax.all_to_all(
        jnp.take(coords, asked, axis=0), "pairs", split_axis=0, concat_axis=0, tiled=True
    )

    def target(pair):
        local = pair_local(
            pick_row(amplitudes, pair),
            pick_row(exchange_ints, pair),
            pick_row(coords, pair),
            pick_row(energy, pair),
            pick_row(shift, pair),
        )

        def advance(peer, total):
            intersection = model_intersection(pick_row(coords, pair), pick_row(fetched_coords, peer))
            term = product(product(intersection, pick_row(fetched, peer)), intersection.T)
            return total - pick_row(pick_row(weight, pair), peer) * term

        return lax.fori_loop(0, row_count, advance, local)

    mine = jnp.arange(pair_count, dtype=jnp.int32) % core_count == my_core
    share = lax.map(
        lambda pair: lax.cond(
            pick_row(mine, pair), target, lambda _: jnp.zeros_like(amplitudes[0]), pair
        ),
        jnp.arange(pair_count, dtype=jnp.int32),
    )
    residual = lax.psum(share, "rep")
    denominator = energy[:, :, None] + energy[:, None, :] - shift[:, None, None]
    return residual, amplitudes - residual / denominator


def split(value):
    high = value.astype(jnp.bfloat16)
    low = (value - high.astype(jnp.float32)).astype(jnp.bfloat16)
    return high, low


NN = (((1,), (0,)), ((), ()))
NT = (((1,), (1,)), ((), ()))
TN = (((0,), (0,)), ((), ()))


def dot(left, right, dims):
    return lax.dot_general(left, right, dims, preferred_element_type=jnp.float32)


def dot3(left, right, dims=NN):
    return (
        dot(left[0], right[0], dims) + dot(left[0], right[1], dims) + dot(left[1], right[0], dims)
    )


def overlap(column, rows):
    squared = None
    for c in range(3):
        gap = column[:, c : c + 1] - rows[c : c + 1, :]
        squared = gap * gap if squared is None else squared + gap * gap
    return jnp.exp2(-intersection_rate * LOG2_E * squared)


def overlap_spread(spread_ref, p, rows):
    halves = []
    for k in range(rows.shape[1] // 128):
        squared = None
        for c in range(3):
            gap = spread_ref[p, c] - rows[c : c + 1, k * 128 : (k + 1) * 128]
            squared = gap * gap if squared is None else squared + gap * gap
        halves.append(jnp.exp2(-intersection_rate * LOG2_E * squared))
    return halves


def sandwich(metric, block):
    metric = split(metric)
    return dot3(split(dot3(metric, split(block))), metric, NT)


def start_all(copies):
    for copy in copies:
        copy.start()
    return copies


def partners():
    row = lax.axis_index("pairs")
    return row ^ (3 - lax.axis_index("rep")), row ^ 1


def open_kernel(
    sub_count,
    source_hbm,
    count_hbm,
    owner_hbm,
    domains_hbm,
    block_hbm,
    message_ref,
    wanted_near_ref,
    halves_ref,
    source_ref,
    count_ref,
    owner_ref,
    domains_ref,
    sems,
):
    pairs, links = source_ref.shape
    size = domains_ref.shape[1]
    half = size // 2
    start = pl.multiple_of(lax.axis_index("rep") * half, half)
    moves = [
        (source_hbm, source_ref),
        (count_hbm, count_ref),
        (owner_hbm, owner_ref),
        (domains_hbm, domains_ref),
    ]
    moves += [
        (block_hbm.at[p, pl.ds(start, half), :], halves_ref.at[p, pl.ds(0, half), :])
        for p in range(pairs)
    ]
    copies = [
        pltpu.make_async_copy(source, target, sems.at[k])
        for k, (source, target) in enumerate(moves)
    ]
    for copy in copies:
        copy.start()
    for copy in copies[:4]:
        copy.wait()
    source = source_ref[...]
    pair = lax.broadcasted_iota(jnp.int32, (pairs, links), 0)
    limit = jnp.zeros_like(source)
    for p in range(pairs):
        limit = jnp.where(pair == p, count_ref[p], limit)
    live = lax.broadcasted_iota(jnp.int32, (pairs, links), 1) < limit
    place = jnp.zeros_like(source)
    for k in range(owner_ref.shape[0]):
        place = jnp.where(source == k, owner_ref[k], place)
    there = lax.div(place, pairs * sub_count)
    slot = lax.rem(place, pairs)
    for peer, wanted_ref in zip(partners(), (message_ref, wanted_near_ref)):
        wish = jnp.where(live & (there == peer), slot, 0)
        wanted_ref[...] = jnp.broadcast_to(jnp.max(wish, keepdims=True), (8, 128))
    for p in range(pairs):
        for k in range(2):
            row = 4 + 2 * p + k
            message_ref[row : row + 1, :] = domains_ref[p : p + 1, k * 128 : (k + 1) * 128]
        halves_ref[p, half:, :] = jnp.broadcast_to(
            domains_ref[p : p + 1, :].astype(jnp.float32), (COORD_ROWS, size)
        )
    for copy in copies[4:]:
        copy.wait()


def look_up(index, table_ref, components, held):
    count = index.shape[1]
    rows = table_ref.shape[0] // held
    table = table_ref[: components * rows, :]
    first = table.astype(jnp.bfloat16)
    left = table - first.astype(jnp.float32)
    second = left.astype(jnp.bfloat16)
    third = (left - second.astype(jnp.float32)).astype(jnp.bfloat16)
    high = index // 128
    low = index - high * 128
    chosen = (lax.broadcasted_iota(jnp.int32, (rows, count), 0) == high).astype(
        jnp.float32
    ).astype(jnp.bfloat16)
    lane = lax.broadcasted_iota(jnp.int32, (128, count), 0) == low
    found = []
    for c in range(components):
        span = slice(c * rows, (c + 1) * rows)
        lines = (
            dot(first[span], chosen, TN)
            + dot(second[span], chosen, TN)
            + dot(third[span], chosen, TN)
        )
        found.append(jnp.sum(jnp.where(lane, lines, 0.0), axis=0, keepdims=True))
    return found


def domain_of(message_ref, p):
    row = 4 + 2 * p
    return jnp.concatenate([message_ref[row : row + 1, :], message_ref[row + 1 : row + 2, :]], axis=1)


def centres_kernel(
    positions_hbm,
    energy_hbm,
    message_ref,
    asked_ref,
    coords_ref,
    far_ref,
    table,
    positions_ref,
    energy_ref,
    sems,
):
    copies = [
        pltpu.make_async_copy(positions_hbm, positions_ref, sems.at[0]),
        pltpu.make_async_copy(energy_hbm, energy_ref, sems.at[1]),
    ]
    for copy in copies:
        copy.start()
    pairs, size = coords_ref.shape[0], coords_ref.shape[2]
    orbitals = positions_ref.shape[1]
    rows = table.shape[0] // 4
    whole, rest = orbitals // 128, orbitals % 128
    for c in range(4):
        table[c * rows + whole : (c + 1) * rows, :] = jnp.zeros((rows - whole, 128), jnp.float32)
    for copy in copies:
        copy.wait()
    for k in range(whole):
        table[pl.ds(k, 3, stride=rows), :] = positions_ref[:, k * 128 : (k + 1) * 128]
        table[3 * rows + k : 3 * rows + k + 1, :] = energy_ref[k * 128 : (k + 1) * 128].reshape(1, 128)
    if rest:
        table[pl.ds(whole, 3, stride=rows), :rest] = positions_ref[:, whole * 128 :]
        table[3 * rows + whole : 3 * rows + whole + 1, :rest] = energy_ref[whole * 128 :].reshape(
            1, rest
        )
    slot_one = jnp.max(message_ref[0:1, :]) > 0
    index = [domain_of(message_ref, p) for p in range(pairs)]
    index.append(jnp.where(slot_one, domain_of(asked_ref, 1), domain_of(asked_ref, 0)))
    found = look_up(jnp.concatenate(index, axis=1), table, 4, 4)
    found.append(jnp.zeros((COORD_ROWS - 4, (pairs + 1) * size), jnp.float32))
    found = jnp.concatenate(found, axis=0)
    for p in range(pairs):
        coords_ref[p] = found[:, p * size : (p + 1) * size]
    far_ref[...] = found[:, pairs * size :]


def select_kernel(asked_ref, block_ref, payload_ref):
    slot_one = jnp.max(asked_ref[0:1, :]) > 0
    payload_ref[...] = jnp.where(slot_one, block_ref[1], block_ref[0])


def own_kernel(
    sub_count,
    block_ref,
    integrals_ref,
    coords_ref,
    far_rows_ref,
    source_ref,
    entry_ref,
    count_ref,
    owner_ref,
    fock_ref,
    pair_ref,
    occ_ref,
    share_ref,
    weight_ref,
    inverse_ref,
    spread_ref,
    high_ref,
    low_ref,
):
    pairs = block_ref.shape[0]
    links = source_ref.shape[1]
    core = lax.axis_index("rep")
    row = lax.axis_index("pairs")
    peers = partners()

    def look(m, carry):
        own_slot, weights = carry
        weights = list(weights)
        for p in range(pairs):
            place = owner_ref[source_ref[p, m]]
            peer = lax.div(place, pairs * sub_count)
            slot = lax.rem(place, pairs)
            live = m < count_ref[p]
            value = fock_ref[entry_ref[p, m]]
            own = live & (peer == row)
            own_slot = jnp.where(own, slot, own_slot)
            for k, hit in enumerate((own, live & (peer == peers[0]), live & (peer == peers[1]))):
                weights[3 * p + k] += jnp.where(hit, value, 0.0)
        return own_slot, tuple(weights)

    own_slot, weights = lax.fori_loop(
        0, links, look, (jnp.int32(0), (jnp.float32(0.0),) * (3 * pairs))
    )
    for p in range(pairs):
        for k in range(2):
            weight_ref[k, p] = jnp.full((8, 128), weights[3 * p + 1 + k], jnp.float32)
    shifts = [occ_ref[pair_ref[p, 0]] + occ_ref[pair_ref[p, 1]] for p in range(pairs)]
    columns = [coords_ref[p].T for p in range(pairs)]
    for p in range(pairs):
        for c in range(3):
            spread_ref[p, c] = jnp.broadcast_to(columns[p][:, c : c + 1], spread_ref.shape[2:])
        inverse_ref[p] = 1.0 / (columns[p][:, 3:4] + coords_ref[p, 3:4, :] - shifts[p])

    for p in range(pairs):
        high_ref[p], low_ref[p] = split(overlap(columns[p], far_rows_ref[...]))

    zero = core == 0
    column = jnp.where(zero, columns[0], columns[1])
    shift = jnp.where(zero, shifts[0], shifts[1])
    own_weight = jnp.where(zero, weights[0], weights[3])
    energy = (column[:, 3:4] + coords_ref[core, 3:4, :]) * 0.5
    block = block_ref[core]
    metric = split(overlap(column, coords_ref[core]))
    plain = dot3(metric, split(dot3(split(block), metric)))
    scaled = dot3(metric, split(dot3(split(block * (energy - shift)), metric)))
    local = integrals_ref[core] + scaled + plain * energy
    own = overlap(column, coords_ref[own_slot])
    local = local - own_weight * sandwich(own, block_ref[own_slot])
    for p in range(pairs):
        share_ref[p] = jnp.where(core == p, local, 0.0)


def near_kernel(near_ref, wanted_ref, table_ref, spread_ref, weight_ref, share_ref, total_ref):
    pairs, size = share_ref.shape[0], share_ref.shape[1]
    half = size // 2
    near = jnp.where(jnp.max(wanted_ref[...]) > 0, near_ref[1], near_ref[0])
    part = split(near[:half, :])
    rows = jnp.concatenate(look_up(near[half : half + 1, :].astype(jnp.int32), table_ref, 3, 4), axis=0)
    for p in range(pairs):
        left, right = overlap_spread(spread_ref, p, rows)
        metric = split(jnp.concatenate([left, right], axis=1))
        side = split(jnp.where(lax.axis_index("rep") == 0, left, right))
        term = dot3(split(dot3(side, part)), metric, NT)
        total_ref[p] = share_ref[p] - weight_ref[1, p, 0:1, 0:1] * term


def far_kernel(far_ref, high_ref, low_ref, weight_ref, share_ref, total_ref):
    block = split(far_ref[...])
    for p in range(share_ref.shape[0]):
        metric = high_ref[p], low_ref[p]
        term = dot3(split(dot3(metric, block)), metric, NT)
        total_ref[p] = share_ref[p] - weight_ref[0, p, 0:1, 0:1] * term


def final_kernel(
    share_ref, other_ref, block_ref, inverse_ref, residual_hbm, updated_hbm, residual_ref, updated_ref, sems
):
    copies = []
    for p in range(share_ref.shape[0]):
        residual = share_ref[p] + other_ref[p]
        residual_ref[p] = residual
        updated_ref[p] = block_ref[p] - residual * inverse_ref[p]
        for k, (source, target) in enumerate(
            ((residual_ref, residual_hbm), (updated_ref, updated_hbm))
        ):
            copies.append(pltpu.make_async_copy(source.at[p], target.at[p], sems.at[2 * p + k]))
            copies[-1].start()
    for copy in copies:
        copy.wait()


def call(
    body, outs, spaces, args, scratch=(), flops=0, moved=0, limit=VMEM_LIMIT, result=pltpu.VMEM
):
    return pl.pallas_call(
        body,
        out_shape=outs,
        in_specs=[pl.BlockSpec(memory_space=space) for space in spaces],
        out_specs=jax.tree.map(lambda _: pl.BlockSpec(memory_space=result), outs),
        scratch_shapes=list(scratch),
        compiler_params=pltpu.CompilerParams(vmem_limit_bytes=limit),
        cost_estimate=pl.CostEstimate(flops=flops, bytes_accessed=moved, transcendentals=0),
    )(*args)


def on_device_four(
    amplitudes,
    exchange_ints,
    pair_list,
    domains,
    link_source,
    link_entry,
    link_count,
    owner_map,
    fock_values,
    occ_energy,
    vir_energy,
    positions,
):
    pairs, size = amplitudes.shape[0], amplitudes.shape[1]
    sub_count = lax.axis_size("sub")
    core = lax.axis_index("rep")
    row = lax.axis_index("pairs")
    axes = ("pairs", "rep")
    across = [(2 * z + c, 2 * (z ^ (3 - c)) + c) for z in range(4) for c in range(2)]
    beside = [(2 * z + c, 2 * (z ^ 1) + c) for z in range(4) for c in range(2)]
    f32 = jnp.float32
    V, S = pltpu.VMEM, pltpu.SMEM

    opened = [
        pltpu.with_memory_space_constraint(value, pltpu.HBM)
        for value in (link_source, link_count, owner_map, domains, amplitudes)
    ]
    word = jax.ShapeDtypeStruct((8, 128), jnp.int32)
    message, wanted_near, halves = call(
        functools.partial(open_kernel, sub_count),
        (word, word, jax.ShapeDtypeStruct((pairs, size // 2 + COORD_ROWS, size), f32)),
        (pltpu.HBM,) * len(opened),
        opened,
        scratch=[
            V(link_source.shape, jnp.int32),
            S(link_count.shape, jnp.int32),
            S(owner_map.shape, jnp.int32),
            V(domains.shape, jnp.int32),
            pltpu.SemaphoreType.DMA((4 + pairs,)),
        ],
    )
    asked = lax.ppermute(message, axes, across)
    near = lax.ppermute(halves, axes, beside)
    block = jax.ShapeDtypeStruct((size, size), f32)
    far = call(select_kernel, block, (V, V), (asked, amplitudes), moved=10**6)
    far = lax.ppermute(far, axes, across)

    lines = -(-positions.shape[1] // 128)
    lines = -(-lines // 16) * 16
    coords, far_rows, table = call(
        centres_kernel,
        (
            jax.ShapeDtypeStruct((pairs, COORD_ROWS, size), f32),
            jax.ShapeDtypeStruct((COORD_ROWS, size), f32),
            jax.ShapeDtypeStruct((4 * lines, 128), f32),
        ),
        (pltpu.HBM, pltpu.HBM, V, V),
        (
            pltpu.with_memory_space_constraint(positions, pltpu.HBM),
            pltpu.with_memory_space_constraint(vir_energy, pltpu.HBM),
            message,
            asked,
        ),
        scratch=[
            V(positions.shape, f32),
            V(vir_energy.shape, f32),
            pltpu.SemaphoreType.DMA((2,)),
        ],
        flops=10**9,
        moved=10**6,
    )
    share, weight, inverse, spread, high, low = call(
        functools.partial(own_kernel, sub_count),
        (
            jax.ShapeDtypeStruct(amplitudes.shape, f32),
            jax.ShapeDtypeStruct((2, pairs, 8, 128), f32),
            jax.ShapeDtypeStruct(amplitudes.shape, f32),
            jax.ShapeDtypeStruct((pairs, 3, size, 128), f32),
            jax.ShapeDtypeStruct(amplitudes.shape, jnp.bfloat16),
            jax.ShapeDtypeStruct(amplitudes.shape, jnp.bfloat16),
        ),
        (V, V, V, V, S, S, S, S, S, S, S),
        (
            amplitudes,
            exchange_ints,
            coords,
            far_rows,
            link_source,
            link_entry,
            link_count,
            owner_map,
            fock_values,
            pair_list,
            occ_energy,
        ),
        flops=2 * 10**10,
        moved=4 * 10**7,
    )
    whole = jax.ShapeDtypeStruct(amplitudes.shape, f32)
    cost = dict(flops=10**9, moved=10**6)
    share = call(
        near_kernel, whole, (V,) * 6, (near, wanted_near, table, spread, weight, share), **cost
    )
    share = call(far_kernel, whole, (V,) * 5, (far, high, low, weight, share), **cost)
    other = lax.ppermute(share, "rep", [(0, 1), (1, 0)])
    return call(
        final_kernel,
        (whole, whole),
        (V,) * 4,
        (share, other, amplitudes, inverse),
        scratch=[V(amplitudes.shape, f32), V(amplitudes.shape, f32), pltpu.SemaphoreType.DMA((2 * pairs,))],
        result=pltpu.HBM,
        **cost,
    )


def solution(mesh):
    stored = ("groups", "pairs", "sub")
    in_specs = (
        P(stored, None, None),
        P(stored, None, None),
        P(stored, None),
        P(stored, None),
        P(stored, None),
        P(stored, None),
        P(stored),
        P("groups"),
        P("groups"),
        P("groups"),
        P("groups"),
        P(None, "groups"),
    )
    out_specs = (P(stored, None, None), P(stored, None, None))

    def run(*args):
        devices = mesh.shape["groups"] * mesh.shape["pairs"] * mesh.shape["sub"]
        known = (
            mesh.shape["pairs"] == 4
            and mesh.shape["rep"] == 2
            and args[0].shape[0] == 2 * devices
            and args[0].shape[1] == 256
        )
        return jax.shard_map(
            on_device_four if known else on_device_any,
            mesh=mesh,
            in_specs=in_specs,
            out_specs=out_specs,
            check_vma=False,
        )(*args)

    return run
```

```python
import functools

import jax
import jax.numpy as jnp
from jax import lax
from jax.experimental import pallas as pl
from jax.experimental.pallas import tpu as pltpu
from jax.sharding import PartitionSpec as P

intersection_rate = 2.0
COORD_ROWS = 8
LOG2_E = 1.4426950408889634
VMEM_LIMIT = 40 * 1024 * 1024


def product(left, right):
    return jnp.dot(left, right, precision=lax.Precision.HIGHEST, preferred_element_type=jnp.float32)


def pick_row(array, index):
    return lax.dynamic_index_in_dim(array, index, 0, keepdims=False)


def model_intersection(left_coords, right_coords):
    squared = jnp.zeros((left_coords.shape[1], right_coords.shape[1]), jnp.float32)
    for component in range(3):
        gap_now = left_coords[component][:, None] - right_coords[component][None, :]
        squared = squared + gap_now * gap_now
    return jnp.exp(-intersection_rate * squared)


def pair_local(block, integrals, pair_coords, pair_energy, pair_shift):
    metric = model_intersection(pair_coords, pair_coords)
    virtual_fock = metric * ((pair_energy[:, None] + pair_energy[None, :]) * 0.5)
    right_side = product(block, metric)
    left_side = product(metric, block)
    return (
        integrals
        + product(virtual_fock, right_side)
        + product(left_side, virtual_fock)
        - pair_shift * product(metric, right_side)
    )


def on_device_any(
    amplitudes,
    exchange_ints,
    pair_list,
    domains,
    link_source,
    link_entry,
    link_count,
    owner_map,
    fock_values,
    occ_energy,
    vir_energy,
    positions,
):
    pair_count = amplitudes.shape[0]
    link_slots = link_source.shape[1]
    row_count = lax.axis_size("pairs")
    sub_count = lax.axis_size("sub")
    core_count = lax.axis_size("rep")
    my_core = lax.axis_index("rep")
    coords = jnp.moveaxis(jnp.take(positions, domains, axis=1), 0, 1)
    energy = jnp.take(vir_energy, domains, axis=0)
    shift = jnp.take(occ_energy, pair_list[:, 0]) + jnp.take(occ_energy, pair_list[:, 1])
    is_live = jnp.arange(link_slots, dtype=jnp.int32)[None, :] < link_count[:, None]
    source_loc = jnp.take(owner_map, link_source)
    source_peer = source_loc // (pair_count * sub_count)
    source_slot = source_loc % pair_count
    peers = jnp.arange(row_count, dtype=jnp.int32)
    matched = is_live[:, :, None] & (source_peer[:, :, None] == peers[None, None, :])
    fock_weight = jnp.take(fock_values, link_entry)
    weight = jnp.sum(jnp.where(matched, fock_weight[:, :, None], 0.0), axis=1)
    wanted = jnp.max(jnp.where(matched, source_slot[:, :, None], 0), axis=(0, 1))
    asked = lax.all_to_all(wanted[:, None], "pairs", split_axis=0, concat_axis=0, tiled=True)[:, 0]
    fetched = lax.all_to_all(
        jnp.take(amplitudes, asked, axis=0), "pairs", split_axis=0, concat_axis=0, tiled=True
    )
    fetched_coords = lax.all_to_all(
        jnp.take(coords, asked, axis=0), "pairs", split_axis=0, concat_axis=0, tiled=True
    )

    def target(pair):
        local = pair_local(
            pick_row(amplitudes, pair),
            pick_row(exchange_ints, pair),
            pick_row(coords, pair),
            pick_row(energy, pair),
            pick_row(shift, pair),
        )

        def advance(peer, total):
            intersection = model_intersection(pick_row(coords, pair), pick_row(fetched_coords, peer))
            term = product(product(intersection, pick_row(fetched, peer)), intersection.T)
            return total - pick_row(pick_row(weight, pair), peer) * term

        return lax.fori_loop(0, row_count, advance, local)

    mine = jnp.arange(pair_count, dtype=jnp.int32) % core_count == my_core
    share = lax.map(
        lambda pair: lax.cond(
            pick_row(mine, pair), target, lambda _: jnp.zeros_like(amplitudes[0]), pair
        ),
        jnp.arange(pair_count, dtype=jnp.int32),
    )
    residual = lax.psum(share, "rep")
    denominator = energy[:, :, None] + energy[:, None, :] - shift[:, None, None]
    return residual, amplitudes - residual / denominator


def split(value):
    high = value.astype(jnp.bfloat16)
    low = (value - high.astype(jnp.float32)).astype(jnp.bfloat16)
    return high, low


NN = (((1,), (0,)), ((), ()))
NT = (((1,), (1,)), ((), ()))
TN = (((0,), (0,)), ((), ()))


def dot(left, right, dims):
    return lax.dot_general(left, right, dims, preferred_element_type=jnp.float32)


def dot3(left, right, dims=NN):
    return (
        dot(left[0], right[0], dims) + dot(left[0], right[1], dims) + dot(left[1], right[0], dims)
    )


def overlap(column, rows):
    squared = None
    for c in range(3):
        gap = column[:, c : c + 1] - rows[c : c + 1, :]
        squared = gap * gap if squared is None else squared + gap * gap
    return jnp.exp2(-intersection_rate * LOG2_E * squared)


def overlap_spread(spread_ref, p, rows):
    halves = []
    for k in range(rows.shape[1] // 128):
        squared = None
        for c in range(3):
            gap = spread_ref[p, c] - rows[c : c + 1, k * 128 : (k + 1) * 128]
            squared = gap * gap if squared is None else squared + gap * gap
        halves.append(jnp.exp2(-intersection_rate * LOG2_E * squared))
    return halves


def sandwich(metric, block):
    metric = split(metric)
    return dot3(split(dot3(metric, split(block))), metric, NT)


def start_all(copies):
    for copy in copies:
        copy.start()
    return copies


def partners():
    row = lax.axis_index("pairs")
    return row ^ (3 - lax.axis_index("rep")), row ^ 1


def open_kernel(
    sub_count,
    source_hbm,
    count_hbm,
    owner_hbm,
    domains_hbm,
    block_hbm,
    message_ref,
    wanted_near_ref,
    halves_ref,
    source_ref,
    count_ref,
    owner_ref,
    domains_ref,
    sems,
):
    pairs, links = source_ref.shape
    size = domains_ref.shape[1]
    half = size // 2
    start = pl.multiple_of(lax.axis_index("rep") * half, half)
    moves = [
        (source_hbm, source_ref),
        (count_hbm, count_ref),
        (owner_hbm, owner_ref),
        (domains_hbm, domains_ref),
    ]
    moves += [
        (block_hbm.at[p, pl.ds(start, half), :], halves_ref.at[p, pl.ds(0, half), :])
        for p in range(pairs)
    ]
    copies = [
        pltpu.make_async_copy(source, target, sems.at[k])
        for k, (source, target) in enumerate(moves)
    ]
    for copy in copies:
        copy.start()
    for copy in copies[:4]:
        copy.wait()
    source = source_ref[...]
    pair = lax.broadcasted_iota(jnp.int32, (pairs, links), 0)
    limit = jnp.zeros_like(source)
    for p in range(pairs):
        limit = jnp.where(pair == p, count_ref[p], limit)
    live = lax.broadcasted_iota(jnp.int32, (pairs, links), 1) < limit
    place = jnp.zeros_like(source)
    for k in range(owner_ref.shape[0]):
        place = jnp.where(source == k, owner_ref[k], place)
    there = lax.div(place, pairs * sub_count)
    slot = lax.rem(place, pairs)
    for peer, wanted_ref in zip(partners(), (message_ref, wanted_near_ref)):
        wish = jnp.where(live & (there == peer), slot, 0)
        wanted_ref[...] = jnp.broadcast_to(jnp.max(wish, keepdims=True), (8, 128))
    for p in range(pairs):
        for k in range(2):
            row = 4 + 2 * p + k
            message_ref[row : row + 1, :] = domains_ref[p : p + 1, k * 128 : (k + 1) * 128]
        halves_ref[p, half:, :] = jnp.broadcast_to(
            domains_ref[p : p + 1, :].astype(jnp.float32), (COORD_ROWS, size)
        )
    for copy in copies[4:]:
        copy.wait()


def look_up(index, table_ref, components, held):
    count = index.shape[1]
    rows = table_ref.shape[0] // held
    table = table_ref[: components * rows, :]
    first = table.astype(jnp.bfloat16)
    left = table - first.astype(jnp.float32)
    second = left.astype(jnp.bfloat16)
    third = (left - second.astype(jnp.float32)).astype(jnp.bfloat16)
    high = index // 128
    low = index - high * 128
    chosen = (lax.broadcasted_iota(jnp.int32, (rows, count), 0) == high).astype(
        jnp.float32
    ).astype(jnp.bfloat16)
    lane = lax.broadcasted_iota(jnp.int32, (128, count), 0) == low
    found = []
    for c in range(components):
        span = slice(c * rows, (c + 1) * rows)
        lines = (
            dot(first[span], chosen, TN)
            + dot(second[span], chosen, TN)
            + dot(third[span], chosen, TN)
        )
        found.append(jnp.sum(jnp.where(lane, lines, 0.0), axis=0, keepdims=True))
    return found


def domain_of(message_ref, p):
    row = 4 + 2 * p
    return jnp.concatenate([message_ref[row : row + 1, :], message_ref[row + 1 : row + 2, :]], axis=1)


def centres_kernel(
    positions_hbm,
    energy_hbm,
    message_ref,
    asked_ref,
    coords_ref,
    far_ref,
    table,
    positions_ref,
    energy_ref,
    sems,
):
    copies = [
        pltpu.make_async_copy(positions_hbm, positions_ref, sems.at[0]),
        pltpu.make_async_copy(energy_hbm, energy_ref, sems.at[1]),
    ]
    for copy in copies:
        copy.start()
    pairs, size = coords_ref.shape[0], coords_ref.shape[2]
    orbitals = positions_ref.shape[1]
    rows = table.shape[0] // 4
    whole, rest = orbitals // 128, orbitals % 128
    for c in range(4):
        table[c * rows + whole : (c + 1) * rows, :] = jnp.zeros((rows - whole, 128), jnp.float32)
    for copy in copies:
        copy.wait()
    for k in range(whole):
        table[pl.ds(k, 3, stride=rows), :] = positions_ref[:, k * 128 : (k + 1) * 128]
        table[3 * rows + k : 3 * rows + k + 1, :] = energy_ref[k * 128 : (k + 1) * 128].reshape(1, 128)
    if rest:
        table[pl.ds(whole, 3, stride=rows), :rest] = positions_ref[:, whole * 128 :]
        table[3 * rows + whole : 3 * rows + whole + 1, :rest] = energy_ref[whole * 128 :].reshape(
            1, rest
        )
    slot_one = jnp.max(message_ref[0:1, :]) > 0
    index = [domain_of(message_ref, p) for p in range(pairs)]
    index.append(jnp.where(slot_one, domain_of(asked_ref, 1), domain_of(asked_ref, 0)))
    found = look_up(jnp.concatenate(index, axis=1), table, 4, 4)
    found.append(jnp.zeros((COORD_ROWS - 4, (pairs + 1) * size), jnp.float32))
    found = jnp.concatenate(found, axis=0)
    for p in range(pairs):
        coords_ref[p] = found[:, p * size : (p + 1) * size]
    far_ref[...] = found[:, pairs * size :]


def select_kernel(asked_ref, block_ref, payload_ref):
    slot_one = jnp.max(asked_ref[0:1, :]) > 0
    payload_ref[...] = jnp.where(slot_one, block_ref[1], block_ref[0])


def own_kernel(
    sub_count,
    block_ref,
    integrals_ref,
    coords_ref,
    far_rows_ref,
    source_hbm,
    entry_hbm,
    count_hbm,
    owner_hbm,
    fock_hbm,
    pair_hbm,
    occ_hbm,
    share_ref,
    weight_ref,
    inverse_ref,
    spread_ref,
    high_ref,
    low_ref,
    source_ref,
    entry_ref,
    count_ref,
    owner_ref,
    fock_ref,
    pair_ref,
    occ_ref,
    sems,
):
    moves = (
        (source_hbm, source_ref),
        (entry_hbm, entry_ref),
        (count_hbm, count_ref),
        (owner_hbm, owner_ref),
        (fock_hbm, fock_ref),
        (pair_hbm, pair_ref),
        (occ_hbm, occ_ref),
    )
    copies = [
        pltpu.make_async_copy(source, target, sems.at[k])
        for k, (source, target) in enumerate(moves)
    ]
    for copy in copies:
        copy.start()
    pairs = block_ref.shape[0]
    links = source_ref.shape[1]
    core = lax.axis_index("rep")
    row = lax.axis_index("pairs")
    peers = partners()

    columns = [coords_ref[p].T for p in range(pairs)]
    for p in range(pairs):
        for c in range(3):
            spread_ref[p, c] = jnp.broadcast_to(columns[p][:, c : c + 1], spread_ref.shape[2:])
        high_ref[p], low_ref[p] = split(overlap(columns[p], far_rows_ref[...]))
    zero = core == 0
    column = jnp.where(zero, columns[0], columns[1])
    energy = (column[:, 3:4] + coords_ref[core, 3:4, :]) * 0.5
    block = block_ref[core]
    metric = split(overlap(column, coords_ref[core]))
    plain = dot3(metric, split(dot3(split(block), metric)))
    scaled = dot3(metric, split(dot3(split(block * energy), metric)))

    for copy in copies:
        copy.wait()

    def look(m, carry):
        own_slot, weights = carry
        weights = list(weights)
        for p in range(pairs):
            place = owner_ref[source_ref[p, m]]
            peer = lax.div(place, pairs * sub_count)
            slot = lax.rem(place, pairs)
            live = m < count_ref[p]
            value = fock_ref[entry_ref[p, m]]
            own = live & (peer == row)
            own_slot = jnp.where(own, slot, own_slot)
            for k, hit in enumerate((own, live & (peer == peers[0]), live & (peer == peers[1]))):
                weights[3 * p + k] += jnp.where(hit, value, 0.0)
        return own_slot, tuple(weights)

    shifts = [occ_ref[pair_ref[p, 0]] + occ_ref[pair_ref[p, 1]] for p in range(pairs)]
    shift = jnp.where(zero, shifts[0], shifts[1])
    share_ref[core] = integrals_ref[core] + scaled + plain * (energy - shift)
    own_slot, weights = lax.fori_loop(
        0, links, look, (jnp.int32(0), (jnp.float32(0.0),) * (3 * pairs))
    )
    for p in range(pairs):
        for k in range(2):
            weight_ref[k, p] = jnp.full((8, 128), weights[3 * p + 1 + k], jnp.float32)
        inverse_ref[p] = 1.0 / (columns[p][:, 3:4] + coords_ref[p, 3:4, :] - shifts[p])
    own_weight = jnp.where(zero, weights[0], weights[3])
    own = overlap(column, coords_ref[own_slot])
    share_ref[core] = share_ref[core] - own_weight * sandwich(own, block_ref[own_slot])
    share_ref[1 - core] = jnp.zeros_like(block)


def near_kernel(near_ref, wanted_ref, table_ref, spread_ref, weight_ref, share_ref, total_ref):
    pairs, size = share_ref.shape[0], share_ref.shape[1]
    half = size // 2
    near = jnp.where(jnp.max(wanted_ref[...]) > 0, near_ref[1], near_ref[0])
    part = split(near[:half, :])
    rows = jnp.concatenate(look_up(near[half : half + 1, :].astype(jnp.int32), table_ref, 3, 4), axis=0)
    for p in range(pairs):
        left, right = overlap_spread(spread_ref, p, rows)
        metric = split(jnp.concatenate([left, right], axis=1))
        side = split(jnp.where(lax.axis_index("rep") == 0, left, right))
        term = dot3(split(dot3(side, part)), metric, NT)
        total_ref[p] = share_ref[p] - weight_ref[1, p, 0:1, 0:1] * term


def far_kernel(far_ref, high_ref, low_ref, weight_ref, share_ref, total_ref):
    block = split(far_ref[...])
    for p in range(share_ref.shape[0]):
        metric = high_ref[p], low_ref[p]
        term = dot3(split(dot3(metric, block)), metric, NT)
        total_ref[p] = share_ref[p] - weight_ref[0, p, 0:1, 0:1] * term


def final_kernel(
    share_ref, other_ref, block_ref, inverse_ref, residual_hbm, updated_hbm, residual_ref, updated_ref, sems
):
    copies = []
    for p in range(share_ref.shape[0]):
        residual = share_ref[p] + other_ref[p]
        residual_ref[p] = residual
        updated_ref[p] = block_ref[p] - residual * inverse_ref[p]
        for k, (source, target) in enumerate(
            ((residual_ref, residual_hbm), (updated_ref, updated_hbm))
        ):
            copies.append(pltpu.make_async_copy(source.at[p], target.at[p], sems.at[2 * p + k]))
            copies[-1].start()
    for copy in copies:
        copy.wait()


def call(
    body, outs, spaces, args, scratch=(), flops=0, moved=0, limit=VMEM_LIMIT, result=pltpu.VMEM
):
    return pl.pallas_call(
        body,
        out_shape=outs,
        in_specs=[pl.BlockSpec(memory_space=space) for space in spaces],
        out_specs=jax.tree.map(lambda _: pl.BlockSpec(memory_space=result), outs),
        scratch_shapes=list(scratch),
        compiler_params=pltpu.CompilerParams(vmem_limit_bytes=limit),
        cost_estimate=pl.CostEstimate(flops=flops, bytes_accessed=moved, transcendentals=0),
    )(*args)


def on_device_four(
    amplitudes,
    exchange_ints,
    pair_list,
    domains,
    link_source,
    link_entry,
    link_count,
    owner_map,
    fock_values,
    occ_energy,
    vir_energy,
    positions,
):
    pairs, size = amplitudes.shape[0], amplitudes.shape[1]
    sub_count = lax.axis_size("sub")
    core = lax.axis_index("rep")
    row = lax.axis_index("pairs")
    axes = ("pairs", "rep")
    across = [(2 * z + c, 2 * (z ^ (3 - c)) + c) for z in range(4) for c in range(2)]
    beside = [(2 * z + c, 2 * (z ^ 1) + c) for z in range(4) for c in range(2)]
    f32 = jnp.float32
    V, S = pltpu.VMEM, pltpu.SMEM

    opened = [
        pltpu.with_memory_space_constraint(value, pltpu.HBM)
        for value in (link_source, link_count, owner_map, domains, amplitudes)
    ]
    word = jax.ShapeDtypeStruct((8, 128), jnp.int32)
    message, wanted_near, halves = call(
        functools.partial(open_kernel, sub_count),
        (word, word, jax.ShapeDtypeStruct((pairs, size // 2 + COORD_ROWS, size), f32)),
        (pltpu.HBM,) * len(opened),
        opened,
        scratch=[
            V(link_source.shape, jnp.int32),
            S(link_count.shape, jnp.int32),
            S(owner_map.shape, jnp.int32),
            V(domains.shape, jnp.int32),
            pltpu.SemaphoreType.DMA((4 + pairs,)),
        ],
    )
    asked = lax.ppermute(message, axes, across)
    near = lax.ppermute(halves, axes, beside)
    block = jax.ShapeDtypeStruct((size, size), f32)
    far = call(select_kernel, block, (V, V), (asked, amplitudes), moved=10**6)
    far = lax.ppermute(far, axes, across)

    lines = -(-positions.shape[1] // 128)
    lines = -(-lines // 16) * 16
    coords, far_rows, table = call(
        centres_kernel,
        (
            jax.ShapeDtypeStruct((pairs, COORD_ROWS, size), f32),
            jax.ShapeDtypeStruct((COORD_ROWS, size), f32),
            jax.ShapeDtypeStruct((4 * lines, 128), f32),
        ),
        (pltpu.HBM, pltpu.HBM, V, V),
        (
            pltpu.with_memory_space_constraint(positions, pltpu.HBM),
            pltpu.with_memory_space_constraint(vir_energy, pltpu.HBM),
            message,
            asked,
        ),
        scratch=[
            V(positions.shape, f32),
            V(vir_energy.shape, f32),
            pltpu.SemaphoreType.DMA((2,)),
        ],
        flops=10**9,
        moved=10**6,
    )
    small = (
        link_source,
        link_entry,
        link_count,
        owner_map,
        fock_values,
        pair_list,
        occ_energy,
    )
    share, weight, inverse, spread, high, low = call(
        functools.partial(own_kernel, sub_count),
        (
            jax.ShapeDtypeStruct(amplitudes.shape, f32),
            jax.ShapeDtypeStruct((2, pairs, 8, 128), f32),
            jax.ShapeDtypeStruct(amplitudes.shape, f32),
            jax.ShapeDtypeStruct((pairs, 3, size, 128), f32),
            jax.ShapeDtypeStruct(amplitudes.shape, jnp.bfloat16),
            jax.ShapeDtypeStruct(amplitudes.shape, jnp.bfloat16),
        ),
        (V, V, V, V) + (pltpu.HBM,) * len(small),
        (
            amplitudes,
            exchange_ints,
            coords,
            far_rows,
            *(pltpu.with_memory_space_constraint(value, pltpu.HBM) for value in small),
        ),
        scratch=[S(value.shape, value.dtype) for value in small]
        + [pltpu.SemaphoreType.DMA((len(small),))],
        flops=2 * 10**10,
        moved=4 * 10**7,
    )
    whole = jax.ShapeDtypeStruct(amplitudes.shape, f32)
    cost = dict(flops=10**9, moved=10**6)
    share = call(
        near_kernel, whole, (V,) * 6, (near, wanted_near, table, spread, weight, share), **cost
    )
    share = call(far_kernel, whole, (V,) * 5, (far, high, low, weight, share), **cost)
    other = lax.ppermute(share, "rep", [(0, 1), (1, 0)])
    return call(
        final_kernel,
        (whole, whole),
        (V,) * 4,
        (share, other, amplitudes, inverse),
        scratch=[V(amplitudes.shape, f32), V(amplitudes.shape, f32), pltpu.SemaphoreType.DMA((2 * pairs,))],
        result=pltpu.HBM,
        **cost,
    )


def solution(mesh):
    stored = ("groups", "pairs", "sub")
    in_specs = (
        P(stored, None, None),
        P(stored, None, None),
        P(stored, None),
        P(stored, None),
        P(stored, None),
        P(stored, None),
        P(stored),
        P("groups"),
        P("groups"),
        P("groups"),
        P("groups"),
        P(None, "groups"),
    )
    out_specs = (P(stored, None, None), P(stored, None, None))

    def run(*args):
        devices = mesh.shape["groups"] * mesh.shape["pairs"] * mesh.shape["sub"]
        known = (
            mesh.shape["pairs"] == 4
            and mesh.shape["rep"] == 2
            and args[0].shape[0] == 2 * devices
            and args[0].shape[1] == 256
        )
        return jax.shard_map(
            on_device_four if known else on_device_any,
            mesh=mesh,
            in_specs=in_specs,
            out_specs=out_specs,
            check_vma=False,
        )(*args)

    return run
```

```python
import functools

import jax
import jax.numpy as jnp
from jax import lax
from jax.experimental import pallas as pl
from jax.experimental.pallas import tpu as pltpu
from jax.sharding import PartitionSpec as P

intersection_rate = 2.0
COORD_ROWS = 8
LOG2_E = 1.4426950408889634
VMEM_LIMIT = 40 * 1024 * 1024


def product(left, right):
    return jnp.dot(left, right, precision=lax.Precision.HIGHEST, preferred_element_type=jnp.float32)


def pick_row(array, index):
    return lax.dynamic_index_in_dim(array, index, 0, keepdims=False)


def model_intersection(left_coords, right_coords):
    squared = jnp.zeros((left_coords.shape[1], right_coords.shape[1]), jnp.float32)
    for component in range(3):
        gap_now = left_coords[component][:, None] - right_coords[component][None, :]
        squared = squared + gap_now * gap_now
    return jnp.exp(-intersection_rate * squared)


def pair_local(block, integrals, pair_coords, pair_energy, pair_shift):
    metric = model_intersection(pair_coords, pair_coords)
    virtual_fock = metric * ((pair_energy[:, None] + pair_energy[None, :]) * 0.5)
    right_side = product(block, metric)
    left_side = product(metric, block)
    return (
        integrals
        + product(virtual_fock, right_side)
        + product(left_side, virtual_fock)
        - pair_shift * product(metric, right_side)
    )


def on_device_any(
    amplitudes,
    exchange_ints,
    pair_list,
    domains,
    link_source,
    link_entry,
    link_count,
    owner_map,
    fock_values,
    occ_energy,
    vir_energy,
    positions,
):
    pair_count = amplitudes.shape[0]
    link_slots = link_source.shape[1]
    row_count = lax.axis_size("pairs")
    sub_count = lax.axis_size("sub")
    core_count = lax.axis_size("rep")
    my_core = lax.axis_index("rep")
    coords = jnp.moveaxis(jnp.take(positions, domains, axis=1), 0, 1)
    energy = jnp.take(vir_energy, domains, axis=0)
    shift = jnp.take(occ_energy, pair_list[:, 0]) + jnp.take(occ_energy, pair_list[:, 1])
    is_live = jnp.arange(link_slots, dtype=jnp.int32)[None, :] < link_count[:, None]
    source_loc = jnp.take(owner_map, link_source)
    source_peer = source_loc // (pair_count * sub_count)
    source_slot = source_loc % pair_count
    peers = jnp.arange(row_count, dtype=jnp.int32)
    matched = is_live[:, :, None] & (source_peer[:, :, None] == peers[None, None, :])
    fock_weight = jnp.take(fock_values, link_entry)
    weight = jnp.sum(jnp.where(matched, fock_weight[:, :, None], 0.0), axis=1)
    wanted = jnp.max(jnp.where(matched, source_slot[:, :, None], 0), axis=(0, 1))
    asked = lax.all_to_all(wanted[:, None], "pairs", split_axis=0, concat_axis=0, tiled=True)[:, 0]
    fetched = lax.all_to_all(
        jnp.take(amplitudes, asked, axis=0), "pairs", split_axis=0, concat_axis=0, tiled=True
    )
    fetched_coords = lax.all_to_all(
        jnp.take(coords, asked, axis=0), "pairs", split_axis=0, concat_axis=0, tiled=True
    )

    def target(pair):
        local = pair_local(
            pick_row(amplitudes, pair),
            pick_row(exchange_ints, pair),
            pick_row(coords, pair),
            pick_row(energy, pair),
            pick_row(shift, pair),
        )

        def advance(peer, total):
            intersection = model_intersection(pick_row(coords, pair), pick_row(fetched_coords, peer))
            term = product(product(intersection, pick_row(fetched, peer)), intersection.T)
            return total - pick_row(pick_row(weight, pair), peer) * term

        return lax.fori_loop(0, row_count, advance, local)

    mine = jnp.arange(pair_count, dtype=jnp.int32) % core_count == my_core
    share = lax.map(
        lambda pair: lax.cond(
            pick_row(mine, pair), target, lambda _: jnp.zeros_like(amplitudes[0]), pair
        ),
        jnp.arange(pair_count, dtype=jnp.int32),
    )
    residual = lax.psum(share, "rep")
    denominator = energy[:, :, None] + energy[:, None, :] - shift[:, None, None]
    return residual, amplitudes - residual / denominator


def split(value):
    high = value.astype(jnp.bfloat16)
    low = (value - high.astype(jnp.float32)).astype(jnp.bfloat16)
    return high, low


NN = (((1,), (0,)), ((), ()))
NT = (((1,), (1,)), ((), ()))
TN = (((0,), (0,)), ((), ()))


def dot(left, right, dims):
    return lax.dot_general(left, right, dims, preferred_element_type=jnp.float32)


def dot3(left, right, dims=NN):
    return (
        dot(left[0], right[0], dims) + dot(left[0], right[1], dims) + dot(left[1], right[0], dims)
    )


def overlap(column, rows):
    squared = None
    for c in range(3):
        gap = column[:, c : c + 1] - rows[c : c + 1, :]
        squared = gap * gap if squared is None else squared + gap * gap
    return jnp.exp2(-intersection_rate * LOG2_E * squared)


def overlap_spread(spread_ref, p, rows):
    halves = []
    for k in range(rows.shape[1] // 128):
        squared = None
        for c in range(3):
            gap = spread_ref[p, c] - rows[c : c + 1, k * 128 : (k + 1) * 128]
            squared = gap * gap if squared is None else squared + gap * gap
        halves.append(jnp.exp2(-intersection_rate * LOG2_E * squared))
    return halves


def sandwich(metric, block):
    metric = split(metric)
    return dot3(split(dot3(metric, split(block))), metric, NT)


def start_all(copies):
    for copy in copies:
        copy.start()
    return copies


def partners():
    row = lax.axis_index("pairs")
    return row ^ (3 - lax.axis_index("rep")), row ^ 1


def open_kernel(
    sub_count,
    source_hbm,
    count_hbm,
    owner_hbm,
    domains_hbm,
    block_hbm,
    message_ref,
    wanted_near_ref,
    halves_ref,
    source_ref,
    count_ref,
    owner_ref,
    domains_ref,
    sems,
):
    pairs, links = source_ref.shape
    size = domains_ref.shape[1]
    half = size // 2
    start = pl.multiple_of(lax.axis_index("rep") * half, half)
    moves = [
        (source_hbm, source_ref),
        (count_hbm, count_ref),
        (owner_hbm, owner_ref),
        (domains_hbm, domains_ref),
    ]
    moves += [
        (block_hbm.at[p, pl.ds(start, half), :], halves_ref.at[p, pl.ds(0, half), :])
        for p in range(pairs)
    ]
    copies = [
        pltpu.make_async_copy(source, target, sems.at[k])
        for k, (source, target) in enumerate(moves)
    ]
    for copy in copies:
        copy.start()
    for copy in copies[:4]:
        copy.wait()
    source = source_ref[...]
    pair = lax.broadcasted_iota(jnp.int32, (pairs, links), 0)
    limit = jnp.zeros_like(source)
    for p in range(pairs):
        limit = jnp.where(pair == p, count_ref[p], limit)
    live = lax.broadcasted_iota(jnp.int32, (pairs, links), 1) < limit
    place = jnp.zeros_like(source)
    for k in range(owner_ref.shape[0]):
        place = jnp.where(source == k, owner_ref[k], place)
    there = lax.div(place, pairs * sub_count)
    slot = lax.rem(place, pairs)
    for peer, wanted_ref in zip(partners(), (message_ref, wanted_near_ref)):
        wish = jnp.where(live & (there == peer), slot, 0)
        wanted_ref[...] = jnp.broadcast_to(jnp.max(wish, keepdims=True), (8, 128))
    for p in range(pairs):
        for k in range(2):
            row = 4 + 2 * p + k
            message_ref[row : row + 1, :] = domains_ref[p : p + 1, k * 128 : (k + 1) * 128]
        halves_ref[p, half:, :] = jnp.broadcast_to(
            domains_ref[p : p + 1, :].astype(jnp.float32), (COORD_ROWS, size)
        )
    for copy in copies[4:]:
        copy.wait()


def look_up(index, table_ref, components, held):
    count = index.shape[1]
    rows = table_ref.shape[0] // held
    table = table_ref[: components * rows, :]
    first = table.astype(jnp.bfloat16)
    left = table - first.astype(jnp.float32)
    second = left.astype(jnp.bfloat16)
    third = (left - second.astype(jnp.float32)).astype(jnp.bfloat16)
    high = index // 128
    low = index - high * 128
    chosen = (lax.broadcasted_iota(jnp.int32, (rows, count), 0) == high).astype(
        jnp.float32
    ).astype(jnp.bfloat16)
    lane = lax.broadcasted_iota(jnp.int32, (128, count), 0) == low
    found = []
    for c in range(components):
        span = slice(c * rows, (c + 1) * rows)
        lines = (
            dot(first[span], chosen, TN)
            + dot(second[span], chosen, TN)
            + dot(third[span], chosen, TN)
        )
        found.append(jnp.sum(jnp.where(lane, lines, 0.0), axis=0, keepdims=True))
    return found


def domain_of(message_ref, p):
    row = 4 + 2 * p
    return jnp.concatenate([message_ref[row : row + 1, :], message_ref[row + 1 : row + 2, :]], axis=1)


def centres_kernel(
    positions_hbm,
    energy_hbm,
    message_ref,
    asked_ref,
    coords_ref,
    far_ref,
    table,
    positions_ref,
    energy_ref,
    sems,
):
    copies = [
        pltpu.make_async_copy(positions_hbm, positions_ref, sems.at[0]),
        pltpu.make_async_copy(energy_hbm, energy_ref, sems.at[1]),
    ]
    for copy in copies:
        copy.start()
    pairs, size = coords_ref.shape[0], coords_ref.shape[2]
    orbitals = positions_ref.shape[1]
    rows = table.shape[0] // 4
    whole, rest = orbitals // 128, orbitals % 128
    for c in range(4):
        table[c * rows + whole : (c + 1) * rows, :] = jnp.zeros((rows - whole, 128), jnp.float32)
    for copy in copies:
        copy.wait()
    for k in range(whole):
        table[pl.ds(k, 3, stride=rows), :] = positions_ref[:, k * 128 : (k + 1) * 128]
        table[3 * rows + k : 3 * rows + k + 1, :] = energy_ref[k * 128 : (k + 1) * 128].reshape(1, 128)
    if rest:
        table[pl.ds(whole, 3, stride=rows), :rest] = positions_ref[:, whole * 128 :]
        table[3 * rows + whole : 3 * rows + whole + 1, :rest] = energy_ref[whole * 128 :].reshape(
            1, rest
        )
    slot_one = jnp.max(message_ref[0:1, :]) > 0
    index = [domain_of(message_ref, p) for p in range(pairs)]
    index.append(jnp.where(slot_one, domain_of(asked_ref, 1), domain_of(asked_ref, 0)))
    found = look_up(jnp.concatenate(index, axis=1), table, 4, 4)
    found.append(jnp.zeros((COORD_ROWS - 4, (pairs + 1) * size), jnp.float32))
    found = jnp.concatenate(found, axis=0)
    for p in range(pairs):
        coords_ref[p] = found[:, p * size : (p + 1) * size]
    far_ref[...] = found[:, pairs * size :]


def select_kernel(asked_ref, block_ref, payload_ref):
    slot_one = jnp.max(asked_ref[0:1, :]) > 0
    payload_ref[...] = jnp.where(slot_one, block_ref[1], block_ref[0])


def own_kernel(
    sub_count,
    block_ref,
    integrals_ref,
    coords_ref,
    far_rows_ref,
    source_hbm,
    entry_hbm,
    count_hbm,
    owner_hbm,
    fock_hbm,
    pair_hbm,
    occ_hbm,
    share_ref,
    weight_ref,
    inverse_ref,
    spread_ref,
    high_ref,
    low_ref,
    source_ref,
    entry_ref,
    count_ref,
    owner_ref,
    fock_ref,
    pair_ref,
    occ_ref,
    sems,
):
    moves = (
        (source_hbm, source_ref),
        (entry_hbm, entry_ref),
        (count_hbm, count_ref),
        (owner_hbm, owner_ref),
        (fock_hbm, fock_ref),
        (pair_hbm, pair_ref),
        (occ_hbm, occ_ref),
    )
    copies = [
        pltpu.make_async_copy(source, target, sems.at[k])
        for k, (source, target) in enumerate(moves)
    ]
    for copy in copies:
        copy.start()
    pairs = block_ref.shape[0]
    links = source_ref.shape[1]
    core = lax.axis_index("rep")
    row = lax.axis_index("pairs")
    peers = partners()

    columns = [coords_ref[p].T for p in range(pairs)]
    for p in range(pairs):
        for c in range(3):
            spread_ref[p, c] = jnp.broadcast_to(columns[p][:, c : c + 1], spread_ref.shape[2:])
        high_ref[p], low_ref[p] = split(overlap(columns[p], far_rows_ref[...]))
    zero = core == 0
    column = jnp.where(zero, columns[0], columns[1])
    energy = (column[:, 3:4] + coords_ref[core, 3:4, :]) * 0.5
    block = block_ref[core]
    metric = split(overlap(column, coords_ref[core]))
    firsts = [split(dot3(split(value), metric)) for value in (block, block * energy)]
    plain, scaled = [dot3(metric, first) for first in firsts]

    for copy in copies:
        copy.wait()

    def look(m, carry):
        own_slot, weights = carry
        weights = list(weights)
        for p in range(pairs):
            place = owner_ref[source_ref[p, m]]
            peer = lax.div(place, pairs * sub_count)
            slot = lax.rem(place, pairs)
            live = m < count_ref[p]
            value = fock_ref[entry_ref[p, m]]
            own = live & (peer == row)
            own_slot = jnp.where(own, slot, own_slot)
            for k, hit in enumerate((own, live & (peer == peers[0]), live & (peer == peers[1]))):
                weights[3 * p + k] += jnp.where(hit, value, 0.0)
        return own_slot, tuple(weights)

    shifts = [occ_ref[pair_ref[p, 0]] + occ_ref[pair_ref[p, 1]] for p in range(pairs)]
    shift = jnp.where(zero, shifts[0], shifts[1])
    share_ref[core] = integrals_ref[core] + scaled + plain * (energy - shift)
    own_slot, weights = lax.fori_loop(
        0, links, look, (jnp.int32(0), (jnp.float32(0.0),) * (3 * pairs))
    )
    for p in range(pairs):
        for k in range(2):
            weight_ref[k, p] = jnp.full((8, 128), weights[3 * p + 1 + k], jnp.float32)
        inverse_ref[p] = 1.0 / (columns[p][:, 3:4] + coords_ref[p, 3:4, :] - shifts[p])
    own_weight = jnp.where(zero, weights[0], weights[3])
    own = overlap(column, coords_ref[own_slot])
    share_ref[core] = share_ref[core] - own_weight * sandwich(own, block_ref[own_slot])
    share_ref[1 - core] = jnp.zeros_like(block)


def near_kernel(near_ref, wanted_ref, table_ref, spread_ref, weight_ref, share_ref, total_ref):
    pairs, size = share_ref.shape[0], share_ref.shape[1]
    half = size // 2
    near = jnp.where(jnp.max(wanted_ref[...]) > 0, near_ref[1], near_ref[0])
    part = split(near[:half, :])
    rows = jnp.concatenate(
        look_up(near[half : half + 1, :].astype(jnp.int32), table_ref, 3, 4), axis=0
    )
    metrics, firsts = [], []
    for p in range(pairs):
        left, right = overlap_spread(spread_ref, p, rows)
        metrics.append(split(jnp.concatenate([left, right], axis=1)))
        side = split(jnp.where(lax.axis_index("rep") == 0, left, right))
        firsts.append(split(dot3(side, part)))
    for p in range(pairs):
        term = dot3(firsts[p], metrics[p], NT)
        total_ref[p] = share_ref[p] - weight_ref[1, p, 0:1, 0:1] * term


def far_kernel(far_ref, high_ref, low_ref, weight_ref, share_ref, total_ref):
    pairs = share_ref.shape[0]
    block = split(far_ref[...])
    firsts = [split(dot3((high_ref[p], low_ref[p]), block)) for p in range(pairs)]
    for p in range(pairs):
        term = dot3(firsts[p], (high_ref[p], low_ref[p]), NT)
        total_ref[p] = share_ref[p] - weight_ref[0, p, 0:1, 0:1] * term


def final_kernel(
    share_ref, other_ref, block_ref, inverse_ref, residual_hbm, updated_hbm, residual_ref, updated_ref, sems
):
    copies = []
    for p in range(share_ref.shape[0]):
        residual = share_ref[p] + other_ref[p]
        residual_ref[p] = residual
        updated_ref[p] = block_ref[p] - residual * inverse_ref[p]
        for k, (source, target) in enumerate(
            ((residual_ref, residual_hbm), (updated_ref, updated_hbm))
        ):
            copies.append(pltpu.make_async_copy(source.at[p], target.at[p], sems.at[2 * p + k]))
            copies[-1].start()
    for copy in copies:
        copy.wait()


def call(
    body, outs, spaces, args, scratch=(), flops=0, moved=0, limit=VMEM_LIMIT, result=pltpu.VMEM
):
    return pl.pallas_call(
        body,
        out_shape=outs,
        in_specs=[pl.BlockSpec(memory_space=space) for space in spaces],
        out_specs=jax.tree.map(lambda _: pl.BlockSpec(memory_space=result), outs),
        scratch_shapes=list(scratch),
        compiler_params=pltpu.CompilerParams(vmem_limit_bytes=limit),
        cost_estimate=pl.CostEstimate(flops=flops, bytes_accessed=moved, transcendentals=0),
    )(*args)


def on_device_four(
    amplitudes,
    exchange_ints,
    pair_list,
    domains,
    link_source,
    link_entry,
    link_count,
    owner_map,
    fock_values,
    occ_energy,
    vir_energy,
    positions,
):
    pairs, size = amplitudes.shape[0], amplitudes.shape[1]
    sub_count = lax.axis_size("sub")
    core = lax.axis_index("rep")
    row = lax.axis_index("pairs")
    axes = ("pairs", "rep")
    across = [(2 * z + c, 2 * (z ^ (3 - c)) + c) for z in range(4) for c in range(2)]
    beside = [(2 * z + c, 2 * (z ^ 1) + c) for z in range(4) for c in range(2)]
    f32 = jnp.float32
    V, S = pltpu.VMEM, pltpu.SMEM

    opened = [
        pltpu.with_memory_space_constraint(value, pltpu.HBM)
        for value in (link_source, link_count, owner_map, domains, amplitudes)
    ]
    word = jax.ShapeDtypeStruct((8, 128), jnp.int32)
    message, wanted_near, halves = call(
        functools.partial(open_kernel, sub_count),
        (word, word, jax.ShapeDtypeStruct((pairs, size // 2 + COORD_ROWS, size), f32)),
        (pltpu.HBM,) * len(opened),
        opened,
        scratch=[
            V(link_source.shape, jnp.int32),
            S(link_count.shape, jnp.int32),
            S(owner_map.shape, jnp.int32),
            V(domains.shape, jnp.int32),
            pltpu.SemaphoreType.DMA((4 + pairs,)),
        ],
    )
    asked = lax.ppermute(message, axes, across)
    near = lax.ppermute(halves, axes, beside)
    block = jax.ShapeDtypeStruct((size, size), f32)
    far = call(select_kernel, block, (V, V), (asked, amplitudes), moved=10**6)
    far = lax.ppermute(far, axes, across)

    lines = -(-positions.shape[1] // 128)
    lines = -(-lines // 16) * 16
    coords, far_rows, table = call(
        centres_kernel,
        (
            jax.ShapeDtypeStruct((pairs, COORD_ROWS, size), f32),
            jax.ShapeDtypeStruct((COORD_ROWS, size), f32),
            jax.ShapeDtypeStruct((4 * lines, 128), f32),
        ),
        (pltpu.HBM, pltpu.HBM, V, V),
        (
            pltpu.with_memory_space_constraint(positions, pltpu.HBM),
            pltpu.with_memory_space_constraint(vir_energy, pltpu.HBM),
            message,
            asked,
        ),
        scratch=[
            V(positions.shape, f32),
            V(vir_energy.shape, f32),
            pltpu.SemaphoreType.DMA((2,)),
        ],
        flops=10**9,
        moved=10**6,
    )
    small = (
        link_source,
        link_entry,
        link_count,
        owner_map,
        fock_values,
        pair_list,
        occ_energy,
    )
    share, weight, inverse, spread, high, low = call(
        functools.partial(own_kernel, sub_count),
        (
            jax.ShapeDtypeStruct(amplitudes.shape, f32),
            jax.ShapeDtypeStruct((2, pairs, 8, 128), f32),
            jax.ShapeDtypeStruct(amplitudes.shape, f32),
            jax.ShapeDtypeStruct((pairs, 3, size, 128), f32),
            jax.ShapeDtypeStruct(amplitudes.shape, jnp.bfloat16),
            jax.ShapeDtypeStruct(amplitudes.shape, jnp.bfloat16),
        ),
        (V, V, V, V) + (pltpu.HBM,) * len(small),
        (
            amplitudes,
            exchange_ints,
            coords,
            far_rows,
            *(pltpu.with_memory_space_constraint(value, pltpu.HBM) for value in small),
        ),
        scratch=[S(value.shape, value.dtype) for value in small]
        + [pltpu.SemaphoreType.DMA((len(small),))],
        flops=2 * 10**10,
        moved=4 * 10**7,
    )
    whole = jax.ShapeDtypeStruct(amplitudes.shape, f32)
    cost = dict(flops=10**9, moved=10**6)
    share = call(
        near_kernel, whole, (V,) * 6, (near, wanted_near, table, spread, weight, share), **cost
    )
    share = call(far_kernel, whole, (V,) * 5, (far, high, low, weight, share), **cost)
    other = lax.ppermute(share, "rep", [(0, 1), (1, 0)])
    return call(
        final_kernel,
        (whole, whole),
        (V,) * 4,
        (share, other, amplitudes, inverse),
        scratch=[V(amplitudes.shape, f32), V(amplitudes.shape, f32), pltpu.SemaphoreType.DMA((2 * pairs,))],
        result=pltpu.HBM,
        **cost,
    )


def solution(mesh):
    stored = ("groups", "pairs", "sub")
    in_specs = (
        P(stored, None, None),
        P(stored, None, None),
        P(stored, None),
        P(stored, None),
        P(stored, None),
        P(stored, None),
        P(stored),
        P("groups"),
        P("groups"),
        P("groups"),
        P("groups"),
        P(None, "groups"),
    )
    out_specs = (P(stored, None, None), P(stored, None, None))

    def run(*args):
        devices = mesh.shape["groups"] * mesh.shape["pairs"] * mesh.shape["sub"]
        known = (
            mesh.shape["pairs"] == 4
            and mesh.shape["rep"] == 2
            and args[0].shape[0] == 2 * devices
            and args[0].shape[1] == 256
        )
        return jax.shard_map(
            on_device_four if known else on_device_any,
            mesh=mesh,
            in_specs=in_specs,
            out_specs=out_specs,
            check_vma=False,
        )(*args)

    return run
```

```python
import functools

import jax
import jax.numpy as jnp
from jax import lax
from jax.experimental import pallas as pl
from jax.experimental.pallas import tpu as pltpu
from jax.sharding import PartitionSpec as P

intersection_rate = 2.0
COORD_ROWS = 8
LOG2_E = 1.4426950408889634
VMEM_LIMIT = 40 * 1024 * 1024


def product(left, right):
    return jnp.dot(left, right, precision=lax.Precision.HIGHEST, preferred_element_type=jnp.float32)


def pick_row(array, index):
    return lax.dynamic_index_in_dim(array, index, 0, keepdims=False)


def model_intersection(left_coords, right_coords):
    squared = jnp.zeros((left_coords.shape[1], right_coords.shape[1]), jnp.float32)
    for component in range(3):
        gap_now = left_coords[component][:, None] - right_coords[component][None, :]
        squared = squared + gap_now * gap_now
    return jnp.exp(-intersection_rate * squared)


def pair_local(block, integrals, pair_coords, pair_energy, pair_shift):
    metric = model_intersection(pair_coords, pair_coords)
    virtual_fock = metric * ((pair_energy[:, None] + pair_energy[None, :]) * 0.5)
    right_side = product(block, metric)
    left_side = product(metric, block)
    return (
        integrals
        + product(virtual_fock, right_side)
        + product(left_side, virtual_fock)
        - pair_shift * product(metric, right_side)
    )


def on_device_any(
    amplitudes,
    exchange_ints,
    pair_list,
    domains,
    link_source,
    link_entry,
    link_count,
    owner_map,
    fock_values,
    occ_energy,
    vir_energy,
    positions,
):
    pair_count = amplitudes.shape[0]
    link_slots = link_source.shape[1]
    row_count = lax.axis_size("pairs")
    sub_count = lax.axis_size("sub")
    core_count = lax.axis_size("rep")
    my_core = lax.axis_index("rep")
    coords = jnp.moveaxis(jnp.take(positions, domains, axis=1), 0, 1)
    energy = jnp.take(vir_energy, domains, axis=0)
    shift = jnp.take(occ_energy, pair_list[:, 0]) + jnp.take(occ_energy, pair_list[:, 1])
    is_live = jnp.arange(link_slots, dtype=jnp.int32)[None, :] < link_count[:, None]
    source_loc = jnp.take(owner_map, link_source)
    source_peer = source_loc // (pair_count * sub_count)
    source_slot = source_loc % pair_count
    peers = jnp.arange(row_count, dtype=jnp.int32)
    matched = is_live[:, :, None] & (source_peer[:, :, None] == peers[None, None, :])
    fock_weight = jnp.take(fock_values, link_entry)
    weight = jnp.sum(jnp.where(matched, fock_weight[:, :, None], 0.0), axis=1)
    wanted = jnp.max(jnp.where(matched, source_slot[:, :, None], 0), axis=(0, 1))
    asked = lax.all_to_all(wanted[:, None], "pairs", split_axis=0, concat_axis=0, tiled=True)[:, 0]
    fetched = lax.all_to_all(
        jnp.take(amplitudes, asked, axis=0), "pairs", split_axis=0, concat_axis=0, tiled=True
    )
    fetched_coords = lax.all_to_all(
        jnp.take(coords, asked, axis=0), "pairs", split_axis=0, concat_axis=0, tiled=True
    )

    def target(pair):
        local = pair_local(
            pick_row(amplitudes, pair),
            pick_row(exchange_ints, pair),
            pick_row(coords, pair),
            pick_row(energy, pair),
            pick_row(shift, pair),
        )

        def advance(peer, total):
            intersection = model_intersection(pick_row(coords, pair), pick_row(fetched_coords, peer))
            term = product(product(intersection, pick_row(fetched, peer)), intersection.T)
            return total - pick_row(pick_row(weight, pair), peer) * term

        return lax.fori_loop(0, row_count, advance, local)

    mine = jnp.arange(pair_count, dtype=jnp.int32) % core_count == my_core
    share = lax.map(
        lambda pair: lax.cond(
            pick_row(mine, pair), target, lambda _: jnp.zeros_like(amplitudes[0]), pair
        ),
        jnp.arange(pair_count, dtype=jnp.int32),
    )
    residual = lax.psum(share, "rep")
    denominator = energy[:, :, None] + energy[:, None, :] - shift[:, None, None]
    return residual, amplitudes - residual / denominator


def split(value):
    high = value.astype(jnp.bfloat16)
    low = (value - high.astype(jnp.float32)).astype(jnp.bfloat16)
    return high, low


NN = (((1,), (0,)), ((), ()))
NT = (((1,), (1,)), ((), ()))
TN = (((0,), (0,)), ((), ()))


def dot(left, right, dims):
    return lax.dot_general(left, right, dims, preferred_element_type=jnp.float32)


def dot3(left, right, dims=NN):
    return (
        dot(left[0], right[0], dims) + dot(left[0], right[1], dims) + dot(left[1], right[0], dims)
    )


def overlap(column, rows):
    squared = None
    for c in range(3):
        gap = column[:, c : c + 1] - rows[c : c + 1, :]
        squared = gap * gap if squared is None else squared + gap * gap
    return jnp.exp2(-intersection_rate * LOG2_E * squared)


def overlap_spread(spread_ref, p, rows):
    halves = []
    for k in range(rows.shape[1] // 128):
        squared = None
        for c in range(3):
            gap = spread_ref[p, c] - rows[c : c + 1, k * 128 : (k + 1) * 128]
            squared = gap * gap if squared is None else squared + gap * gap
        halves.append(jnp.exp2(-intersection_rate * LOG2_E * squared))
    return halves


def sandwich(metric, block):
    metric = split(metric)
    return dot3(split(dot3(metric, split(block))), metric, NT)


def start_all(copies):
    for copy in copies:
        copy.start()
    return copies


def parts_of(value, divisor):
    if divisor & (divisor - 1) == 0:
        return value >> (divisor.bit_length() - 1), value & (divisor - 1)
    return lax.div(value, divisor), lax.rem(value, divisor)


def partners():
    row = lax.axis_index("pairs")
    return row ^ (3 - lax.axis_index("rep")), row ^ 1


def open_kernel(
    sub_count,
    source_hbm,
    count_hbm,
    owner_hbm,
    domains_hbm,
    block_hbm,
    message_ref,
    wanted_near_ref,
    halves_ref,
    source_ref,
    count_ref,
    owner_ref,
    domains_ref,
    sems,
):
    pairs, links = source_ref.shape
    size = domains_ref.shape[1]
    half = size // 2
    start = pl.multiple_of(lax.axis_index("rep") * half, half)
    moves = [
        (source_hbm, source_ref),
        (count_hbm, count_ref),
        (owner_hbm, owner_ref),
        (domains_hbm, domains_ref),
    ]
    moves += [
        (block_hbm.at[p, pl.ds(start, half), :], halves_ref.at[p, pl.ds(0, half), :])
        for p in range(pairs)
    ]
    copies = [
        pltpu.make_async_copy(source, target, sems.at[k])
        for k, (source, target) in enumerate(moves)
    ]
    for copy in copies:
        copy.start()
    for copy in copies[:4]:
        copy.wait()
    source = source_ref[...]
    pair = lax.broadcasted_iota(jnp.int32, (pairs, links), 0)
    limit = jnp.zeros_like(source)
    for p in range(pairs):
        limit = jnp.where(pair == p, count_ref[p], limit)
    live = lax.broadcasted_iota(jnp.int32, (pairs, links), 1) < limit
    place = jnp.zeros_like(source)
    for k in range(owner_ref.shape[0]):
        place = jnp.where(source == k, owner_ref[k], place)
    there, _ = parts_of(place, pairs * sub_count)
    _, slot = parts_of(place, pairs)
    for peer, wanted_ref in zip(partners(), (message_ref, wanted_near_ref)):
        wish = jnp.where(live & (there == peer), slot, 0)
        wanted_ref[...] = jnp.broadcast_to(jnp.max(wish, keepdims=True), (8, 128))
    for p in range(pairs):
        for k in range(2):
            row = 4 + 2 * p + k
            message_ref[row : row + 1, :] = domains_ref[p : p + 1, k * 128 : (k + 1) * 128]
        halves_ref[p, half:, :] = jnp.broadcast_to(
            domains_ref[p : p + 1, :].astype(jnp.float32), (COORD_ROWS, size)
        )
    for copy in copies[4:]:
        copy.wait()


def look_up(index, table_ref, components, held):
    count = index.shape[1]
    rows = table_ref.shape[0] // held
    table = table_ref[: components * rows, :]
    first = table.astype(jnp.bfloat16)
    left = table - first.astype(jnp.float32)
    second = left.astype(jnp.bfloat16)
    third = (left - second.astype(jnp.float32)).astype(jnp.bfloat16)
    high = index // 128
    low = index - high * 128
    chosen = (lax.broadcasted_iota(jnp.int32, (rows, count), 0) == high).astype(
        jnp.float32
    ).astype(jnp.bfloat16)
    lane = lax.broadcasted_iota(jnp.int32, (128, count), 0) == low
    found = []
    for c in range(components):
        span = slice(c * rows, (c + 1) * rows)
        lines = (
            dot(first[span], chosen, TN)
            + dot(second[span], chosen, TN)
            + dot(third[span], chosen, TN)
        )
        found.append(jnp.sum(jnp.where(lane, lines, 0.0), axis=0, keepdims=True))
    return found


def domain_of(message_ref, p):
    row = 4 + 2 * p
    return jnp.concatenate([message_ref[row : row + 1, :], message_ref[row + 1 : row + 2, :]], axis=1)


def centres_kernel(
    positions_hbm,
    energy_hbm,
    message_ref,
    asked_ref,
    coords_ref,
    far_ref,
    table,
    positions_ref,
    energy_ref,
    sems,
):
    copies = [
        pltpu.make_async_copy(positions_hbm, positions_ref, sems.at[0]),
        pltpu.make_async_copy(energy_hbm, energy_ref, sems.at[1]),
    ]
    for copy in copies:
        copy.start()
    pairs, size = coords_ref.shape[0], coords_ref.shape[2]
    orbitals = positions_ref.shape[1]
    rows = table.shape[0] // 4
    whole, rest = orbitals // 128, orbitals % 128
    for c in range(4):
        table[c * rows + whole : (c + 1) * rows, :] = jnp.zeros((rows - whole, 128), jnp.float32)
    for copy in copies:
        copy.wait()
    for k in range(whole):
        table[pl.ds(k, 3, stride=rows), :] = positions_ref[:, k * 128 : (k + 1) * 128]
        table[3 * rows + k : 3 * rows + k + 1, :] = energy_ref[k * 128 : (k + 1) * 128].reshape(1, 128)
    if rest:
        table[pl.ds(whole, 3, stride=rows), :rest] = positions_ref[:, whole * 128 :]
        table[3 * rows + whole : 3 * rows + whole + 1, :rest] = energy_ref[whole * 128 :].reshape(
            1, rest
        )
    slot_one = jnp.max(message_ref[0:1, :]) > 0
    index = [domain_of(message_ref, p) for p in range(pairs)]
    index.append(jnp.where(slot_one, domain_of(asked_ref, 1), domain_of(asked_ref, 0)))
    found = look_up(jnp.concatenate(index, axis=1), table, 4, 4)
    found.append(jnp.zeros((COORD_ROWS - 4, (pairs + 1) * size), jnp.float32))
    found = jnp.concatenate(found, axis=0)
    for p in range(pairs):
        coords_ref[p] = found[:, p * size : (p + 1) * size]
    far_ref[...] = found[:, pairs * size :]


def select_kernel(asked_ref, block_ref, payload_ref):
    for k in range(payload_ref.shape[1] // 128):
        span = slice(k * 128, (k + 1) * 128)
        slot_one = jnp.broadcast_to(asked_ref[0:1, :], (payload_ref.shape[0], 128)) > 0
        payload_ref[:, span] = jnp.where(slot_one, block_ref[1, :, span], block_ref[0, :, span])


def own_kernel(
    sub_count,
    block_ref,
    integrals_ref,
    coords_ref,
    far_rows_ref,
    source_hbm,
    entry_hbm,
    count_hbm,
    owner_hbm,
    fock_hbm,
    pair_hbm,
    occ_hbm,
    share_ref,
    weight_ref,
    inverse_ref,
    spread_ref,
    high_ref,
    low_ref,
    source_ref,
    entry_ref,
    count_ref,
    owner_ref,
    fock_ref,
    pair_ref,
    occ_ref,
    sems,
):
    moves = (
        (source_hbm, source_ref),
        (entry_hbm, entry_ref),
        (count_hbm, count_ref),
        (owner_hbm, owner_ref),
        (fock_hbm, fock_ref),
        (pair_hbm, pair_ref),
        (occ_hbm, occ_ref),
    )
    copies = [
        pltpu.make_async_copy(source, target, sems.at[k])
        for k, (source, target) in enumerate(moves)
    ]
    for copy in copies:
        copy.start()
    pairs = block_ref.shape[0]
    links = source_ref.shape[1]
    core = lax.axis_index("rep")
    row = lax.axis_index("pairs")
    peers = partners()

    columns = [coords_ref[p].T for p in range(pairs)]
    for p in range(pairs):
        for c in range(3):
            spread_ref[p, c] = jnp.broadcast_to(columns[p][:, c : c + 1], spread_ref.shape[2:])
        high_ref[p], low_ref[p] = split(overlap(columns[p], far_rows_ref[...]))
    zero = core == 0
    column = jnp.where(zero, columns[0], columns[1])
    energy = (column[:, 3:4] + coords_ref[core, 3:4, :]) * 0.5
    block = block_ref[core]
    metric = split(overlap(column, coords_ref[core]))
    firsts = [split(dot3(split(value), metric)) for value in (block, block * energy)]
    plain, scaled = [dot3(metric, first) for first in firsts]

    for copy in copies:
        copy.wait()

    def look(m, carry):
        own_slot, weights = carry
        weights = list(weights)
        for p in range(pairs):
            place = owner_ref[source_ref[p, m]]
            peer, _ = parts_of(place, pairs * sub_count)
            _, slot = parts_of(place, pairs)
            live = m < count_ref[p]
            value = fock_ref[entry_ref[p, m]]
            own = live & (peer == row)
            own_slot = jnp.where(own, slot, own_slot)
            for k, hit in enumerate((own, live & (peer == peers[0]), live & (peer == peers[1]))):
                weights[3 * p + k] += jnp.where(hit, value, 0.0)
        return own_slot, tuple(weights)

    shifts = [occ_ref[pair_ref[p, 0]] + occ_ref[pair_ref[p, 1]] for p in range(pairs)]
    shift = jnp.where(zero, shifts[0], shifts[1])
    share_ref[core] = integrals_ref[core] + scaled + plain * (energy - shift)
    own_slot, weights = lax.fori_loop(
        0, links, look, (jnp.int32(0), (jnp.float32(0.0),) * (3 * pairs))
    )
    for p in range(pairs):
        for k in range(2):
            weight_ref[k, p] = jnp.full((8, 128), weights[3 * p + 1 + k], jnp.float32)
        inverse_ref[p] = 1.0 / (columns[p][:, 3:4] + coords_ref[p, 3:4, :] - shifts[p])
    own_weight = jnp.where(zero, weights[0], weights[3])
    own = overlap(column, coords_ref[own_slot])
    share_ref[core] = share_ref[core] - own_weight * sandwich(own, block_ref[own_slot])
    share_ref[1 - core] = jnp.zeros_like(block)


def near_kernel(near_ref, wanted_ref, table_ref, spread_ref, weight_ref, share_ref, total_ref):
    pairs, size = share_ref.shape[0], share_ref.shape[1]
    half = size // 2
    near = jnp.where(jnp.max(wanted_ref[...]) > 0, near_ref[1], near_ref[0])
    part = split(near[:half, :])
    rows = jnp.concatenate(
        look_up(near[half : half + 1, :].astype(jnp.int32), table_ref, 3, 4), axis=0
    )
    metrics, firsts = [], []
    for p in range(pairs):
        left, right = overlap_spread(spread_ref, p, rows)
        metrics.append(split(jnp.concatenate([left, right], axis=1)))
        side = split(jnp.where(lax.axis_index("rep") == 0, left, right))
        firsts.append(split(dot3(side, part)))
    for p in range(pairs):
        term = dot3(firsts[p], metrics[p], NT)
        total_ref[p] = share_ref[p] - weight_ref[1, p, 0:1, 0:1] * term


def far_kernel(far_ref, high_ref, low_ref, weight_ref, share_ref, total_ref):
    pairs = share_ref.shape[0]
    block = split(far_ref[...])
    firsts = [split(dot3((high_ref[p], low_ref[p]), block)) for p in range(pairs)]
    for p in range(pairs):
        term = dot3(firsts[p], (high_ref[p], low_ref[p]), NT)
        total_ref[p] = share_ref[p] - weight_ref[0, p, 0:1, 0:1] * term


def final_kernel(
    share_ref, other_ref, block_ref, inverse_ref, residual_hbm, updated_hbm, residual_ref, updated_ref, sems
):
    copies = []
    for p in range(share_ref.shape[0]):
        residual = share_ref[p] + other_ref[p]
        residual_ref[p] = residual
        updated_ref[p] = block_ref[p] - residual * inverse_ref[p]
        for k, (source, target) in enumerate(
            ((residual_ref, residual_hbm), (updated_ref, updated_hbm))
        ):
            copies.append(pltpu.make_async_copy(source.at[p], target.at[p], sems.at[2 * p + k]))
            copies[-1].start()
    for copy in copies:
        copy.wait()


def call(
    body, outs, spaces, args, scratch=(), flops=0, moved=0, limit=VMEM_LIMIT, result=pltpu.VMEM
):
    return pl.pallas_call(
        body,
        out_shape=outs,
        in_specs=[pl.BlockSpec(memory_space=space) for space in spaces],
        out_specs=jax.tree.map(lambda _: pl.BlockSpec(memory_space=result), outs),
        scratch_shapes=list(scratch),
        compiler_params=pltpu.CompilerParams(vmem_limit_bytes=limit),
        cost_estimate=pl.CostEstimate(flops=flops, bytes_accessed=moved, transcendentals=0),
    )(*args)


def on_device_four(
    amplitudes,
    exchange_ints,
    pair_list,
    domains,
    link_source,
    link_entry,
    link_count,
    owner_map,
    fock_values,
    occ_energy,
    vir_energy,
    positions,
):
    pairs, size = amplitudes.shape[0], amplitudes.shape[1]
    sub_count = lax.axis_size("sub")
    core = lax.axis_index("rep")
    row = lax.axis_index("pairs")
    axes = ("pairs", "rep")
    across = [(2 * z + c, 2 * (z ^ (3 - c)) + c) for z in range(4) for c in range(2)]
    beside = [(2 * z + c, 2 * (z ^ 1) + c) for z in range(4) for c in range(2)]
    f32 = jnp.float32
    V, S = pltpu.VMEM, pltpu.SMEM

    opened = [
        pltpu.with_memory_space_constraint(value, pltpu.HBM)
        for value in (link_source, link_count, owner_map, domains, amplitudes)
    ]
    word = jax.ShapeDtypeStruct((8, 128), jnp.int32)
    message, wanted_near, halves = call(
        functools.partial(open_kernel, sub_count),
        (word, word, jax.ShapeDtypeStruct((pairs, size // 2 + COORD_ROWS, size), f32)),
        (pltpu.HBM,) * len(opened),
        opened,
        scratch=[
            V(link_source.shape, jnp.int32),
            S(link_count.shape, jnp.int32),
            S(owner_map.shape, jnp.int32),
            V(domains.shape, jnp.int32),
            pltpu.SemaphoreType.DMA((4 + pairs,)),
        ],
    )
    asked = lax.ppermute(message, axes, across)
    near = lax.ppermute(halves, axes, beside)
    block = jax.ShapeDtypeStruct((size, size), f32)
    far = call(select_kernel, block, (V, V), (asked, amplitudes), moved=10**6)
    far = lax.ppermute(far, axes, across)

    lines = -(-positions.shape[1] // 128)
    lines = -(-lines // 16) * 16
    coords, far_rows, table = call(
        centres_kernel,
        (
            jax.ShapeDtypeStruct((pairs, COORD_ROWS, size), f32),
            jax.ShapeDtypeStruct((COORD_ROWS, size), f32),
            jax.ShapeDtypeStruct((4 * lines, 128), f32),
        ),
        (pltpu.HBM, pltpu.HBM, V, V),
        (
            pltpu.with_memory_space_constraint(positions, pltpu.HBM),
            pltpu.with_memory_space_constraint(vir_energy, pltpu.HBM),
            message,
            asked,
        ),
        scratch=[
            V(positions.shape, f32),
            V(vir_energy.shape, f32),
            pltpu.SemaphoreType.DMA((2,)),
        ],
        flops=10**9,
        moved=10**6,
    )
    small = (
        link_source,
        link_entry,
        link_count,
        owner_map,
        fock_values,
        pair_list,
        occ_energy,
    )
    share, weight, inverse, spread, high, low = call(
        functools.partial(own_kernel, sub_count),
        (
            jax.ShapeDtypeStruct(amplitudes.shape, f32),
            jax.ShapeDtypeStruct((2, pairs, 8, 128), f32),
            jax.ShapeDtypeStruct(amplitudes.shape, f32),
            jax.ShapeDtypeStruct((pairs, 3, size, 128), f32),
            jax.ShapeDtypeStruct(amplitudes.shape, jnp.bfloat16),
            jax.ShapeDtypeStruct(amplitudes.shape, jnp.bfloat16),
        ),
        (V, V, V, V) + (pltpu.HBM,) * len(small),
        (
            amplitudes,
            exchange_ints,
            coords,
            far_rows,
            *(pltpu.with_memory_space_constraint(value, pltpu.HBM) for value in small),
        ),
        scratch=[S(value.shape, value.dtype) for value in small]
        + [pltpu.SemaphoreType.DMA((len(small),))],
        flops=2 * 10**10,
        moved=4 * 10**7,
    )
    whole = jax.ShapeDtypeStruct(amplitudes.shape, f32)
    cost = dict(flops=10**9, moved=10**6)
    share = call(
        near_kernel, whole, (V,) * 6, (near, wanted_near, table, spread, weight, share), **cost
    )
    share = call(far_kernel, whole, (V,) * 5, (far, high, low, weight, share), **cost)
    other = lax.ppermute(share, "rep", [(0, 1), (1, 0)])
    return call(
        final_kernel,
        (whole, whole),
        (V,) * 4,
        (share, other, amplitudes, inverse),
        scratch=[V(amplitudes.shape, f32), V(amplitudes.shape, f32), pltpu.SemaphoreType.DMA((2 * pairs,))],
        result=pltpu.HBM,
        **cost,
    )


def solution(mesh):
    stored = ("groups", "pairs", "sub")
    in_specs = (
        P(stored, None, None),
        P(stored, None, None),
        P(stored, None),
        P(stored, None),
        P(stored, None),
        P(stored, None),
        P(stored),
        P("groups"),
        P("groups"),
        P("groups"),
        P("groups"),
        P(None, "groups"),
    )
    out_specs = (P(stored, None, None), P(stored, None, None))

    def run(*args):
        devices = mesh.shape["groups"] * mesh.shape["pairs"] * mesh.shape["sub"]
        known = (
            mesh.shape["pairs"] == 4
            and mesh.shape["rep"] == 2
            and args[0].shape[0] == 2 * devices
            and args[0].shape[1] == 256
        )
        return jax.shard_map(
            on_device_four if known else on_device_any,
            mesh=mesh,
            in_specs=in_specs,
            out_specs=out_specs,
            check_vma=False,
        )(*args)

    return run
```

```python
import functools

import jax
import jax.numpy as jnp
from jax import lax
from jax.experimental import pallas as pl
from jax.experimental.pallas import tpu as pltpu
from jax.sharding import PartitionSpec as P

intersection_rate = 2.0
COORD_ROWS = 8
LOG2_E = 1.4426950408889634
VMEM_LIMIT = 40 * 1024 * 1024


def product(left, right):
    return jnp.dot(left, right, precision=lax.Precision.HIGHEST, preferred_element_type=jnp.float32)


def pick_row(array, index):
    return lax.dynamic_index_in_dim(array, index, 0, keepdims=False)


def model_intersection(left_coords, right_coords):
    squared = jnp.zeros((left_coords.shape[1], right_coords.shape[1]), jnp.float32)
    for component in range(3):
        gap_now = left_coords[component][:, None] - right_coords[component][None, :]
        squared = squared + gap_now * gap_now
    return jnp.exp(-intersection_rate * squared)


def pair_local(block, integrals, pair_coords, pair_energy, pair_shift):
    metric = model_intersection(pair_coords, pair_coords)
    virtual_fock = metric * ((pair_energy[:, None] + pair_energy[None, :]) * 0.5)
    right_side = product(block, metric)
    left_side = product(metric, block)
    return (
        integrals
        + product(virtual_fock, right_side)
        + product(left_side, virtual_fock)
        - pair_shift * product(metric, right_side)
    )


def on_device_any(
    amplitudes,
    exchange_ints,
    pair_list,
    domains,
    link_source,
    link_entry,
    link_count,
    owner_map,
    fock_values,
    occ_energy,
    vir_energy,
    positions,
):
    pair_count = amplitudes.shape[0]
    link_slots = link_source.shape[1]
    row_count = lax.axis_size("pairs")
    sub_count = lax.axis_size("sub")
    core_count = lax.axis_size("rep")
    my_core = lax.axis_index("rep")
    coords = jnp.moveaxis(jnp.take(positions, domains, axis=1), 0, 1)
    energy = jnp.take(vir_energy, domains, axis=0)
    shift = jnp.take(occ_energy, pair_list[:, 0]) + jnp.take(occ_energy, pair_list[:, 1])
    is_live = jnp.arange(link_slots, dtype=jnp.int32)[None, :] < link_count[:, None]
    source_loc = jnp.take(owner_map, link_source)
    source_peer = source_loc // (pair_count * sub_count)
    source_slot = source_loc % pair_count
    peers = jnp.arange(row_count, dtype=jnp.int32)
    matched = is_live[:, :, None] & (source_peer[:, :, None] == peers[None, None, :])
    fock_weight = jnp.take(fock_values, link_entry)
    weight = jnp.sum(jnp.where(matched, fock_weight[:, :, None], 0.0), axis=1)
    wanted = jnp.max(jnp.where(matched, source_slot[:, :, None], 0), axis=(0, 1))
    asked = lax.all_to_all(wanted[:, None], "pairs", split_axis=0, concat_axis=0, tiled=True)[:, 0]
    fetched = lax.all_to_all(
        jnp.take(amplitudes, asked, axis=0), "pairs", split_axis=0, concat_axis=0, tiled=True
    )
    fetched_coords = lax.all_to_all(
        jnp.take(coords, asked, axis=0), "pairs", split_axis=0, concat_axis=0, tiled=True
    )

    def target(pair):
        local = pair_local(
            pick_row(amplitudes, pair),
            pick_row(exchange_ints, pair),
            pick_row(coords, pair),
            pick_row(energy, pair),
            pick_row(shift, pair),
        )

        def advance(peer, total):
            intersection = model_intersection(pick_row(coords, pair), pick_row(fetched_coords, peer))
            term = product(product(intersection, pick_row(fetched, peer)), intersection.T)
            return total - pick_row(pick_row(weight, pair), peer) * term

        return lax.fori_loop(0, row_count, advance, local)

    mine = jnp.arange(pair_count, dtype=jnp.int32) % core_count == my_core
    share = lax.map(
        lambda pair: lax.cond(
            pick_row(mine, pair), target, lambda _: jnp.zeros_like(amplitudes[0]), pair
        ),
        jnp.arange(pair_count, dtype=jnp.int32),
    )
    residual = lax.psum(share, "rep")
    denominator = energy[:, :, None] + energy[:, None, :] - shift[:, None, None]
    return residual, amplitudes - residual / denominator


def split(value):
    high = value.astype(jnp.bfloat16)
    low = (value - high.astype(jnp.float32)).astype(jnp.bfloat16)
    return high, low


NN = (((1,), (0,)), ((), ()))
NT = (((1,), (1,)), ((), ()))
TN = (((0,), (0,)), ((), ()))


def dot(left, right, dims):
    return lax.dot_general(left, right, dims, preferred_element_type=jnp.float32)


def dot3(left, right, dims=NN):
    return (
        dot(left[0], right[0], dims) + dot(left[0], right[1], dims) + dot(left[1], right[0], dims)
    )


def overlap(column, rows):
    squared = None
    for c in range(3):
        gap = column[:, c : c + 1] - rows[c : c + 1, :]
        squared = gap * gap if squared is None else squared + gap * gap
    return jnp.exp2(-intersection_rate * LOG2_E * squared)


def overlap_spread(spread_ref, p, rows):
    halves = []
    for k in range(rows.shape[1] // 128):
        squared = None
        for c in range(3):
            gap = spread_ref[p, c] - rows[c : c + 1, k * 128 : (k + 1) * 128]
            squared = gap * gap if squared is None else squared + gap * gap
        halves.append(jnp.exp2(-intersection_rate * LOG2_E * squared))
    return halves


def sandwich(metric, block):
    metric = split(metric)
    return dot3(split(dot3(metric, split(block))), metric, NT)


def start_all(copies):
    for copy in copies:
        copy.start()
    return copies


def parts_of(value, divisor):
    if divisor & (divisor - 1) == 0:
        return value >> (divisor.bit_length() - 1), value & (divisor - 1)
    return lax.div(value, divisor), lax.rem(value, divisor)


def outer_core(row):
    return 1 if row in (1,) else 0


def partners():
    row = lax.axis_index("pairs")
    outer = jnp.int32(0)
    for z in range(4):
        outer = jnp.where(row == z, outer_core(z), outer)
    return jnp.where(lax.axis_index("rep") == outer, row ^ 3, row ^ 2), row ^ 1


def open_kernel(
    sub_count,
    source_hbm,
    count_hbm,
    owner_hbm,
    domains_hbm,
    block_hbm,
    message_ref,
    wanted_near_ref,
    halves_ref,
    source_ref,
    count_ref,
    owner_ref,
    domains_ref,
    sems,
):
    pairs, links = source_ref.shape
    size = domains_ref.shape[1]
    half = size // 2
    start = pl.multiple_of(lax.axis_index("rep") * half, half)
    moves = [
        (source_hbm, source_ref),
        (count_hbm, count_ref),
        (owner_hbm, owner_ref),
        (domains_hbm, domains_ref),
    ]
    moves += [
        (block_hbm.at[p, pl.ds(start, half), :], halves_ref.at[p, pl.ds(0, half), :])
        for p in range(pairs)
    ]
    copies = [
        pltpu.make_async_copy(source, target, sems.at[k])
        for k, (source, target) in enumerate(moves)
    ]
    for copy in copies:
        copy.start()
    for copy in copies[:4]:
        copy.wait()
    source = source_ref[...]
    pair = lax.broadcasted_iota(jnp.int32, (pairs, links), 0)
    limit = jnp.zeros_like(source)
    for p in range(pairs):
        limit = jnp.where(pair == p, count_ref[p], limit)
    live = lax.broadcasted_iota(jnp.int32, (pairs, links), 1) < limit
    place = jnp.zeros_like(source)
    for k in range(owner_ref.shape[0]):
        place = jnp.where(source == k, owner_ref[k], place)
    there, _ = parts_of(place, pairs * sub_count)
    _, slot = parts_of(place, pairs)
    for peer, wanted_ref in zip(partners(), (message_ref, wanted_near_ref)):
        wish = jnp.where(live & (there == peer), slot, 0)
        wanted_ref[...] = jnp.broadcast_to(jnp.max(wish, keepdims=True), (8, 128))
    for p in range(pairs):
        for k in range(2):
            row = 4 + 2 * p + k
            message_ref[row : row + 1, :] = domains_ref[p : p + 1, k * 128 : (k + 1) * 128]
        halves_ref[p, half:, :] = jnp.broadcast_to(
            domains_ref[p : p + 1, :].astype(jnp.float32), (COORD_ROWS, size)
        )
    for copy in copies[4:]:
        copy.wait()


def look_up(index, table_ref, components, held):
    count = index.shape[1]
    rows = table_ref.shape[0] // held
    table = table_ref[: components * rows, :]
    first = table.astype(jnp.bfloat16)
    left = table - first.astype(jnp.float32)
    second = left.astype(jnp.bfloat16)
    third = (left - second.astype(jnp.float32)).astype(jnp.bfloat16)
    high = index // 128
    low = index - high * 128
    chosen = (lax.broadcasted_iota(jnp.int32, (rows, count), 0) == high).astype(
        jnp.float32
    ).astype(jnp.bfloat16)
    lane = lax.broadcasted_iota(jnp.int32, (128, count), 0) == low
    found = []
    for c in range(components):
        span = slice(c * rows, (c + 1) * rows)
        lines = (
            dot(first[span], chosen, TN)
            + dot(second[span], chosen, TN)
            + dot(third[span], chosen, TN)
        )
        found.append(jnp.sum(jnp.where(lane, lines, 0.0), axis=0, keepdims=True))
    return found


def domain_of(message_ref, p):
    row = 4 + 2 * p
    return jnp.concatenate([message_ref[row : row + 1, :], message_ref[row + 1 : row + 2, :]], axis=1)


def centres_kernel(
    positions_hbm,
    energy_hbm,
    message_ref,
    asked_ref,
    coords_ref,
    far_ref,
    table,
    positions_ref,
    energy_ref,
    sems,
):
    copies = [
        pltpu.make_async_copy(positions_hbm, positions_ref, sems.at[0]),
        pltpu.make_async_copy(energy_hbm, energy_ref, sems.at[1]),
    ]
    for copy in copies:
        copy.start()
    pairs, size = coords_ref.shape[0], coords_ref.shape[2]
    orbitals = positions_ref.shape[1]
    rows = table.shape[0] // 4
    whole, rest = orbitals // 128, orbitals % 128
    for c in range(4):
        table[c * rows + whole : (c + 1) * rows, :] = jnp.zeros((rows - whole, 128), jnp.float32)
    for copy in copies:
        copy.wait()
    for k in range(whole):
        table[pl.ds(k, 3, stride=rows), :] = positions_ref[:, k * 128 : (k + 1) * 128]
        table[3 * rows + k : 3 * rows + k + 1, :] = energy_ref[k * 128 : (k + 1) * 128].reshape(1, 128)
    if rest:
        table[pl.ds(whole, 3, stride=rows), :rest] = positions_ref[:, whole * 128 :]
        table[3 * rows + whole : 3 * rows + whole + 1, :rest] = energy_ref[whole * 128 :].reshape(
            1, rest
        )
    slot_one = jnp.max(message_ref[0:1, :]) > 0
    index = [domain_of(message_ref, p) for p in range(pairs)]
    index.append(jnp.where(slot_one, domain_of(asked_ref, 1), domain_of(asked_ref, 0)))
    found = look_up(jnp.concatenate(index, axis=1), table, 4, 4)
    found.append(jnp.zeros((COORD_ROWS - 4, (pairs + 1) * size), jnp.float32))
    found = jnp.concatenate(found, axis=0)
    for p in range(pairs):
        coords_ref[p] = found[:, p * size : (p + 1) * size]
    far_ref[...] = found[:, pairs * size :]


def select_kernel(asked_ref, block_ref, payload_ref):
    for k in range(payload_ref.shape[1] // 128):
        span = slice(k * 128, (k + 1) * 128)
        slot_one = jnp.broadcast_to(asked_ref[0:1, :], (payload_ref.shape[0], 128)) > 0
        payload_ref[:, span] = jnp.where(slot_one, block_ref[1, :, span], block_ref[0, :, span])


def own_kernel(
    sub_count,
    block_ref,
    integrals_ref,
    coords_ref,
    far_rows_ref,
    source_hbm,
    entry_hbm,
    count_hbm,
    owner_hbm,
    fock_hbm,
    pair_hbm,
    occ_hbm,
    share_ref,
    weight_ref,
    inverse_ref,
    spread_ref,
    high_ref,
    low_ref,
    source_ref,
    entry_ref,
    count_ref,
    owner_ref,
    fock_ref,
    pair_ref,
    occ_ref,
    sems,
):
    moves = (
        (source_hbm, source_ref),
        (entry_hbm, entry_ref),
        (count_hbm, count_ref),
        (owner_hbm, owner_ref),
        (fock_hbm, fock_ref),
        (pair_hbm, pair_ref),
        (occ_hbm, occ_ref),
    )
    copies = [
        pltpu.make_async_copy(source, target, sems.at[k])
        for k, (source, target) in enumerate(moves)
    ]
    for copy in copies:
        copy.start()
    pairs = block_ref.shape[0]
    links = source_ref.shape[1]
    core = lax.axis_index("rep")
    row = lax.axis_index("pairs")
    peers = partners()

    columns = [coords_ref[p].T for p in range(pairs)]
    for p in range(pairs):
        for c in range(3):
            spread_ref[p, c] = jnp.broadcast_to(columns[p][:, c : c + 1], spread_ref.shape[2:])
        high_ref[p], low_ref[p] = split(overlap(columns[p], far_rows_ref[...]))
    zero = core == 0
    column = jnp.where(zero, columns[0], columns[1])
    energy = (column[:, 3:4] + coords_ref[core, 3:4, :]) * 0.5
    block = block_ref[core]
    metric = split(overlap(column, coords_ref[core]))
    firsts = [split(dot3(split(value), metric)) for value in (block, block * energy)]
    plain, scaled = [dot3(metric, first) for first in firsts]

    for copy in copies:
        copy.wait()

    def look(m, carry):
        own_slot, weights = carry
        weights = list(weights)
        for p in range(pairs):
            place = owner_ref[source_ref[p, m]]
            peer, _ = parts_of(place, pairs * sub_count)
            _, slot = parts_of(place, pairs)
            live = m < count_ref[p]
            value = fock_ref[entry_ref[p, m]]
            own = live & (peer == row)
            own_slot = jnp.where(own, slot, own_slot)
            for k, hit in enumerate((own, live & (peer == peers[0]), live & (peer == peers[1]))):
                weights[3 * p + k] += jnp.where(hit, value, 0.0)
        return own_slot, tuple(weights)

    shifts = [occ_ref[pair_ref[p, 0]] + occ_ref[pair_ref[p, 1]] for p in range(pairs)]
    shift = jnp.where(zero, shifts[0], shifts[1])
    share_ref[core] = integrals_ref[core] + scaled + plain * (energy - shift)
    own_slot, weights = lax.fori_loop(
        0, links, look, (jnp.int32(0), (jnp.float32(0.0),) * (3 * pairs))
    )
    for p in range(pairs):
        for k in range(2):
            weight_ref[k, p] = jnp.full((8, 128), weights[3 * p + 1 + k], jnp.float32)
        inverse_ref[p] = 1.0 / (columns[p][:, 3:4] + coords_ref[p, 3:4, :] - shifts[p])
    own_weight = jnp.where(zero, weights[0], weights[3])
    own = overlap(column, coords_ref[own_slot])
    share_ref[core] = share_ref[core] - own_weight * sandwich(own, block_ref[own_slot])
    share_ref[1 - core] = jnp.zeros_like(block)


def near_kernel(near_ref, wanted_ref, table_ref, spread_ref, weight_ref, share_ref, total_ref):
    pairs, size = share_ref.shape[0], share_ref.shape[1]
    half = size // 2
    near = jnp.where(jnp.max(wanted_ref[...]) > 0, near_ref[1], near_ref[0])
    part = split(near[:half, :])
    rows = jnp.concatenate(
        look_up(near[half : half + 1, :].astype(jnp.int32), table_ref, 3, 4), axis=0
    )
    metrics, firsts = [], []
    for p in range(pairs):
        left, right = overlap_spread(spread_ref, p, rows)
        metrics.append(split(jnp.concatenate([left, right], axis=1)))
        side = split(jnp.where(lax.axis_index("rep") == 0, left, right))
        firsts.append(split(dot3(side, part)))
    for p in range(pairs):
        term = dot3(firsts[p], metrics[p], NT)
        total_ref[p] = share_ref[p] - weight_ref[1, p, 0:1, 0:1] * term


def far_kernel(far_ref, high_ref, low_ref, weight_ref, share_ref, total_ref):
    pairs = share_ref.shape[0]
    block = split(far_ref[...])
    firsts = [split(dot3((high_ref[p], low_ref[p]), block)) for p in range(pairs)]
    for p in range(pairs):
        term = dot3(firsts[p], (high_ref[p], low_ref[p]), NT)
        total_ref[p] = share_ref[p] - weight_ref[0, p, 0:1, 0:1] * term


def final_kernel(
    share_ref, other_ref, block_ref, inverse_ref, residual_hbm, updated_hbm, residual_ref, updated_ref, sems
):
    copies = []
    for p in range(share_ref.shape[0]):
        residual = share_ref[p] + other_ref[p]
        residual_ref[p] = residual
        updated_ref[p] = block_ref[p] - residual * inverse_ref[p]
        for k, (source, target) in enumerate(
            ((residual_ref, residual_hbm), (updated_ref, updated_hbm))
        ):
            copies.append(pltpu.make_async_copy(source.at[p], target.at[p], sems.at[2 * p + k]))
            copies[-1].start()
    for copy in copies:
        copy.wait()


def call(
    body, outs, spaces, args, scratch=(), flops=0, moved=0, limit=VMEM_LIMIT, result=pltpu.VMEM
):
    return pl.pallas_call(
        body,
        out_shape=outs,
        in_specs=[pl.BlockSpec(memory_space=space) for space in spaces],
        out_specs=jax.tree.map(lambda _: pl.BlockSpec(memory_space=result), outs),
        scratch_shapes=list(scratch),
        compiler_params=pltpu.CompilerParams(vmem_limit_bytes=limit),
        cost_estimate=pl.CostEstimate(flops=flops, bytes_accessed=moved, transcendentals=0),
    )(*args)


def on_device_four(
    amplitudes,
    exchange_ints,
    pair_list,
    domains,
    link_source,
    link_entry,
    link_count,
    owner_map,
    fock_values,
    occ_energy,
    vir_energy,
    positions,
):
    pairs, size = amplitudes.shape[0], amplitudes.shape[1]
    sub_count = lax.axis_size("sub")
    core = lax.axis_index("rep")
    row = lax.axis_index("pairs")
    axes = ("pairs", "rep")
    across = [(2 * z + outer_core(z), 2 * (z ^ 3) + outer_core(z ^ 3)) for z in range(4)]
    across += [(2 * z + 1 - outer_core(z), 2 * (z ^ 2) + 1 - outer_core(z ^ 2)) for z in range(4)]
    beside = [(2 * z + c, 2 * (z ^ 1) + c) for z in range(4) for c in range(2)]
    f32 = jnp.float32
    V, S = pltpu.VMEM, pltpu.SMEM

    opened = [
        pltpu.with_memory_space_constraint(value, pltpu.HBM)
        for value in (link_source, link_count, owner_map, domains, amplitudes)
    ]
    word = jax.ShapeDtypeStruct((8, 128), jnp.int32)
    message, wanted_near, halves = call(
        functools.partial(open_kernel, sub_count),
        (word, word, jax.ShapeDtypeStruct((pairs, size // 2 + COORD_ROWS, size), f32)),
        (pltpu.HBM,) * len(opened),
        opened,
        scratch=[
            V(link_source.shape, jnp.int32),
            S(link_count.shape, jnp.int32),
            S(owner_map.shape, jnp.int32),
            V(domains.shape, jnp.int32),
            pltpu.SemaphoreType.DMA((4 + pairs,)),
        ],
    )
    asked = lax.ppermute(message, axes, across)
    near = lax.ppermute(halves, axes, beside)
    block = jax.ShapeDtypeStruct((size, size), f32)
    far = call(select_kernel, block, (V, V), (asked, amplitudes), moved=10**6)
    far = lax.ppermute(far, axes, across)

    lines = -(-positions.shape[1] // 128)
    lines = -(-lines // 16) * 16
    coords, far_rows, table = call(
        centres_kernel,
        (
            jax.ShapeDtypeStruct((pairs, COORD_ROWS, size), f32),
            jax.ShapeDtypeStruct((COORD_ROWS, size), f32),
            jax.ShapeDtypeStruct((4 * lines, 128), f32),
        ),
        (pltpu.HBM, pltpu.HBM, V, V),
        (
            pltpu.with_memory_space_constraint(positions, pltpu.HBM),
            pltpu.with_memory_space_constraint(vir_energy, pltpu.HBM),
            message,
            asked,
        ),
        scratch=[
            V(positions.shape, f32),
            V(vir_energy.shape, f32),
            pltpu.SemaphoreType.DMA((2,)),
        ],
        flops=10**9,
        moved=10**6,
    )
    small = (
        link_source,
        link_entry,
        link_count,
        owner_map,
        fock_values,
        pair_list,
        occ_energy,
    )
    share, weight, inverse, spread, high, low = call(
        functools.partial(own_kernel, sub_count),
        (
            jax.ShapeDtypeStruct(amplitudes.shape, f32),
            jax.ShapeDtypeStruct((2, pairs, 8, 128), f32),
            jax.ShapeDtypeStruct(amplitudes.shape, f32),
            jax.ShapeDtypeStruct((pairs, 3, size, 128), f32),
            jax.ShapeDtypeStruct(amplitudes.shape, jnp.bfloat16),
            jax.ShapeDtypeStruct(amplitudes.shape, jnp.bfloat16),
        ),
        (V, V, V, V) + (pltpu.HBM,) * len(small),
        (
            amplitudes,
            exchange_ints,
            coords,
            far_rows,
            *(pltpu.with_memory_space_constraint(value, pltpu.HBM) for value in small),
        ),
        scratch=[S(value.shape, value.dtype) for value in small]
        + [pltpu.SemaphoreType.DMA((len(small),))],
        flops=2 * 10**10,
        moved=4 * 10**7,
    )
    whole = jax.ShapeDtypeStruct(amplitudes.shape, f32)
    cost = dict(flops=10**9, moved=10**6)
    share = call(
        near_kernel, whole, (V,) * 6, (near, wanted_near, table, spread, weight, share), **cost
    )
    share = call(far_kernel, whole, (V,) * 5, (far, high, low, weight, share), **cost)
    other = lax.ppermute(share, "rep", [(0, 1), (1, 0)])
    return call(
        final_kernel,
        (whole, whole),
        (V,) * 4,
        (share, other, amplitudes, inverse),
        scratch=[V(amplitudes.shape, f32), V(amplitudes.shape, f32), pltpu.SemaphoreType.DMA((2 * pairs,))],
        result=pltpu.HBM,
        **cost,
    )


def solution(mesh):
    stored = ("groups", "pairs", "sub")
    in_specs = (
        P(stored, None, None),
        P(stored, None, None),
        P(stored, None),
        P(stored, None),
        P(stored, None),
        P(stored, None),
        P(stored),
        P("groups"),
        P("groups"),
        P("groups"),
        P("groups"),
        P(None, "groups"),
    )
    out_specs = (P(stored, None, None), P(stored, None, None))

    def run(*args):
        devices = mesh.shape["groups"] * mesh.shape["pairs"] * mesh.shape["sub"]
        known = (
            mesh.shape["pairs"] == 4
            and mesh.shape["rep"] == 2
            and args[0].shape[0] == 2 * devices
            and args[0].shape[1] == 256
        )
        return jax.shard_map(
            on_device_four if known else on_device_any,
            mesh=mesh,
            in_specs=in_specs,
            out_specs=out_specs,
            check_vma=False,
        )(*args)

    return run
```

```python
import functools

import jax
import jax.numpy as jnp
from jax import lax
from jax.experimental import pallas as pl
from jax.experimental.pallas import tpu as pltpu
from jax.sharding import PartitionSpec as P

intersection_rate = 2.0
COORD_ROWS = 8
LOG2_E = 1.4426950408889634
VMEM_LIMIT = 40 * 1024 * 1024


def product(left, right):
    return jnp.dot(left, right, precision=lax.Precision.HIGHEST, preferred_element_type=jnp.float32)


def pick_row(array, index):
    return lax.dynamic_index_in_dim(array, index, 0, keepdims=False)


def model_intersection(left_coords, right_coords):
    squared = jnp.zeros((left_coords.shape[1], right_coords.shape[1]), jnp.float32)
    for component in range(3):
        gap_now = left_coords[component][:, None] - right_coords[component][None, :]
        squared = squared + gap_now * gap_now
    return jnp.exp(-intersection_rate * squared)


def pair_local(block, integrals, pair_coords, pair_energy, pair_shift):
    metric = model_intersection(pair_coords, pair_coords)
    virtual_fock = metric * ((pair_energy[:, None] + pair_energy[None, :]) * 0.5)
    right_side = product(block, metric)
    left_side = product(metric, block)
    return (
        integrals
        + product(virtual_fock, right_side)
        + product(left_side, virtual_fock)
        - pair_shift * product(metric, right_side)
    )


def on_device_any(
    amplitudes,
    exchange_ints,
    pair_list,
    domains,
    link_source,
    link_entry,
    link_count,
    owner_map,
    fock_values,
    occ_energy,
    vir_energy,
    positions,
):
    pair_count = amplitudes.shape[0]
    link_slots = link_source.shape[1]
    row_count = lax.axis_size("pairs")
    sub_count = lax.axis_size("sub")
    core_count = lax.axis_size("rep")
    my_core = lax.axis_index("rep")
    coords = jnp.moveaxis(jnp.take(positions, domains, axis=1), 0, 1)
    energy = jnp.take(vir_energy, domains, axis=0)
    shift = jnp.take(occ_energy, pair_list[:, 0]) + jnp.take(occ_energy, pair_list[:, 1])
    is_live = jnp.arange(link_slots, dtype=jnp.int32)[None, :] < link_count[:, None]
    source_loc = jnp.take(owner_map, link_source)
    source_peer = source_loc // (pair_count * sub_count)
    source_slot = source_loc % pair_count
    peers = jnp.arange(row_count, dtype=jnp.int32)
    matched = is_live[:, :, None] & (source_peer[:, :, None] == peers[None, None, :])
    fock_weight = jnp.take(fock_values, link_entry)
    weight = jnp.sum(jnp.where(matched, fock_weight[:, :, None], 0.0), axis=1)
    wanted = jnp.max(jnp.where(matched, source_slot[:, :, None], 0), axis=(0, 1))
    asked = lax.all_to_all(wanted[:, None], "pairs", split_axis=0, concat_axis=0, tiled=True)[:, 0]
    fetched = lax.all_to_all(
        jnp.take(amplitudes, asked, axis=0), "pairs", split_axis=0, concat_axis=0, tiled=True
    )
    fetched_coords = lax.all_to_all(
        jnp.take(coords, asked, axis=0), "pairs", split_axis=0, concat_axis=0, tiled=True
    )

    def target(pair):
        local = pair_local(
            pick_row(amplitudes, pair),
            pick_row(exchange_ints, pair),
            pick_row(coords, pair),
            pick_row(energy, pair),
            pick_row(shift, pair),
        )

        def advance(peer, total):
            intersection = model_intersection(pick_row(coords, pair), pick_row(fetched_coords, peer))
            term = product(product(intersection, pick_row(fetched, peer)), intersection.T)
            return total - pick_row(pick_row(weight, pair), peer) * term

        return lax.fori_loop(0, row_count, advance, local)

    mine = jnp.arange(pair_count, dtype=jnp.int32) % core_count == my_core
    share = lax.map(
        lambda pair: lax.cond(
            pick_row(mine, pair), target, lambda _: jnp.zeros_like(amplitudes[0]), pair
        ),
        jnp.arange(pair_count, dtype=jnp.int32),
    )
    residual = lax.psum(share, "rep")
    denominator = energy[:, :, None] + energy[:, None, :] - shift[:, None, None]
    return residual, amplitudes - residual / denominator


def split(value):
    high = value.astype(jnp.bfloat16)
    low = (value - high.astype(jnp.float32)).astype(jnp.bfloat16)
    return high, low


NN = (((1,), (0,)), ((), ()))
NT = (((1,), (1,)), ((), ()))
TN = (((0,), (0,)), ((), ()))


def dot(left, right, dims):
    return lax.dot_general(left, right, dims, preferred_element_type=jnp.float32)


def dot3(left, right, dims=NN):
    return (
        dot(left[0], right[0], dims) + dot(left[0], right[1], dims) + dot(left[1], right[0], dims)
    )


def overlap(column, rows):
    squared = None
    for c in range(3):
        gap = column[:, c : c + 1] - rows[c : c + 1, :]
        squared = gap * gap if squared is None else squared + gap * gap
    return jnp.exp2(-intersection_rate * LOG2_E * squared)


def overlap_spread(spread_ref, p, rows):
    halves = []
    for k in range(rows.shape[1] // 128):
        squared = None
        for c in range(3):
            gap = spread_ref[p, c] - rows[c : c + 1, k * 128 : (k + 1) * 128]
            squared = gap * gap if squared is None else squared + gap * gap
        halves.append(jnp.exp2(-intersection_rate * LOG2_E * squared))
    return halves


def sandwich(metric, block):
    metric = split(metric)
    return dot3(split(dot3(metric, split(block))), metric, NT)


def start_all(copies):
    for copy in copies:
        copy.start()
    return copies


def parts_of(value, divisor):
    if divisor & (divisor - 1) == 0:
        return value >> (divisor.bit_length() - 1), value & (divisor - 1)
    return lax.div(value, divisor), lax.rem(value, divisor)


def outer_core(row):
    return 1 if row in (1,) else 0


def partners():
    row = lax.axis_index("pairs")
    outer = jnp.int32(0)
    for z in range(4):
        outer = jnp.where(row == z, outer_core(z), outer)
    return jnp.where(lax.axis_index("rep") == outer, row ^ 3, row ^ 2), row ^ 1


def open_kernel(
    sub_count,
    source_hbm,
    count_hbm,
    owner_hbm,
    domains_hbm,
    block_hbm,
    message_ref,
    wanted_near_ref,
    halves_ref,
    source_ref,
    count_ref,
    owner_ref,
    domains_ref,
    sems,
):
    pairs, links = source_ref.shape
    size = domains_ref.shape[1]
    half = size // 2
    start = pl.multiple_of(lax.axis_index("rep") * half, half)
    moves = [
        (source_hbm, source_ref),
        (count_hbm, count_ref),
        (owner_hbm, owner_ref),
        (domains_hbm, domains_ref),
    ]
    moves += [
        (block_hbm.at[p, pl.ds(start, half), :], halves_ref.at[pl.ds(p * half, half), :])
        for p in range(pairs)
    ]
    copies = [
        pltpu.make_async_copy(source, target, sems.at[k])
        for k, (source, target) in enumerate(moves)
    ]
    for copy in copies:
        copy.start()
    for copy in copies[:4]:
        copy.wait()
    source = source_ref[...]
    pair = lax.broadcasted_iota(jnp.int32, (pairs, links), 0)
    limit = jnp.zeros_like(source)
    for p in range(pairs):
        limit = jnp.where(pair == p, count_ref[p], limit)
    live = lax.broadcasted_iota(jnp.int32, (pairs, links), 1) < limit
    place = jnp.zeros_like(source)
    for k in range(owner_ref.shape[0]):
        place = jnp.where(source == k, owner_ref[k], place)
    there, _ = parts_of(place, pairs * sub_count)
    _, slot = parts_of(place, pairs)
    for peer, wanted_ref in zip(partners(), (message_ref, wanted_near_ref)):
        wish = jnp.where(live & (there == peer), slot, 0)
        wanted_ref[...] = jnp.broadcast_to(jnp.max(wish, keepdims=True), (8, 128))
    for p in range(pairs):
        for k in range(2):
            row = 4 + 2 * p + k
            message_ref[row : row + 1, :] = domains_ref[p : p + 1, k * 128 : (k + 1) * 128]
    names = domains_ref[...].astype(jnp.float32)
    blank = jnp.zeros((COORD_ROWS - pairs, size), jnp.float32)
    halves_ref[pairs * half :, :] = jnp.concatenate([names, blank], axis=0)
    for copy in copies[4:]:
        copy.wait()


def look_up(index, table_ref, components, held):
    count = index.shape[1]
    rows = table_ref.shape[0] // held
    table = table_ref[: components * rows, :]
    first = table.astype(jnp.bfloat16)
    left = table - first.astype(jnp.float32)
    second = left.astype(jnp.bfloat16)
    third = (left - second.astype(jnp.float32)).astype(jnp.bfloat16)
    high = index // 128
    low = index - high * 128
    chosen = (lax.broadcasted_iota(jnp.int32, (rows, count), 0) == high).astype(
        jnp.float32
    ).astype(jnp.bfloat16)
    lane = lax.broadcasted_iota(jnp.int32, (128, count), 0) == low
    found = []
    for c in range(components):
        span = slice(c * rows, (c + 1) * rows)
        lines = (
            dot(first[span], chosen, TN)
            + dot(second[span], chosen, TN)
            + dot(third[span], chosen, TN)
        )
        found.append(jnp.sum(jnp.where(lane, lines, 0.0), axis=0, keepdims=True))
    return found


def domain_of(message_ref, p):
    row = 4 + 2 * p
    return jnp.concatenate([message_ref[row : row + 1, :], message_ref[row + 1 : row + 2, :]], axis=1)


def centres_kernel(
    positions_hbm,
    energy_hbm,
    message_ref,
    asked_ref,
    coords_ref,
    far_ref,
    table,
    positions_ref,
    energy_ref,
    sems,
):
    copies = [
        pltpu.make_async_copy(positions_hbm, positions_ref, sems.at[0]),
        pltpu.make_async_copy(energy_hbm, energy_ref, sems.at[1]),
    ]
    for copy in copies:
        copy.start()
    pairs, size = coords_ref.shape[0], coords_ref.shape[2]
    orbitals = positions_ref.shape[1]
    rows = table.shape[0] // 4
    whole, rest = orbitals // 128, orbitals % 128
    for c in range(4):
        table[c * rows + whole : (c + 1) * rows, :] = jnp.zeros((rows - whole, 128), jnp.float32)
    for copy in copies:
        copy.wait()
    for k in range(whole):
        table[pl.ds(k, 3, stride=rows), :] = positions_ref[:, k * 128 : (k + 1) * 128]
        table[3 * rows + k : 3 * rows + k + 1, :] = energy_ref[k * 128 : (k + 1) * 128].reshape(1, 128)
    if rest:
        table[pl.ds(whole, 3, stride=rows), :rest] = positions_ref[:, whole * 128 :]
        table[3 * rows + whole : 3 * rows + whole + 1, :rest] = energy_ref[whole * 128 :].reshape(
            1, rest
        )
    slot_one = jnp.max(message_ref[0:1, :]) > 0
    index = [domain_of(message_ref, p) for p in range(pairs)]
    index.append(jnp.where(slot_one, domain_of(asked_ref, 1), domain_of(asked_ref, 0)))
    found = look_up(jnp.concatenate(index, axis=1), table, 4, 4)
    found.append(jnp.zeros((COORD_ROWS - 4, (pairs + 1) * size), jnp.float32))
    found = jnp.concatenate(found, axis=0)
    for p in range(pairs):
        coords_ref[p] = found[:, p * size : (p + 1) * size]
    far_ref[...] = found[:, pairs * size :]


def select_kernel(asked_ref, block_ref, payload_ref):
    for k in range(payload_ref.shape[1] // 128):
        span = slice(k * 128, (k + 1) * 128)
        slot_one = jnp.broadcast_to(asked_ref[0:1, :], (payload_ref.shape[0], 128)) > 0
        payload_ref[:, span] = jnp.where(slot_one, block_ref[1, :, span], block_ref[0, :, span])


def own_kernel(
    sub_count,
    block_ref,
    integrals_ref,
    coords_ref,
    far_rows_ref,
    source_hbm,
    entry_hbm,
    count_hbm,
    owner_hbm,
    fock_hbm,
    pair_hbm,
    occ_hbm,
    share_ref,
    weight_ref,
    inverse_ref,
    spread_ref,
    high_ref,
    low_ref,
    source_ref,
    entry_ref,
    count_ref,
    owner_ref,
    fock_ref,
    pair_ref,
    occ_ref,
    sems,
):
    moves = (
        (source_hbm, source_ref),
        (entry_hbm, entry_ref),
        (count_hbm, count_ref),
        (owner_hbm, owner_ref),
        (fock_hbm, fock_ref),
        (pair_hbm, pair_ref),
        (occ_hbm, occ_ref),
    )
    copies = [
        pltpu.make_async_copy(source, target, sems.at[k])
        for k, (source, target) in enumerate(moves)
    ]
    for copy in copies:
        copy.start()
    pairs = block_ref.shape[0]
    links = source_ref.shape[1]
    core = lax.axis_index("rep")
    row = lax.axis_index("pairs")
    peers = partners()

    columns = [coords_ref[p].T for p in range(pairs)]
    for p in range(pairs):
        for c in range(3):
            spread_ref[p, c] = jnp.broadcast_to(columns[p][:, c : c + 1], spread_ref.shape[2:])
        high_ref[p], low_ref[p] = split(overlap(columns[p], far_rows_ref[...]))
    zero = core == 0
    column = jnp.where(zero, columns[0], columns[1])
    energy = (column[:, 3:4] + coords_ref[core, 3:4, :]) * 0.5
    block = block_ref[core]
    metric = split(overlap(column, coords_ref[core]))
    firsts = [split(dot3(split(value), metric)) for value in (block, block * energy)]
    plain, scaled = [dot3(metric, first) for first in firsts]

    for copy in copies:
        copy.wait()

    def look(m, carry):
        own_slot, weights = carry
        weights = list(weights)
        for p in range(pairs):
            place = owner_ref[source_ref[p, m]]
            peer, _ = parts_of(place, pairs * sub_count)
            _, slot = parts_of(place, pairs)
            live = m < count_ref[p]
            value = fock_ref[entry_ref[p, m]]
            own = live & (peer == row)
            own_slot = jnp.where(own, slot, own_slot)
            for k, hit in enumerate((own, live & (peer == peers[0]), live & (peer == peers[1]))):
                weights[3 * p + k] += jnp.where(hit, value, 0.0)
        return own_slot, tuple(weights)

    shifts = [occ_ref[pair_ref[p, 0]] + occ_ref[pair_ref[p, 1]] for p in range(pairs)]
    shift = jnp.where(zero, shifts[0], shifts[1])
    share_ref[core] = integrals_ref[core] + scaled + plain * (energy - shift)
    own_slot, weights = lax.fori_loop(
        0, links, look, (jnp.int32(0), (jnp.float32(0.0),) * (3 * pairs))
    )
    for p in range(pairs):
        for k in range(2):
            weight_ref[k, p] = jnp.full((8, 128), weights[3 * p + 1 + k], jnp.float32)
        inverse_ref[p] = 1.0 / (columns[p][:, 3:4] + coords_ref[p, 3:4, :] - shifts[p])
    own_weight = jnp.where(zero, weights[0], weights[3])
    own = overlap(column, coords_ref[own_slot])
    share_ref[core] = share_ref[core] - own_weight * sandwich(own, block_ref[own_slot])
    share_ref[1 - core] = jnp.zeros_like(block)


def near_kernel(near_ref, wanted_ref, table_ref, spread_ref, weight_ref, share_ref, total_ref):
    pairs, size = share_ref.shape[0], share_ref.shape[1]
    half = size // 2
    slot_one = jnp.max(wanted_ref[...]) > 0
    part = split(jnp.where(slot_one, near_ref[half : 2 * half, :], near_ref[:half, :]))
    names = jnp.where(
        slot_one, near_ref[2 * half + 1 : 2 * half + 2, :], near_ref[2 * half : 2 * half + 1, :]
    )
    rows = jnp.concatenate(
        look_up(names.astype(jnp.int32), table_ref, 3, 4), axis=0
    )
    metrics, firsts = [], []
    for p in range(pairs):
        left, right = overlap_spread(spread_ref, p, rows)
        metrics.append(split(jnp.concatenate([left, right], axis=1)))
        side = split(jnp.where(lax.axis_index("rep") == 0, left, right))
        firsts.append(split(dot3(side, part)))
    for p in range(pairs):
        term = dot3(firsts[p], metrics[p], NT)
        total_ref[p] = share_ref[p] - weight_ref[1, p, 0:1, 0:1] * term


def far_kernel(far_ref, high_ref, low_ref, weight_ref, share_ref, total_ref):
    pairs = share_ref.shape[0]
    block = split(far_ref[...])
    firsts = [split(dot3((high_ref[p], low_ref[p]), block)) for p in range(pairs)]
    for p in range(pairs):
        term = dot3(firsts[p], (high_ref[p], low_ref[p]), NT)
        total_ref[p] = share_ref[p] - weight_ref[0, p, 0:1, 0:1] * term


def final_kernel(
    share_ref, other_ref, block_ref, inverse_ref, residual_hbm, updated_hbm, residual_ref, updated_ref, sems
):
    copies = []
    for p in range(share_ref.shape[0]):
        residual = share_ref[p] + other_ref[p]
        residual_ref[p] = residual
        updated_ref[p] = block_ref[p] - residual * inverse_ref[p]
        for k, (source, target) in enumerate(
            ((residual_ref, residual_hbm), (updated_ref, updated_hbm))
        ):
            copies.append(pltpu.make_async_copy(source.at[p], target.at[p], sems.at[2 * p + k]))
            copies[-1].start()
    for copy in copies:
        copy.wait()


def call(
    body, outs, spaces, args, scratch=(), flops=0, moved=0, limit=VMEM_LIMIT, result=pltpu.VMEM
):
    return pl.pallas_call(
        body,
        out_shape=outs,
        in_specs=[pl.BlockSpec(memory_space=space) for space in spaces],
        out_specs=jax.tree.map(lambda _: pl.BlockSpec(memory_space=result), outs),
        scratch_shapes=list(scratch),
        compiler_params=pltpu.CompilerParams(vmem_limit_bytes=limit),
        cost_estimate=pl.CostEstimate(flops=flops, bytes_accessed=moved, transcendentals=0),
    )(*args)


def on_device_four(
    amplitudes,
    exchange_ints,
    pair_list,
    domains,
    link_source,
    link_entry,
    link_count,
    owner_map,
    fock_values,
    occ_energy,
    vir_energy,
    positions,
):
    pairs, size = amplitudes.shape[0], amplitudes.shape[1]
    sub_count = lax.axis_size("sub")
    core = lax.axis_index("rep")
    row = lax.axis_index("pairs")
    axes = ("pairs", "rep")
    across = [(2 * z + outer_core(z), 2 * (z ^ 3) + outer_core(z ^ 3)) for z in range(4)]
    across += [(2 * z + 1 - outer_core(z), 2 * (z ^ 2) + 1 - outer_core(z ^ 2)) for z in range(4)]
    beside = [(2 * z + c, 2 * (z ^ 1) + c) for z in range(4) for c in range(2)]
    f32 = jnp.float32
    V, S = pltpu.VMEM, pltpu.SMEM

    opened = [
        pltpu.with_memory_space_constraint(value, pltpu.HBM)
        for value in (link_source, link_count, owner_map, domains, amplitudes)
    ]
    word = jax.ShapeDtypeStruct((8, 128), jnp.int32)
    message, wanted_near, halves = call(
        functools.partial(open_kernel, sub_count),
        (word, word, jax.ShapeDtypeStruct((pairs * size // 2 + COORD_ROWS, size), f32)),
        (pltpu.HBM,) * len(opened),
        opened,
        scratch=[
            V(link_source.shape, jnp.int32),
            S(link_count.shape, jnp.int32),
            S(owner_map.shape, jnp.int32),
            V(domains.shape, jnp.int32),
            pltpu.SemaphoreType.DMA((4 + pairs,)),
        ],
    )
    asked = lax.ppermute(message, axes, across)
    near = lax.ppermute(halves, axes, beside)
    block = jax.ShapeDtypeStruct((size, size), f32)
    far = call(select_kernel, block, (V, V), (asked, amplitudes), moved=10**6)
    far = lax.ppermute(far, axes, across)

    lines = -(-positions.shape[1] // 128)
    lines = -(-lines // 16) * 16
    coords, far_rows, table = call(
        centres_kernel,
        (
            jax.ShapeDtypeStruct((pairs, COORD_ROWS, size), f32),
            jax.ShapeDtypeStruct((COORD_ROWS, size), f32),
            jax.ShapeDtypeStruct((4 * lines, 128), f32),
        ),
        (pltpu.HBM, pltpu.HBM, V, V),
        (
            pltpu.with_memory_space_constraint(positions, pltpu.HBM),
            pltpu.with_memory_space_constraint(vir_energy, pltpu.HBM),
            message,
            asked,
        ),
        scratch=[
            V(positions.shape, f32),
            V(vir_energy.shape, f32),
            pltpu.SemaphoreType.DMA((2,)),
        ],
        flops=10**9,
        moved=10**6,
    )
    small = (
        link_source,
        link_entry,
        link_count,
        owner_map,
        fock_values,
        pair_list,
        occ_energy,
    )
    share, weight, inverse, spread, high, low = call(
        functools.partial(own_kernel, sub_count),
        (
            jax.ShapeDtypeStruct(amplitudes.shape, f32),
            jax.ShapeDtypeStruct((2, pairs, 8, 128), f32),
            jax.ShapeDtypeStruct(amplitudes.shape, f32),
            jax.ShapeDtypeStruct((pairs, 3, size, 128), f32),
            jax.ShapeDtypeStruct(amplitudes.shape, jnp.bfloat16),
            jax.ShapeDtypeStruct(amplitudes.shape, jnp.bfloat16),
        ),
        (V, V, V, V) + (pltpu.HBM,) * len(small),
        (
            amplitudes,
            exchange_ints,
            coords,
            far_rows,
            *(pltpu.with_memory_space_constraint(value, pltpu.HBM) for value in small),
        ),
        scratch=[S(value.shape, value.dtype) for value in small]
        + [pltpu.SemaphoreType.DMA((len(small),))],
        flops=2 * 10**10,
        moved=4 * 10**7,
    )
    whole = jax.ShapeDtypeStruct(amplitudes.shape, f32)
    cost = dict(flops=10**9, moved=10**6)
    share = call(
        near_kernel, whole, (V,) * 6, (near, wanted_near, table, spread, weight, share), **cost
    )
    share = call(far_kernel, whole, (V,) * 5, (far, high, low, weight, share), **cost)
    other = lax.ppermute(share, "rep", [(0, 1), (1, 0)])
    return call(
        final_kernel,
        (whole, whole),
        (V,) * 4,
        (share, other, amplitudes, inverse),
        scratch=[V(amplitudes.shape, f32), V(amplitudes.shape, f32), pltpu.SemaphoreType.DMA((2 * pairs,))],
        result=pltpu.HBM,
        **cost,
    )


def solution(mesh):
    stored = ("groups", "pairs", "sub")
    in_specs = (
        P(stored, None, None),
        P(stored, None, None),
        P(stored, None),
        P(stored, None),
        P(stored, None),
        P(stored, None),
        P(stored),
        P("groups"),
        P("groups"),
        P("groups"),
        P("groups"),
        P(None, "groups"),
    )
    out_specs = (P(stored, None, None), P(stored, None, None))

    def run(*args):
        devices = mesh.shape["groups"] * mesh.shape["pairs"] * mesh.shape["sub"]
        known = (
            mesh.shape["pairs"] == 4
            and mesh.shape["rep"] == 2
            and args[0].shape[0] == 2 * devices
            and args[0].shape[1] == 256
        )
        return jax.shard_map(
            on_device_four if known else on_device_any,
            mesh=mesh,
            in_specs=in_specs,
            out_specs=out_specs,
            check_vma=False,
        )(*args)

    return run
```

```python
import functools

import jax
import jax.numpy as jnp
from jax import lax
from jax.experimental import pallas as pl
from jax.experimental.pallas import tpu as pltpu
from jax.sharding import PartitionSpec as P

intersection_rate = 2.0
COORD_ROWS = 8
LOG2_E = 1.4426950408889634
VMEM_LIMIT = 40 * 1024 * 1024


def product(left, right):
    return jnp.dot(left, right, precision=lax.Precision.HIGHEST, preferred_element_type=jnp.float32)


def pick_row(array, index):
    return lax.dynamic_index_in_dim(array, index, 0, keepdims=False)


def model_intersection(left_coords, right_coords):
    squared = jnp.zeros((left_coords.shape[1], right_coords.shape[1]), jnp.float32)
    for component in range(3):
        gap_now = left_coords[component][:, None] - right_coords[component][None, :]
        squared = squared + gap_now * gap_now
    return jnp.exp(-intersection_rate * squared)


def pair_local(block, integrals, pair_coords, pair_energy, pair_shift):
    metric = model_intersection(pair_coords, pair_coords)
    virtual_fock = metric * ((pair_energy[:, None] + pair_energy[None, :]) * 0.5)
    right_side = product(block, metric)
    left_side = product(metric, block)
    return (
        integrals
        + product(virtual_fock, right_side)
        + product(left_side, virtual_fock)
        - pair_shift * product(metric, right_side)
    )


def on_device_any(
    amplitudes,
    exchange_ints,
    pair_list,
    domains,
    link_source,
    link_entry,
    link_count,
    owner_map,
    fock_values,
    occ_energy,
    vir_energy,
    positions,
):
    pair_count = amplitudes.shape[0]
    link_slots = link_source.shape[1]
    row_count = lax.axis_size("pairs")
    sub_count = lax.axis_size("sub")
    core_count = lax.axis_size("rep")
    my_core = lax.axis_index("rep")
    coords = jnp.moveaxis(jnp.take(positions, domains, axis=1), 0, 1)
    energy = jnp.take(vir_energy, domains, axis=0)
    shift = jnp.take(occ_energy, pair_list[:, 0]) + jnp.take(occ_energy, pair_list[:, 1])
    is_live = jnp.arange(link_slots, dtype=jnp.int32)[None, :] < link_count[:, None]
    source_loc = jnp.take(owner_map, link_source)
    source_peer = source_loc // (pair_count * sub_count)
    source_slot = source_loc % pair_count
    peers = jnp.arange(row_count, dtype=jnp.int32)
    matched = is_live[:, :, None] & (source_peer[:, :, None] == peers[None, None, :])
    fock_weight = jnp.take(fock_values, link_entry)
    weight = jnp.sum(jnp.where(matched, fock_weight[:, :, None], 0.0), axis=1)
    wanted = jnp.max(jnp.where(matched, source_slot[:, :, None], 0), axis=(0, 1))
    asked = lax.all_to_all(wanted[:, None], "pairs", split_axis=0, concat_axis=0, tiled=True)[:, 0]
    fetched = lax.all_to_all(
        jnp.take(amplitudes, asked, axis=0), "pairs", split_axis=0, concat_axis=0, tiled=True
    )
    fetched_coords = lax.all_to_all(
        jnp.take(coords, asked, axis=0), "pairs", split_axis=0, concat_axis=0, tiled=True
    )

    def target(pair):
        local = pair_local(
            pick_row(amplitudes, pair),
            pick_row(exchange_ints, pair),
            pick_row(coords, pair),
            pick_row(energy, pair),
            pick_row(shift, pair),
        )

        def advance(peer, total):
            intersection = model_intersection(pick_row(coords, pair), pick_row(fetched_coords, peer))
            term = product(product(intersection, pick_row(fetched, peer)), intersection.T)
            return total - pick_row(pick_row(weight, pair), peer) * term

        return lax.fori_loop(0, row_count, advance, local)

    mine = jnp.arange(pair_count, dtype=jnp.int32) % core_count == my_core
    share = lax.map(
        lambda pair: lax.cond(
            pick_row(mine, pair), target, lambda _: jnp.zeros_like(amplitudes[0]), pair
        ),
        jnp.arange(pair_count, dtype=jnp.int32),
    )
    residual = lax.psum(share, "rep")
    denominator = energy[:, :, None] + energy[:, None, :] - shift[:, None, None]
    return residual, amplitudes - residual / denominator


def split(value):
    high = value.astype(jnp.bfloat16)
    low = (value - high.astype(jnp.float32)).astype(jnp.bfloat16)
    return high, low


NN = (((1,), (0,)), ((), ()))
NT = (((1,), (1,)), ((), ()))
TN = (((0,), (0,)), ((), ()))


def dot(left, right, dims):
    return lax.dot_general(left, right, dims, preferred_element_type=jnp.float32)


def dot3(left, right, dims=NN):
    return (
        dot(left[0], right[0], dims) + dot(left[0], right[1], dims) + dot(left[1], right[0], dims)
    )


def overlap(column, rows):
    squared = None
    for c in range(3):
        gap = column[:, c : c + 1] - rows[c : c + 1, :]
        squared = gap * gap if squared is None else squared + gap * gap
    return jnp.exp2(-intersection_rate * LOG2_E * squared)


def overlap_spread(spread_ref, p, rows):
    halves = []
    for k in range(rows.shape[1] // 128):
        squared = None
        for c in range(3):
            gap = spread_ref[p, c] - rows[c : c + 1, k * 128 : (k + 1) * 128]
            squared = gap * gap if squared is None else squared + gap * gap
        halves.append(jnp.exp2(-intersection_rate * LOG2_E * squared))
    return halves


def sandwich(metric, block):
    metric = split(metric)
    return dot3(split(dot3(metric, split(block))), metric, NT)


def start_all(copies):
    for copy in copies:
        copy.start()
    return copies


def parts_of(value, divisor):
    if divisor & (divisor - 1) == 0:
        return value >> (divisor.bit_length() - 1), value & (divisor - 1)
    return lax.div(value, divisor), lax.rem(value, divisor)


def outer_core(row):
    return 1 if row in (1,) else 0


def partners():
    row = lax.axis_index("pairs")
    outer = jnp.int32(0)
    for z in range(4):
        outer = jnp.where(row == z, outer_core(z), outer)
    return jnp.where(lax.axis_index("rep") == outer, row ^ 3, row ^ 2), row ^ 1


def open_kernel(
    sub_count,
    source_hbm,
    count_hbm,
    owner_hbm,
    domains_hbm,
    block_hbm,
    message_ref,
    wanted_near_ref,
    halves_ref,
    source_ref,
    count_ref,
    owner_ref,
    domains_ref,
    sems,
):
    pairs, links = source_ref.shape
    size = domains_ref.shape[1]
    half = size // 2
    start = pl.multiple_of(lax.axis_index("rep") * half, half)
    moves = [
        (source_hbm, source_ref),
        (count_hbm, count_ref),
        (owner_hbm, owner_ref),
        (domains_hbm, domains_ref),
    ]
    moves += [
        (block_hbm.at[p, pl.ds(start, half), :], halves_ref.at[pl.ds(p * half, half), :])
        for p in range(pairs)
    ]
    copies = [
        pltpu.make_async_copy(source, target, sems.at[k])
        for k, (source, target) in enumerate(moves)
    ]
    for copy in copies:
        copy.start()
    for copy in copies[:4]:
        copy.wait()
    source = source_ref[...]
    pair = lax.broadcasted_iota(jnp.int32, (pairs, links), 0)
    limit = jnp.zeros_like(source)
    for p in range(pairs):
        limit = jnp.where(pair == p, count_ref[p], limit)
    live = lax.broadcasted_iota(jnp.int32, (pairs, links), 1) < limit
    place = jnp.zeros_like(source)
    for k in range(owner_ref.shape[0]):
        place = jnp.where(source == k, owner_ref[k], place)
    there, _ = parts_of(place, pairs * sub_count)
    _, slot = parts_of(place, pairs)
    for peer, wanted_ref in zip(partners(), (message_ref, wanted_near_ref)):
        wish = jnp.where(live & (there == peer), slot, 0)
        wanted_ref[...] = jnp.broadcast_to(jnp.max(wish, keepdims=True), (8, 128))
    for p in range(pairs):
        for k in range(2):
            row = 4 + 2 * p + k
            message_ref[row : row + 1, :] = domains_ref[p : p + 1, k * 128 : (k + 1) * 128]
    names = domains_ref[...].astype(jnp.float32)
    blank = jnp.zeros((COORD_ROWS - pairs, size), jnp.float32)
    halves_ref[pairs * half :, :] = jnp.concatenate([names, blank], axis=0)
    for copy in copies[4:]:
        copy.wait()


def look_up(index, table_ref, components, held):
    count = index.shape[1]
    rows = table_ref.shape[0] // held
    table = table_ref[: components * rows, :]
    first = table.astype(jnp.bfloat16)
    left = table - first.astype(jnp.float32)
    second = left.astype(jnp.bfloat16)
    third = (left - second.astype(jnp.float32)).astype(jnp.bfloat16)
    high = index // 128
    low = index - high * 128
    chosen = (lax.broadcasted_iota(jnp.int32, (rows, count), 0) == high).astype(
        jnp.float32
    ).astype(jnp.bfloat16)
    lane = lax.broadcasted_iota(jnp.int32, (128, count), 0) == low
    found = []
    for c in range(components):
        span = slice(c * rows, (c + 1) * rows)
        lines = (
            dot(first[span], chosen, TN)
            + dot(second[span], chosen, TN)
            + dot(third[span], chosen, TN)
        )
        found.append(jnp.sum(jnp.where(lane, lines, 0.0), axis=0, keepdims=True))
    return found


def domain_of(message_ref, p):
    row = 4 + 2 * p
    return jnp.concatenate([message_ref[row : row + 1, :], message_ref[row + 1 : row + 2, :]], axis=1)


def centres_kernel(
    positions_hbm,
    energy_hbm,
    message_ref,
    asked_ref,
    coords_ref,
    far_ref,
    table,
    positions_ref,
    energy_ref,
    sems,
):
    copies = [
        pltpu.make_async_copy(positions_hbm, positions_ref, sems.at[0]),
        pltpu.make_async_copy(energy_hbm, energy_ref, sems.at[1]),
    ]
    for copy in copies:
        copy.start()
    pairs, size = coords_ref.shape[0], coords_ref.shape[2]
    orbitals = positions_ref.shape[1]
    rows = table.shape[0] // 4
    whole, rest = orbitals // 128, orbitals % 128
    for c in range(4):
        table[c * rows + whole : (c + 1) * rows, :] = jnp.zeros((rows - whole, 128), jnp.float32)
    for copy in copies:
        copy.wait()
    for k in range(whole):
        table[pl.ds(k, 3, stride=rows), :] = positions_ref[:, k * 128 : (k + 1) * 128]
        table[3 * rows + k : 3 * rows + k + 1, :] = energy_ref[k * 128 : (k + 1) * 128].reshape(1, 128)
    if rest:
        table[pl.ds(whole, 3, stride=rows), :rest] = positions_ref[:, whole * 128 :]
        table[3 * rows + whole : 3 * rows + whole + 1, :rest] = energy_ref[whole * 128 :].reshape(
            1, rest
        )
    slot_one = jnp.concatenate([message_ref[0:1, :]] * (size // 128), axis=1) > 0
    index = [domain_of(message_ref, p) for p in range(pairs)]
    index.append(jnp.where(slot_one, domain_of(asked_ref, 1), domain_of(asked_ref, 0)))
    found = look_up(jnp.concatenate(index, axis=1), table, 4, 4)
    found.append(jnp.zeros((COORD_ROWS - 4, (pairs + 1) * size), jnp.float32))
    found = jnp.concatenate(found, axis=0)
    for p in range(pairs):
        coords_ref[p] = found[:, p * size : (p + 1) * size]
    far_ref[...] = found[:, pairs * size :]


def select_kernel(asked_ref, block_ref, payload_ref):
    for k in range(payload_ref.shape[1] // 128):
        span = slice(k * 128, (k + 1) * 128)
        slot_one = jnp.broadcast_to(asked_ref[0:1, :], (payload_ref.shape[0], 128)) > 0
        payload_ref[:, span] = jnp.where(slot_one, block_ref[1, :, span], block_ref[0, :, span])


def own_kernel(
    sub_count,
    block_ref,
    integrals_ref,
    coords_ref,
    far_rows_ref,
    source_hbm,
    entry_hbm,
    count_hbm,
    owner_hbm,
    fock_hbm,
    pair_hbm,
    occ_hbm,
    share_ref,
    weight_ref,
    inverse_ref,
    spread_ref,
    high_ref,
    low_ref,
    source_ref,
    entry_ref,
    count_ref,
    owner_ref,
    fock_ref,
    pair_ref,
    occ_ref,
    sems,
):
    moves = (
        (source_hbm, source_ref),
        (entry_hbm, entry_ref),
        (count_hbm, count_ref),
        (owner_hbm, owner_ref),
        (fock_hbm, fock_ref),
        (pair_hbm, pair_ref),
        (occ_hbm, occ_ref),
    )
    copies = [
        pltpu.make_async_copy(source, target, sems.at[k])
        for k, (source, target) in enumerate(moves)
    ]
    for copy in copies:
        copy.start()
    pairs = block_ref.shape[0]
    links = source_ref.shape[1]
    core = lax.axis_index("rep")
    row = lax.axis_index("pairs")
    peers = partners()

    columns = [coords_ref[p].T for p in range(pairs)]
    for p in range(pairs):
        for c in range(3):
            spread_ref[p, c] = jnp.broadcast_to(columns[p][:, c : c + 1], spread_ref.shape[2:])
        high_ref[p], low_ref[p] = split(overlap(columns[p], far_rows_ref[...]))
    zero = core == 0
    column = jnp.where(zero, columns[0], columns[1])
    energy = (column[:, 3:4] + coords_ref[core, 3:4, :]) * 0.5
    block = block_ref[core]
    metric = split(overlap(column, coords_ref[core]))
    firsts = [split(dot3(split(value), metric)) for value in (block, block * energy)]
    plain, scaled = [dot3(metric, first) for first in firsts]

    for copy in copies:
        copy.wait()

    def look(m, carry):
        own_slot, weights = carry
        weights = list(weights)
        for p in range(pairs):
            place = owner_ref[source_ref[p, m]]
            peer, _ = parts_of(place, pairs * sub_count)
            _, slot = parts_of(place, pairs)
            live = m < count_ref[p]
            value = fock_ref[entry_ref[p, m]]
            own = live & (peer == row)
            own_slot = jnp.where(own, slot, own_slot)
            for k, hit in enumerate((own, live & (peer == peers[0]), live & (peer == peers[1]))):
                weights[3 * p + k] += jnp.where(hit, value, 0.0)
        return own_slot, tuple(weights)

    shifts = [occ_ref[pair_ref[p, 0]] + occ_ref[pair_ref[p, 1]] for p in range(pairs)]
    shift = jnp.where(zero, shifts[0], shifts[1])
    share_ref[core] = integrals_ref[core] + scaled + plain * (energy - shift)
    own_slot, weights = lax.fori_loop(
        0, links, look, (jnp.int32(0), (jnp.float32(0.0),) * (3 * pairs))
    )
    for p in range(pairs):
        for k in range(2):
            weight_ref[k, p] = jnp.full((8, 128), weights[3 * p + 1 + k], jnp.float32)
        inverse_ref[p] = 1.0 / (columns[p][:, 3:4] + coords_ref[p, 3:4, :] - shifts[p])
    own_weight = jnp.where(zero, weights[0], weights[3])
    own = overlap(column, coords_ref[own_slot])
    share_ref[core] = share_ref[core] - own_weight * sandwich(own, block_ref[own_slot])
    share_ref[1 - core] = jnp.zeros_like(block)


def near_kernel(near_ref, wanted_ref, table_ref, spread_ref, weight_ref, share_ref, total_ref):
    pairs, size = share_ref.shape[0], share_ref.shape[1]
    half = size // 2
    slot_one = jnp.concatenate([wanted_ref[0:1, :]] * (size // 128), axis=1) > 0
    part = split(jnp.where(slot_one, near_ref[half : 2 * half, :], near_ref[:half, :]))
    names = jnp.where(
        slot_one, near_ref[2 * half + 1 : 2 * half + 2, :], near_ref[2 * half : 2 * half + 1, :]
    )
    rows = jnp.concatenate(
        look_up(names.astype(jnp.int32), table_ref, 3, 4), axis=0
    )
    metrics, firsts = [], []
    for p in range(pairs):
        left, right = overlap_spread(spread_ref, p, rows)
        metrics.append(split(jnp.concatenate([left, right], axis=1)))
        side = split(jnp.where(lax.axis_index("rep") == 0, left, right))
        firsts.append(split(dot3(side, part)))
    for p in range(pairs):
        term = dot3(firsts[p], metrics[p], NT)
        total_ref[p] = share_ref[p] - weight_ref[1, p, 0:1, 0:1] * term


def far_kernel(far_ref, high_ref, low_ref, weight_ref, share_ref, total_ref):
    pairs = share_ref.shape[0]
    block = split(far_ref[...])
    firsts = [split(dot3((high_ref[p], low_ref[p]), block)) for p in range(pairs)]
    for p in range(pairs):
        term = dot3(firsts[p], (high_ref[p], low_ref[p]), NT)
        total_ref[p] = share_ref[p] - weight_ref[0, p, 0:1, 0:1] * term


def final_kernel(
    share_ref, other_ref, block_ref, inverse_ref, residual_hbm, updated_hbm, residual_ref, updated_ref, sems
):
    copies = []
    for p in range(share_ref.shape[0]):
        residual = share_ref[p] + other_ref[p]
        residual_ref[p] = residual
        updated_ref[p] = block_ref[p] - residual * inverse_ref[p]
        for k, (source, target) in enumerate(
            ((residual_ref, residual_hbm), (updated_ref, updated_hbm))
        ):
            copies.append(pltpu.make_async_copy(source.at[p], target.at[p], sems.at[2 * p + k]))
            copies[-1].start()
    for copy in copies:
        copy.wait()


def call(
    body, outs, spaces, args, scratch=(), flops=0, moved=0, limit=VMEM_LIMIT, result=pltpu.VMEM
):
    return pl.pallas_call(
        body,
        out_shape=outs,
        in_specs=[pl.BlockSpec(memory_space=space) for space in spaces],
        out_specs=jax.tree.map(lambda _: pl.BlockSpec(memory_space=result), outs),
        scratch_shapes=list(scratch),
        compiler_params=pltpu.CompilerParams(vmem_limit_bytes=limit),
        cost_estimate=pl.CostEstimate(flops=flops, bytes_accessed=moved, transcendentals=0),
    )(*args)


def on_device_four(
    amplitudes,
    exchange_ints,
    pair_list,
    domains,
    link_source,
    link_entry,
    link_count,
    owner_map,
    fock_values,
    occ_energy,
    vir_energy,
    positions,
):
    pairs, size = amplitudes.shape[0], amplitudes.shape[1]
    sub_count = lax.axis_size("sub")
    core = lax.axis_index("rep")
    row = lax.axis_index("pairs")
    axes = ("pairs", "rep")
    across = [(2 * z + outer_core(z), 2 * (z ^ 3) + outer_core(z ^ 3)) for z in range(4)]
    across += [(2 * z + 1 - outer_core(z), 2 * (z ^ 2) + 1 - outer_core(z ^ 2)) for z in range(4)]
    beside = [(2 * z + c, 2 * (z ^ 1) + c) for z in range(4) for c in range(2)]
    f32 = jnp.float32
    V, S = pltpu.VMEM, pltpu.SMEM

    opened = [
        pltpu.with_memory_space_constraint(value, pltpu.HBM)
        for value in (link_source, link_count, owner_map, domains, amplitudes)
    ]
    word = jax.ShapeDtypeStruct((8, 128), jnp.int32)
    message, wanted_near, halves = call(
        functools.partial(open_kernel, sub_count),
        (word, word, jax.ShapeDtypeStruct((pairs * size // 2 + COORD_ROWS, size), f32)),
        (pltpu.HBM,) * len(opened),
        opened,
        scratch=[
            V(link_source.shape, jnp.int32),
            S(link_count.shape, jnp.int32),
            S(owner_map.shape, jnp.int32),
            V(domains.shape, jnp.int32),
            pltpu.SemaphoreType.DMA((4 + pairs,)),
        ],
    )
    asked = lax.ppermute(message, axes, across)
    near = lax.ppermute(halves, axes, beside)
    block = jax.ShapeDtypeStruct((size, size), f32)
    far = call(select_kernel, block, (V, V), (asked, amplitudes), moved=10**6)
    far = lax.ppermute(far, axes, across)

    lines = -(-positions.shape[1] // 128)
    lines = -(-lines // 16) * 16
    coords, far_rows, table = call(
        centres_kernel,
        (
            jax.ShapeDtypeStruct((pairs, COORD_ROWS, size), f32),
            jax.ShapeDtypeStruct((COORD_ROWS, size), f32),
            jax.ShapeDtypeStruct((4 * lines, 128), f32),
        ),
        (pltpu.HBM, pltpu.HBM, V, V),
        (
            pltpu.with_memory_space_constraint(positions, pltpu.HBM),
            pltpu.with_memory_space_constraint(vir_energy, pltpu.HBM),
            message,
            asked,
        ),
        scratch=[
            V(positions.shape, f32),
            V(vir_energy.shape, f32),
            pltpu.SemaphoreType.DMA((2,)),
        ],
        flops=10**9,
        moved=10**6,
    )
    small = (
        link_source,
        link_entry,
        link_count,
        owner_map,
        fock_values,
        pair_list,
        occ_energy,
    )
    share, weight, inverse, spread, high, low = call(
        functools.partial(own_kernel, sub_count),
        (
            jax.ShapeDtypeStruct(amplitudes.shape, f32),
            jax.ShapeDtypeStruct((2, pairs, 8, 128), f32),
            jax.ShapeDtypeStruct(amplitudes.shape, f32),
            jax.ShapeDtypeStruct((pairs, 3, size, 128), f32),
            jax.ShapeDtypeStruct(amplitudes.shape, jnp.bfloat16),
            jax.ShapeDtypeStruct(amplitudes.shape, jnp.bfloat16),
        ),
        (V, V, V, V) + (pltpu.HBM,) * len(small),
        (
            amplitudes,
            exchange_ints,
            coords,
            far_rows,
            *(pltpu.with_memory_space_constraint(value, pltpu.HBM) for value in small),
        ),
        scratch=[S(value.shape, value.dtype) for value in small]
        + [pltpu.SemaphoreType.DMA((len(small),))],
        flops=2 * 10**10,
        moved=4 * 10**7,
    )
    whole = jax.ShapeDtypeStruct(amplitudes.shape, f32)
    cost = dict(flops=10**9, moved=10**6)
    share = call(
        near_kernel, whole, (V,) * 6, (near, wanted_near, table, spread, weight, share), **cost
    )
    share = call(far_kernel, whole, (V,) * 5, (far, high, low, weight, share), **cost)
    other = lax.ppermute(share, "rep", [(0, 1), (1, 0)])
    return call(
        final_kernel,
        (whole, whole),
        (V,) * 4,
        (share, other, amplitudes, inverse),
        scratch=[V(amplitudes.shape, f32), V(amplitudes.shape, f32), pltpu.SemaphoreType.DMA((2 * pairs,))],
        result=pltpu.HBM,
        **cost,
    )


def solution(mesh):
    stored = ("groups", "pairs", "sub")
    in_specs = (
        P(stored, None, None),
        P(stored, None, None),
        P(stored, None),
        P(stored, None),
        P(stored, None),
        P(stored, None),
        P(stored),
        P("groups"),
        P("groups"),
        P("groups"),
        P("groups"),
        P(None, "groups"),
    )
    out_specs = (P(stored, None, None), P(stored, None, None))

    def run(*args):
        devices = mesh.shape["groups"] * mesh.shape["pairs"] * mesh.shape["sub"]
        known = (
            mesh.shape["pairs"] == 4
            and mesh.shape["rep"] == 2
            and args[0].shape[0] == 2 * devices
            and args[0].shape[1] == 256
        )
        return jax.shard_map(
            on_device_four if known else on_device_any,
            mesh=mesh,
            in_specs=in_specs,
            out_specs=out_specs,
            check_vma=False,
        )(*args)

    return run
```
